32 devices in a mesh: groups: 2 (over y), rows: 4 (over x, core), cols: 4 (over z).
Axes of the slice: x: 2, y: 2, z: 4, core: 2. Of those that a mesh axis runs over, the one named last changes fastest.
Arguments:
- object_field: float32 [4, 512, 1024], P('groups', 'cols', 'rows'), parts along dimension 0, may hold values from -6 to 6
- probe: float32 [8, 2, 512, 512], P('groups', None, 'cols'), parts along dimension 0, may hold values from -3 to 3
- amplitudes: float32 [48, 512, 512], P(('groups', 'rows'), 'cols'), parts along dimension 0, may hold values from 0.5 to 3.5
- strip_counts: int32 [8], P(('groups', 'rows')), parts along dimension 0, may hold values from 1 to 6, 12 in all
- row_offsets: int32 [48], P(('groups', 'rows')), parts along dimension 0, may hold values from 0 to 255
- col_offsets: int32 [48], P(('groups', 'rows')), parts along dimension 0, may hold values from 0 to 127
Outputs:
- object_grad: float32 [4, 512, 1024], P('groups', 'cols', 'rows'), parts along dimension 0
- probe_grad: float32 [8, 2, 512, 512], P('groups', None, 'cols'), parts along dimension 0
The draws below stay inside these ranges and needn't reach their ends.
There are 2 independent parts, one for each index of `groups`. The reference program is written for one: setup_inputs(seed, part) draws one part's arguments, and reference() takes and returns one part's arrays. A program takes and returns all parts, laid end to end along the dimension named above; each array names one. Nothing has to cross between parts.
Inputs may be any that keep to these rules, and one draw needn't show every extreme that they name: `strip_counts`: the counts sum to 12, and the largest is exactly 6.
All inputs are finite; a program needn't handle non-finite values. No bound on the sum of `strip_counts` on one device may be relied on, other than what follows from the above.
Results may differ from the reference program's by a relative error of at most 0.012.
The reference program's roundings to bfloat16 on the way count: a program that leaves them out, or rounds other values in their place, can miss the bound.
Values may be sent and summed in bfloat16 or wider, within the bound.
A program may use at most 64 MiB of HBM per device.

```python
import math
import jax
import jax.numpy as jnp
import numpy as np
from jax import lax

PROBE = 512
MODES = 4
ROWS_DEV = 256
POS_MAX = 6
TOTAL = 12
CB = 128
NX = 1024
NY = 512
N_ROWS = 4


def place_ends(result, stream_key, smallest, largest):
    index_at = [jax.random.randint(jax.random.fold_in(stream_key, axis), (), 0, length) for axis, length in enumerate(result.shape)]
    longest = result.shape.index(max(result.shape))
    neighbour = index_at[:longest] + [(index_at[longest] + 1) % result.shape[longest]] + index_at[longest + 1:]
    return result.at[tuple(index_at)].set(smallest).at[tuple(neighbour)].set(largest)


def steps_of(rng, shape, pieces, smallest, high):
    def one(dim, blocks):
        draws = jax.random.uniform(jax.random.fold_in(jax.random.fold_in(rng, 6), dim), (blocks,), jnp.float32, smallest / len(pieces), high / len(pieces))
        return jnp.repeat(jnp.exp(draws), shape[dim] // blocks).reshape((-1,) + (1,) * (len(shape) - dim - 1))

    gain = one(*pieces[0])
    for cut in pieces[1:]:
        gain = gain * one(*cut)
    return gain


def profile(amount, total, most, skew):
    loads = [(1 << 20) // math.isqrt(rank ** skew) + 1 for rank in range(2, amount + 1)]
    spare, given = total - most - (amount - 1), [1] * (amount - 1)
    while spare > 0:
        movable = [i for i in range(amount - 1) if given[i] < most]
        mass, left = sum([loads[i] for i in movable]), spare
        for i in movable:
            extra = min(most - given[i], max(1, left * loads[i] // mass), spare)
            given[i] = given[i] + extra
            spare = spare - extra
    return np.array([most] + given)


def uneven(own_key, amount, total, reach, slope):
    if amount == 2:
        one = jax.random.randint(own_key, (), max(1, total - reach), min(reach, total - 1) + 1)
        return jnp.stack([one, total - one])
    lengths = jnp.asarray(profile(amount, total, reach, slope), jnp.int32)
    couples = (amount - 1) // 2
    source_of, taker = lengths[1:1 + 2 * couples:2], lengths[2:2 + 2 * couples:2]
    slack = jnp.minimum(source_of - 1, reach - taker)
    passed = jax.random.randint(jax.random.fold_in(own_key, 1), (couples,), 0, 1 << 20) % (slack + 1)
    lengths = lengths.at[1:1 + 2 * couples:2].set(source_of - passed).at[2:2 + 2 * couples:2].set(taker + passed)
    return lengths[jax.random.permutation(jax.random.fold_in(own_key, 2), amount)]


def centred(key, extent, spread, limit, shards=(), held_as=jnp.bfloat16):
    result = jax.random.normal(key, extent, jnp.float32) * spread
    if len(shards) > 0:
        result = steps_of(key, extent, shards, -0.22, 0.18) * result
    return jnp.clip(result, min=-limit, max=limit).astype(held_as)


def setup_inputs(seed: int = 0, part: int = 0) -> dict:
    keys = jax.random.split(jax.random.key(seed), 7)
    part_keys = jax.random.split(jax.random.fold_in(keys[6], part), 7)
    return {
        "object_field": centred(part_keys[0], (2, NY, NX), 1.0, 6.0, ((1, 4), (2, 4)), jnp.float32),
        "probe": centred(part_keys[1], (MODES, 2, PROBE, PROBE), 0.5, 3.0, ((2, 4),), jnp.float32),
        "amplitudes": jnp.clip(0.5 + 3.0 * jax.random.uniform(part_keys[2], (N_ROWS * POS_MAX, PROBE, PROBE), jnp.float32) ** steps_of(part_keys[2], (N_ROWS * POS_MAX, PROBE, PROBE), ((0, 4), (1, 4)), -0.2, 0.2), 0.5, 3.5),
        "strip_counts": uneven(part_keys[3], N_ROWS, TOTAL, POS_MAX, 2).astype(jnp.int32),
        "row_offsets": place_ends(jax.random.randint(part_keys[4], (N_ROWS * POS_MAX,), 0, ROWS_DEV), jax.random.fold_in(part_keys[4], 1), 0, ROWS_DEV - 1).astype(jnp.int32),
        "col_offsets": place_ends(jax.random.randint(part_keys[5], (N_ROWS * POS_MAX,), 0, CB), jax.random.fold_in(part_keys[5], 1), 0, CB - 1).astype(jnp.int32),
    }


def dft_tables(length):
    indices = jnp.arange(length, dtype=jnp.int32)
    product = indices[:, None] * indices[None, :] % length
    angles = product.astype(jnp.float32) * jnp.float32(2.0 * 3.141592653589793 / length)
    scaling = jnp.float32(1.0 / length ** 0.5)
    cosine_table = (jnp.cos(angles) * scaling).astype(jnp.bfloat16)
    sine_table = (jnp.sin(angles) * scaling).astype(jnp.bfloat16)
    return (cosine_table, sine_table)

def contract(spec, left, right):
    return jnp.einsum(spec, left.astype(jnp.float32), right.astype(jnp.float32), precision=lax.Precision.HIGHEST)

def position_terms(patch_real, patch_imag, probe, measured, cosine_table, sine_table):
    probe_real = probe[:, 0]
    probe_imag = probe[:, 1]
    wave_real = (probe_real * patch_real - probe_imag * patch_imag).astype(jnp.bfloat16)
    wave_imag = (probe_real * patch_imag + probe_imag * patch_real).astype(jnp.bfloat16)
    first_real = (contract('mca,au->mcu', wave_real, cosine_table) + contract('mca,au->mcu', wave_imag, sine_table)).astype(jnp.bfloat16)
    first_imag = (contract('mca,au->mcu', wave_imag, cosine_table) - contract('mca,au->mcu', wave_real, sine_table)).astype(jnp.bfloat16)
    field_real = contract('mcu,cv->muv', first_real, cosine_table) + contract('mcu,cv->muv', first_imag, sine_table)
    field_imag = contract('mcu,cv->muv', first_imag, cosine_table) - contract('mcu,cv->muv', first_real, sine_table)
    intensity = lax.optimization_barrier(jnp.sum(field_real * field_real + field_imag * field_imag, axis=0))
    modulus = jnp.sqrt(jnp.maximum(intensity, 0.25))
    factor = 1.0 - measured / modulus
    back_real = (field_real * factor).astype(jnp.bfloat16)
    back_imag = (field_imag * factor).astype(jnp.bfloat16)
    inner_real = (contract('muv,vb->mub', back_real, cosine_table) - contract('muv,vb->mub', back_imag, sine_table)).astype(jnp.bfloat16)
    inner_imag = (contract('muv,vb->mub', back_imag, cosine_table) + contract('muv,vb->mub', back_real, sine_table)).astype(jnp.bfloat16)
    grad_real = contract('mub,ua->mba', inner_real, cosine_table) - contract('mub,ua->mba', inner_imag, sine_table)
    grad_imag = contract('mub,ua->mba', inner_imag, cosine_table) + contract('mub,ua->mba', inner_real, sine_table)
    object_real = lax.optimization_barrier(jnp.sum(probe_real * grad_real + probe_imag * grad_imag, axis=0))
    object_imag = lax.optimization_barrier(jnp.sum(probe_real * grad_imag - probe_imag * grad_real, axis=0))
    probe_real_term = patch_real * grad_real + patch_imag * grad_imag
    probe_imag_term = patch_real * grad_imag - patch_imag * grad_real
    return (jnp.stack([object_real, object_imag]), jnp.stack([probe_real_term, probe_imag_term], axis=1))

def reference(object_field, probe, amplitudes, strip_counts, row_offsets, col_offsets):
    cosine_table, sine_table = dft_tables(PROBE)
    counts_int = strip_counts.astype(jnp.int32)
    totals = jnp.cumsum(counts_int).astype(jnp.int32)
    starts = (totals - counts_int).astype(jnp.int32)
    position_ids = jnp.arange(TOTAL, dtype=jnp.int32)
    strip_of = lax.optimization_barrier(jnp.sum((totals[None, :] <= position_ids[:, None]).astype(jnp.int32), axis=1)).astype(jnp.int32)
    slot_of = (strip_of * POS_MAX + position_ids - jnp.take(starts, strip_of)).astype(jnp.int32)
    cell_range = jnp.arange(PROBE, dtype=jnp.int32)

    def visit_slot(state_pair, slot_index):
        object_sum, probe_sum = state_pair
        strip_index = slot_index // POS_MAX
        first_row = strip_index * ROWS_DEV + row_offsets[slot_index]
        raw_rows = (first_row + cell_range).astype(jnp.int32)
        raw_cols = (col_offsets[slot_index] + cell_range).astype(jnp.int32)
        valid = (raw_cols[:, None] < NY) & (raw_rows[None, :] < NX)
        row_index = (raw_rows % NX).astype(jnp.int32)
        col_index = (raw_cols % NY).astype(jnp.int32)
        patch_cells = jnp.take(jnp.take(object_field, col_index, axis=1), row_index, axis=2)
        patch_real = jnp.where(valid, patch_cells[0], jnp.float32(1.0))
        patch_imag = jnp.where(valid, patch_cells[1], jnp.float32(0.0))
        measured = amplitudes[slot_index]
        object_term, probe_term = position_terms(patch_real, patch_imag, probe, measured, cosine_table, sine_table)
        object_term = jnp.where(valid[None], object_term, jnp.float32(0.0))
        object_sum = object_sum.at[:, col_index[:, None], row_index[None, :]].add(object_term)
        return ((object_sum, probe_sum + probe_term), None)
    initial = (jnp.zeros(object_field.shape, jnp.float32), jnp.zeros(probe.shape, jnp.float32))
    (object_grad, probe_grad), unused = lax.scan(visit_slot, initial, slot_of)
    return (object_grad, probe_grad)
```

```python
import functools

import jax
import jax.numpy as jnp
import numpy as np
from jax import lax
from jax.experimental import pallas as pl
from jax.experimental.pallas import tpu as pltpu
from jax.sharding import PartitionSpec as P

POS_AVG = 3
POS_MAX = 6


def shifted(block, axis, distance):
    devices = range(lax.axis_size(axis))
    route = [(i - distance, i) for i in devices if i - distance in devices]
    return lax.ppermute(block, axis, route)


def dft_tables(length):
    indices = jnp.arange(length, dtype=jnp.int32)
    product = indices[:, None] * indices[None, :] % length
    angles = product.astype(jnp.float32) * jnp.float32(2.0 * 3.141592653589793 / length)
    scaling = jnp.float32(1.0 / length**0.5)
    cosine_table = (jnp.cos(angles) * scaling).astype(jnp.bfloat16)
    sine_table = (jnp.sin(angles) * scaling).astype(jnp.bfloat16)
    return (cosine_table, sine_table)


def leading(values, matrix):
    return jnp.einsum("mca,asu->mscu", values, matrix, preferred_element_type=jnp.float32)


def second(values, matrix):
    return jnp.einsum("mscu,scv->muv", values, matrix, preferred_element_type=jnp.float32)


def third(values, matrix):
    return jnp.einsum("muv,vsb->msub", values, matrix, preferred_element_type=jnp.float32)


def fourth(values, matrix):
    return jnp.einsum("msub,sua->mba", values, matrix, preferred_element_type=jnp.float32)


def vacuum_where(block, outside):
    fill_real = jnp.where(outside, jnp.float32(1.0), block[0])
    fill_imag = jnp.where(outside, jnp.float32(0.0), block[1])
    return jnp.stack([fill_real, fill_imag])


def spectral_pass(patch_cells, probe, measured, cosine_table, sine_table, block_count):
    mode_count = probe.shape[0]
    block_cols = patch_cells.shape[1]
    length = patch_cells.shape[2]
    block_freq = length // block_count
    probe_real = probe[:, 0]
    probe_imag = probe[:, 1]
    patch_real = patch_cells[0]
    patch_imag = patch_cells[1]
    wave_real = (probe_real * patch_real - probe_imag * patch_imag).astype(jnp.bfloat16)
    wave_imag = (probe_real * patch_imag + probe_imag * patch_real).astype(jnp.bfloat16)
    cos_lead = cosine_table.reshape(length, block_count, block_freq)
    sin_lead = sine_table.reshape(length, block_count, block_freq)
    first_real = leading(wave_real, cos_lead) + leading(wave_imag, sin_lead)
    first_imag = leading(wave_imag, cos_lead) - leading(wave_real, sin_lead)
    outgoing = jnp.stack([first_real, first_imag], axis=1).astype(jnp.bfloat16)
    outgoing = outgoing.reshape(mode_count, 2, block_count, block_cols * block_freq)
    arrived = lax.all_to_all(outgoing, "cols", split_axis=2, concat_axis=2, tiled=True)
    arrived = arrived.reshape(mode_count, 2, block_count, block_cols, block_freq)
    cos_rows = cosine_table.reshape(block_count, block_cols, length)
    sin_rows = sine_table.reshape(block_count, block_cols, length)
    field_real = second(arrived[:, 0], cos_rows) + second(arrived[:, 1], sin_rows)
    field_imag = second(arrived[:, 1], cos_rows) - second(arrived[:, 0], sin_rows)
    intensity = jnp.sum(field_real * field_real + field_imag * field_imag, axis=0)
    modulus = jnp.sqrt(jnp.maximum(intensity, 0.25))
    factor = 1.0 - measured / modulus
    back_real = (field_real * factor).astype(jnp.bfloat16)
    back_imag = (field_imag * factor).astype(jnp.bfloat16)
    cos_back = cosine_table.reshape(length, block_count, block_cols)
    sin_back = sine_table.reshape(length, block_count, block_cols)
    inner_real = third(back_real, cos_back) - third(back_imag, sin_back)
    inner_imag = third(back_imag, cos_back) + third(back_real, sin_back)
    returning = jnp.stack([inner_real, inner_imag], axis=1).astype(jnp.bfloat16)
    returning = returning.reshape(mode_count, 2, block_count, block_freq * block_cols)
    landed = lax.all_to_all(returning, "cols", split_axis=2, concat_axis=2, tiled=True)
    landed = landed.reshape(mode_count, 2, block_count, block_freq, block_cols)
    cos_freq = cosine_table.reshape(block_count, block_freq, length)
    sin_freq = sine_table.reshape(block_count, block_freq, length)
    grad_real = fourth(landed[:, 0], cos_freq) - fourth(landed[:, 1], sin_freq)
    grad_imag = fourth(landed[:, 1], cos_freq) + fourth(landed[:, 0], sin_freq)
    object_real = jnp.sum(probe_real * grad_real + probe_imag * grad_imag, axis=0)
    object_imag = jnp.sum(probe_real * grad_imag - probe_imag * grad_real, axis=0)
    probe_real_term = patch_real * grad_real + patch_imag * grad_imag
    probe_imag_term = patch_real * grad_imag - patch_imag * grad_real
    return (
        jnp.stack([object_real, object_imag]),
        jnp.stack([probe_real_term, probe_imag_term], axis=1),
    )


def run_positions(
    window,
    probe,
    frames,
    first_rows,
    first_cols,
    slot_total,
    used_count,
    cosine_table,
    sine_table,
    block_count,
):
    block_cols = probe.shape[2]
    length = probe.shape[3]

    def visit_slot(slot_index, state_pair):
        window_grad, probe_sum = state_pair
        first_row = first_rows[slot_index]
        first_col = first_cols[slot_index]
        patch_cells = lax.dynamic_slice(window, (0, first_col, first_row), (2, block_cols, length))
        measured = lax.dynamic_index_in_dim(frames, slot_index, 0, keepdims=False)
        object_term, probe_term = spectral_pass(
            patch_cells, probe, measured, cosine_table, sine_table, block_count
        )
        active = (slot_index < used_count).astype(jnp.float32)
        current = lax.dynamic_slice(window_grad, (0, first_col, first_row), (2, block_cols, length))
        window_grad = lax.dynamic_update_slice(
            window_grad, current + active * object_term, (0, first_col, first_row)
        )
        return (window_grad, probe_sum + active * probe_term)

    initial = (jnp.zeros(window.shape, jnp.float32), jnp.zeros(probe.shape, jnp.float32))
    return lax.fori_loop(0, slot_total, visit_slot, initial)


def general_device(object_field, probe, amplitudes, strip_counts, row_offsets, col_offsets):
    block_cols = object_field.shape[1]
    strip_rows = object_field.shape[2]
    length = probe.shape[3]
    block_count = lax.axis_size("cols")
    strip_total = lax.axis_size("rows")
    cosine_table, sine_table = dft_tables(length)
    beside = shifted(object_field, "cols", -1)
    beside = vacuum_where(beside, lax.axis_index("cols") == block_count - 1)
    paired = jnp.concatenate([object_field, beside], axis=1)
    counts_all, rows_all, cols_all = (
        lax.all_gather(strip_counts, "rows", axis=0, tiled=True),
        lax.all_gather(row_offsets, "rows", axis=0, tiled=True),
        lax.all_gather(col_offsets, "rows", axis=0, tiled=True),
    )
    totals = jnp.cumsum(counts_all)
    starts = totals - counts_all
    position_block = (lax.axis_index("rows") + strip_total // 2) % strip_total
    my_positions = position_block * POS_AVG + jnp.arange(POS_AVG, dtype=jnp.int32)
    strip_of = jnp.sum((totals[None, :] <= my_positions[:, None]).astype(jnp.int32), axis=1)
    wanted = strip_of * POS_MAX + my_positions - jnp.take(starts, strip_of)
    first_rows = strip_of * strip_rows + jnp.take(rows_all, wanted)
    first_cols = jnp.take(cols_all, wanted)
    empty_frames = jnp.zeros((POS_AVG,) + amplitudes.shape[1:], jnp.float32)
    received = lax.all_gather(amplitudes, "rows", axis=0, tiled=True)
    inside = (wanted >= 0) & (wanted < received.shape[0])
    picked = jnp.take(received, jnp.clip(wanted, 0, received.shape[0] - 1), axis=0)
    frames = jnp.where(inside[:, None, None], picked, empty_frames)
    column_all = lax.all_gather(paired, "rows", axis=2, tiled=True)
    all_rows = column_all.shape[2]
    vacuum_tail = vacuum_where(jnp.zeros((2, column_all.shape[1], length), jnp.float32), True)
    window = jnp.concatenate([column_all, vacuum_tail], axis=2)
    window_grad, probe_sum = run_positions(
        window,
        probe,
        frames,
        first_rows,
        first_cols,
        POS_AVG,
        POS_AVG,
        cosine_table,
        sine_table,
        block_count,
    )
    folded = window_grad[:, :, :all_rows]
    summed = lax.psum_scatter(folded, "rows", scatter_dimension=2, tiled=True)
    upper_half = shifted(summed[:, block_cols:], "cols", 1)
    object_grad = summed[:, :block_cols] + upper_half
    probe_grad = lax.psum(probe_sum, "rows")
    return (object_grad, probe_grad)


def tables(length):
    indices = np.arange(length)
    angles = (indices[:, None] * indices[None, :] % length) * (2.0 * np.pi / length)
    scaling = 1.0 / length**0.5
    return jnp.asarray(np.cos(angles) * scaling, jnp.bfloat16), jnp.asarray(np.sin(angles) * scaling, jnp.bfloat16)


ANY = pl.BlockSpec(memory_space=pl.ANY)
WHOLE = pl.BlockSpec(memory_space=pltpu.VMEM)
LIMIT = 56 * 1024 * 1024
N = 4


def greet(axes):
    barrier = pltpu.get_barrier_semaphore()
    for axis in axes:
        me = lax.axis_index(axis)
        for k in range(1, N):
            pl.semaphore_signal(
                barrier, inc=1, device_id={axis: lax.rem(me + k, N)}, device_id_type=pl.DeviceIdType.MESH
            )
    pl.semaphore_wait(barrier, (N - 1) * len(axes))


def remote(src, dst, sems, slot, device):
    return pltpu.make_async_remote_copy(
        src_ref=src,
        dst_ref=dst,
        send_sem=sems.at[0, slot],
        recv_sem=sems.at[1, slot],
        device_id=device,
        device_id_type=pl.DeviceIdType.MESH,
    )


class Gather:
    def __init__(self, axis, src, out, sems, base, scatter=False):
        self.me = lax.axis_index(axis)
        self.axis, self.src, self.out, self.sems, self.base, self.scatter = axis, src, out, sems, base, scatter

    def piece(self, index):
        return self.src.at[index] if self.scatter else self.src

    def start(self):
        self.local = pltpu.make_async_copy(
            self.piece(self.me), self.out.at[self.me], self.sems.at[0, self.base]
        )
        self.sent = []
        for k in range(1, N):
            to = lax.rem(self.me + k, N)
            copy = remote(self.piece(to), self.out.at[self.me], self.sems, self.base + k, {self.axis: to})
            copy.start()
            self.sent.append(copy)
        self.local.start()

    def wait(self):
        self.local.wait()
        for k in range(1, N):
            source = lax.rem(self.me + N - k, N)
            remote(
                self.piece(source), self.out.at[source], self.sems, self.base + k, {self.axis: source}
            ).wait_recv()
        for copy in self.sent:
            copy.wait_send()


def spread_inputs(meta, probe, cells, frames, meta_out, probe_out, cells_out, frames_out, sems):
    row, col = lax.axis_index("rows"), lax.axis_index("cols")
    sibling = row + 1 - 2 * lax.rem(row, 2)
    across = lax.rem(row + 2, N)
    greet(("rows", "cols"))
    blocks = Gather("cols", cells, cells_out.at[row], sems, 0)
    blocks.start()
    small = Gather("rows", meta, meta_out, sems, 4)
    small.start()
    modes = Gather("cols", probe, probe_out, sems, 8)
    modes.start()
    local_frames = pltpu.make_async_copy(frames, frames_out.at[row], sems.at[0, 12])

    @pl.when(row == col)
    def _():
        local_frames.start()

    for k in range(1, N):

        @pl.when(lax.rem(row + k, N) == col)
        def _():
            remote(frames, frames_out.at[row], sems, 12 + k, {"rows": lax.rem(row + k, N)}).start()

    started = []
    for k in range(N):
        source = lax.rem(col + N - k, N)
        mine = cells_out.at[row, source]
        if k == 0:
            blocks.local.wait()
        else:
            remote(cells, mine, sems, k, {"cols": source}).wait_recv()
        for slot, to in ((16 + k, across), (20 + k, sibling)):
            copy = remote(mine, mine, sems, slot, {"rows": to})
            copy.start()
            started.append(copy)
    for k in range(N):
        source = lax.rem(col + N - k, N)
        landed = cells_out.at[across, source]
        remote(landed, landed, sems, 16 + k, {"rows": across}).wait_recv()
        copy = remote(landed, landed, sems, 24 + k, {"rows": sibling})
        copy.start()
        started.append(copy)
    opposite = lax.rem(sibling + 2, N)
    for k in range(N):
        source = lax.rem(col + N - k, N)
        near = cells_out.at[sibling, source]
        remote(near, near, sems, 20 + k, {"rows": sibling}).wait_recv()
        far = cells_out.at[opposite, source]
        remote(far, far, sems, 24 + k, {"rows": sibling}).wait_recv()
    for copy in started + blocks.sent:
        copy.wait_send()
    small.wait()
    modes.wait()

    @pl.when(row == col)
    def _():
        local_frames.wait()
        for k in range(1, N):
            source = lax.rem(row + N - k, N)
            remote(frames, frames_out.at[source], sems, 12 + k, {"rows": source}).wait_recv()

    for k in range(1, N):

        @pl.when(lax.rem(row + k, N) == col)
        def _():
            remote(frames, frames_out.at[row], sems, 12 + k, {"rows": lax.rem(row + k, N)}).wait_send()


def exchange_intensity(intensity, frames, parts_out, frames_out, sems):
    row, col = lax.axis_index("rows"), lax.axis_index("cols")
    greet(("rows", "cols"))
    parts = Gather("rows", intensity, parts_out, sems, 0, scatter=True)
    parts.start()

    @pl.when(row == col)
    def _():
        local = pltpu.make_async_copy(frames.at[col], frames_out, sems.at[0, 4])
        copies = []
        for k in range(1, N):
            to = lax.rem(col + k, N)
            copies.append(remote(frames.at[to], frames_out, sems, 4 + k, {"cols": to}))
            copies[-1].start()
        local.start()
        local.wait()
        for copy in copies:
            copy.wait_send()

    for k in range(1, N):

        @pl.when(lax.rem(row + k, N) == col)
        def _():
            remote(frames.at[col], frames_out, sems, 4 + k, {"cols": row}).wait_recv()

    parts.wait()


def gather_factors(factor, out, sems):
    greet(("rows",))
    job = Gather("rows", factor, out, sems, 0)
    job.start()
    job.wait()


def scatter_gradients(probe_grad, cells_grad, probe_out, cells_out, sems):
    greet(("rows", "cols"))
    jobs = [
        Gather("cols", probe_grad, probe_out, sems, 0, scatter=True),
        Gather("rows", cells_grad, cells_out, sems, 4, scatter=True),
    ]
    for job in jobs:
        job.start()
    for job in jobs:
        job.wait()


def finish_gradients(cells_grad, probe_grad, cells_out, probe_out, sems):
    greet(("rows", "cols"))
    jobs = [
        Gather("cols", cells_grad, cells_out, sems, 0, scatter=True),
        Gather("rows", probe_grad, probe_out, sems, 4),
    ]
    for job in jobs:
        job.start()
    for job in jobs:
        job.wait()


def communicate(kernel, number, slots, outs, *args):
    return pl.pallas_call(
        kernel,
        out_shape=[jax.ShapeDtypeStruct(shape, dtype) for shape, dtype in outs],
        in_specs=[ANY] * len(args),
        out_specs=[ANY] * len(outs),
        scratch_shapes=[pltpu.SemaphoreType.DMA((2, slots))],
        compiler_params=pltpu.CompilerParams(collective_id=number, has_side_effects=True),
        name=kernel.__name__,
    )(*args)


def mul(left, right):
    return jnp.dot(left, right, preferred_element_type=jnp.float32)


def mul_t(left, right):
    return lax.dot_general(left, right, (((1,), (1,)), ((), ())), preferred_element_type=jnp.float32)


def forward(rows, cols, cells, probe, cosine, sine, patch_out, field_out, power_out, window):
    p = pl.program_id(0)
    strips, blocks, _, width, depth = cells.shape
    length = cosine.shape[0]
    all_rows, all_cols = strips * depth, blocks * width

    @pl.when(p == 0)
    def _():
        for part, fill in ((0, 1.0), (1, 0.0)):
            window[part, all_cols:, :] = jnp.full((width, window.shape[2]), fill, jnp.float32)
            window[part, :all_cols, all_rows:] = jnp.full((all_cols, length), fill, jnp.float32)
            for s in range(strips):
                for b in range(blocks):
                    window[part, pl.ds(b * width, width), pl.ds(s * depth, depth)] = cells[s, b, part].astype(
                        jnp.float32
                    )

    first = rows[p]
    rest = lax.rem(first, 128)
    base = pl.multiple_of(first - rest, 128)
    span = length + 128
    patch = []
    for part in range(2):
        block = pltpu.roll(window[part, :, pl.ds(base, span)], lax.rem(span - rest, span), 1)[:, :length]
        tall = window.shape[1]
        patch.append(pltpu.roll(block, lax.rem(tall - cols[p], tall), 0)[:length])
        patch_out[0, part] = patch[part].astype(jnp.bfloat16)
    probe_real = probe[:, 0].reshape(length, length).astype(jnp.float32)
    probe_imag = probe[:, 1].reshape(length, length).astype(jnp.float32)
    wave_real = (probe_real * patch[0] - probe_imag * patch[1]).astype(jnp.bfloat16)
    wave_imag = (probe_real * patch[1] + probe_imag * patch[0]).astype(jnp.bfloat16)
    c, s = cosine[...], sine[...]
    spread_real = (mul_t(c, wave_real) + mul_t(s, wave_imag)).astype(jnp.bfloat16)
    spread_imag = (mul_t(c, wave_imag) - mul_t(s, wave_real)).astype(jnp.bfloat16)
    field_real = mul(spread_real, c) + mul(spread_imag, s)
    field_imag = mul(spread_imag, c) - mul(spread_real, s)
    field_out[0, 0] = field_real
    field_out[0, 1] = field_imag
    power = field_real * field_real + field_imag * field_imag
    power_out[:, 0] = power.reshape(N, length // N, length).astype(jnp.bfloat16)


def backward(
    rows, cols, factor, field, patch, probe, cosine, sine, probe_out, cells_out, window, total, padded
):
    p = pl.program_id(0)
    strips, blocks, _, width, depth = cells_out.shape
    length = cosine.shape[0]
    span = length + 128

    @pl.when(p == 0)
    def _():
        window[...] = jnp.zeros(window.shape, jnp.float32)
        total[...] = jnp.zeros(total.shape, jnp.float32)
        padded[...] = jnp.zeros(padded.shape, jnp.float32)

    scale = factor[:, 0].reshape(length, length).astype(jnp.float32)
    c, s = cosine[...], sine[...]
    corrected_real = (field[0, 0] * scale).astype(jnp.bfloat16)
    corrected_imag = (field[0, 1] * scale).astype(jnp.bfloat16)
    inner_real = (mul_t(c, corrected_real) - mul_t(s, corrected_imag)).astype(jnp.bfloat16)
    inner_imag = (mul_t(c, corrected_imag) + mul_t(s, corrected_real)).astype(jnp.bfloat16)
    back_real = mul(inner_real, c) - mul(inner_imag, s)
    back_imag = mul(inner_imag, c) + mul(inner_real, s)
    patch_real = patch[0, 0].astype(jnp.float32)
    patch_imag = patch[0, 1].astype(jnp.float32)
    total[0] += patch_real * back_real + patch_imag * back_imag
    total[1] += patch_real * back_imag - patch_imag * back_real
    probe_real = probe[:, 0].reshape(length, length).astype(jnp.float32)
    probe_imag = probe[:, 1].reshape(length, length).astype(jnp.float32)
    first = rows[p]
    rest = lax.rem(first, 128)
    base = pl.multiple_of(first - rest, 128)
    for part in range(2):
        if part == 0:
            term = probe_real * back_real + probe_imag * back_imag
        else:
            term = probe_real * back_imag - probe_imag * back_real
        padded[:length, :length] = term
        window[part, :, pl.ds(base, span)] += pltpu.roll(pltpu.roll(padded[...], cols[p], 0), rest, 1)

    @pl.when(p == pl.num_programs(0) - 1)
    def _():
        for part in range(2):
            for b in range(blocks):
                probe_out[b, part] = total[part, pl.ds(b * width, width), :].astype(jnp.bfloat16)
                for s in range(strips):
                    cells_out[s, b, part] = window[part, pl.ds(b * width, width), pl.ds(s * depth, depth)].astype(
                        jnp.bfloat16
                    )


def balanced_device(object_field, probe, amplitudes, strip_counts, row_offsets, col_offsets):
    f32, bf16 = jnp.float32, jnp.bfloat16
    width, depth = object_field.shape[1:]
    length = probe.shape[3]
    row, col = lax.axis_index("rows"), lax.axis_index("cols")
    cosine, sine = tables(length)
    meta = jnp.concatenate([strip_counts, row_offsets, col_offsets])
    meta = jnp.pad(meta, (0, 128 - meta.shape[0]))[None, :]
    meta = jnp.broadcast_to(meta, (8, 128))
    mode = lax.dynamic_index_in_dim(probe, row, 0, keepdims=False).astype(bf16)
    meta_all, mode_all, cells, frames_all = communicate(
        spread_inputs,
        1,
        28,
        [
            ((N, 8, 128), jnp.int32),
            ((N,) + mode.shape, bf16),
            ((N, N) + object_field.shape, bf16),
            ((N,) + amplitudes.shape, bf16),
        ],
        meta,
        mode,
        object_field.astype(bf16),
        amplitudes.astype(bf16),
    )
    counts = meta_all[:, 0, 0]
    totals = jnp.cumsum(counts)
    starts = totals - counts
    ids = jnp.arange(POS_AVG * N, dtype=jnp.int32)
    strip_of = jnp.sum((totals[None, :] <= ids[:, None]).astype(jnp.int32), axis=1)
    slot = strip_of * POS_MAX + ids - jnp.take(starts, strip_of)
    rows_all = meta_all[:, 0, 1 : 1 + POS_MAX].reshape(-1)
    cols_all = meta_all[:, 0, 1 + POS_MAX : 1 + 2 * POS_MAX].reshape(-1)
    mine = lax.dynamic_slice(slot, (col * POS_AVG,), (POS_AVG,))
    my_strip = lax.dynamic_slice(strip_of, (col * POS_AVG,), (POS_AVG,))
    first_rows = my_strip * depth + jnp.take(rows_all, mine)
    first_cols = jnp.take(cols_all, mine)
    frames = jnp.take(frames_all.reshape((-1,) + amplitudes.shape[1:]), slot, axis=0)
    frames = frames.reshape((N, POS_AVG) + amplitudes.shape[1:])

    plane = (1, 2, length, length)
    whole = lambda *shape: pl.BlockSpec(shape, lambda p, *_: (0,) * len(shape))
    per_slot = pl.BlockSpec(plane, lambda p, *_: (p, 0, 0, 0))
    quarters = pl.BlockSpec((N, 1, length // N, length), lambda p, *_: (0, p, 0, 0))
    window = pltpu.VMEM((2, N * width + 128, N * depth + length), f32)
    patch, field, power = pl.pallas_call(
        forward,
        grid_spec=pltpu.PrefetchScalarGridSpec(
            num_scalar_prefetch=2,
            grid=(POS_AVG,),
            in_specs=[
                whole(*cells.shape),
                whole(*mode_all.shape),
                whole(length, length),
                whole(length, length),
            ],
            out_specs=[per_slot, per_slot, quarters],
            scratch_shapes=[window],
        ),
        out_shape=[
            jax.ShapeDtypeStruct((POS_AVG,) + plane[1:], bf16),
            jax.ShapeDtypeStruct((POS_AVG,) + plane[1:], f32),
            jax.ShapeDtypeStruct((N, POS_AVG, length // N, length), bf16),
        ],
        compiler_params=pltpu.CompilerParams(vmem_limit_bytes=LIMIT),
        name="forward",
    )(first_rows, first_cols, cells, mode_all, cosine, sine)
    powers, measured = communicate(
        exchange_intensity, 2, 8, [(power.shape, bf16), (power.shape[1:], bf16)], power, frames
    )
    intensity = jnp.sum(powers.astype(f32), axis=0)
    factor = 1.0 - measured.astype(f32) * lax.rsqrt(jnp.maximum(intensity, 0.25))
    (factors,) = communicate(gather_factors, 3, 4, [(power.shape, bf16)], factor.astype(bf16))
    probe_part, cells_part = pl.pallas_call(
        backward,
        grid_spec=pltpu.PrefetchScalarGridSpec(
            num_scalar_prefetch=2,
            grid=(POS_AVG,),
            in_specs=[
                quarters,
                per_slot,
                per_slot,
                whole(*mode_all.shape),
                whole(length, length),
                whole(length, length),
            ],
            out_specs=[whole(*mode_all.shape), whole(*cells.shape)],
            scratch_shapes=[
                window,
                pltpu.VMEM((2, length, length), f32),
                pltpu.VMEM((window.shape[1], length + 128), f32),
            ],
        ),
        out_shape=[jax.ShapeDtypeStruct(mode_all.shape, bf16), jax.ShapeDtypeStruct(cells.shape, bf16)],
        compiler_params=pltpu.CompilerParams(vmem_limit_bytes=LIMIT),
        name="backward",
    )(first_rows, first_cols, factors, field, patch, mode_all, cosine, sine)
    probe_parts, cells_parts = communicate(
        scatter_gradients, 4, 8, [(probe_part.shape, bf16), (cells_part.shape, bf16)], probe_part, cells_part
    )
    probe_sum = jnp.sum(probe_parts.astype(f32), axis=0).astype(bf16)
    cells_sum = jnp.sum(cells_parts.astype(f32), axis=0).astype(bf16)
    cells_last, probe_last = communicate(
        finish_gradients, 5, 8, [(cells_sum.shape, bf16), ((N,) + probe_sum.shape, bf16)], cells_sum, probe_sum
    )
    return jnp.sum(cells_last.astype(f32), axis=0), probe_last.astype(f32)


def solution(mesh):
    on_device = balanced_device if mesh.shape["rows"] == N and mesh.shape["cols"] == N else general_device
    placed = (
        P("groups", "cols", "rows"),
        P("groups", None, "cols", None),
        P(("groups", "rows"), "cols", None),
        P(("groups", "rows")),
        P(("groups", "rows")),
        P(("groups", "rows")),
    )
    return jax.shard_map(
        on_device,
        mesh=mesh,
        in_specs=placed,
        out_specs=(P("groups", "cols", "rows"), P("groups", None, "cols", None)),
        check_vma=False,
    )
```

```python
import functools

import jax
import jax.numpy as jnp
import numpy as np
from jax import lax
from jax.experimental import pallas as pl
from jax.experimental.pallas import tpu as pltpu
from jax.sharding import PartitionSpec as P

POS_AVG = 3
POS_MAX = 6


def shifted(block, axis, distance):
    devices = range(lax.axis_size(axis))
    route = [(i - distance, i) for i in devices if i - distance in devices]
    return lax.ppermute(block, axis, route)


def dft_tables(length):
    indices = jnp.arange(length, dtype=jnp.int32)
    product = indices[:, None] * indices[None, :] % length
    angles = product.astype(jnp.float32) * jnp.float32(2.0 * 3.141592653589793 / length)
    scaling = jnp.float32(1.0 / length**0.5)
    cosine_table = (jnp.cos(angles) * scaling).astype(jnp.bfloat16)
    sine_table = (jnp.sin(angles) * scaling).astype(jnp.bfloat16)
    return (cosine_table, sine_table)


def leading(values, matrix):
    return jnp.einsum("mca,asu->mscu", values, matrix, preferred_element_type=jnp.float32)


def second(values, matrix):
    return jnp.einsum("mscu,scv->muv", values, matrix, preferred_element_type=jnp.float32)


def third(values, matrix):
    return jnp.einsum("muv,vsb->msub", values, matrix, preferred_element_type=jnp.float32)


def fourth(values, matrix):
    return jnp.einsum("msub,sua->mba", values, matrix, preferred_element_type=jnp.float32)


def vacuum_where(block, outside):
    fill_real = jnp.where(outside, jnp.float32(1.0), block[0])
    fill_imag = jnp.where(outside, jnp.float32(0.0), block[1])
    return jnp.stack([fill_real, fill_imag])


def spectral_pass(patch_cells, probe, measured, cosine_table, sine_table, block_count):
    mode_count = probe.shape[0]
    block_cols = patch_cells.shape[1]
    length = patch_cells.shape[2]
    block_freq = length // block_count
    probe_real = probe[:, 0]
    probe_imag = probe[:, 1]
    patch_real = patch_cells[0]
    patch_imag = patch_cells[1]
    wave_real = (probe_real * patch_real - probe_imag * patch_imag).astype(jnp.bfloat16)
    wave_imag = (probe_real * patch_imag + probe_imag * patch_real).astype(jnp.bfloat16)
    cos_lead = cosine_table.reshape(length, block_count, block_freq)
    sin_lead = sine_table.reshape(length, block_count, block_freq)
    first_real = leading(wave_real, cos_lead) + leading(wave_imag, sin_lead)
    first_imag = leading(wave_imag, cos_lead) - leading(wave_real, sin_lead)
    outgoing = jnp.stack([first_real, first_imag], axis=1).astype(jnp.bfloat16)
    outgoing = outgoing.reshape(mode_count, 2, block_count, block_cols * block_freq)
    arrived = lax.all_to_all(outgoing, "cols", split_axis=2, concat_axis=2, tiled=True)
    arrived = arrived.reshape(mode_count, 2, block_count, block_cols, block_freq)
    cos_rows = cosine_table.reshape(block_count, block_cols, length)
    sin_rows = sine_table.reshape(block_count, block_cols, length)
    field_real = second(arrived[:, 0], cos_rows) + second(arrived[:, 1], sin_rows)
    field_imag = second(arrived[:, 1], cos_rows) - second(arrived[:, 0], sin_rows)
    intensity = jnp.sum(field_real * field_real + field_imag * field_imag, axis=0)
    modulus = jnp.sqrt(jnp.maximum(intensity, 0.25))
    factor = 1.0 - measured / modulus
    back_real = (field_real * factor).astype(jnp.bfloat16)
    back_imag = (field_imag * factor).astype(jnp.bfloat16)
    cos_back = cosine_table.reshape(length, block_count, block_cols)
    sin_back = sine_table.reshape(length, block_count, block_cols)
    inner_real = third(back_real, cos_back) - third(back_imag, sin_back)
    inner_imag = third(back_imag, cos_back) + third(back_real, sin_back)
    returning = jnp.stack([inner_real, inner_imag], axis=1).astype(jnp.bfloat16)
    returning = returning.reshape(mode_count, 2, block_count, block_freq * block_cols)
    landed = lax.all_to_all(returning, "cols", split_axis=2, concat_axis=2, tiled=True)
    landed = landed.reshape(mode_count, 2, block_count, block_freq, block_cols)
    cos_freq = cosine_table.reshape(block_count, block_freq, length)
    sin_freq = sine_table.reshape(block_count, block_freq, length)
    grad_real = fourth(landed[:, 0], cos_freq) - fourth(landed[:, 1], sin_freq)
    grad_imag = fourth(landed[:, 1], cos_freq) + fourth(landed[:, 0], sin_freq)
    object_real = jnp.sum(probe_real * grad_real + probe_imag * grad_imag, axis=0)
    object_imag = jnp.sum(probe_real * grad_imag - probe_imag * grad_real, axis=0)
    probe_real_term = patch_real * grad_real + patch_imag * grad_imag
    probe_imag_term = patch_real * grad_imag - patch_imag * grad_real
    return (
        jnp.stack([object_real, object_imag]),
        jnp.stack([probe_real_term, probe_imag_term], axis=1),
    )


def run_positions(
    window,
    probe,
    frames,
    first_rows,
    first_cols,
    slot_total,
    used_count,
    cosine_table,
    sine_table,
    block_count,
):
    block_cols = probe.shape[2]
    length = probe.shape[3]

    def visit_slot(slot_index, state_pair):
        window_grad, probe_sum = state_pair
        first_row = first_rows[slot_index]
        first_col = first_cols[slot_index]
        patch_cells = lax.dynamic_slice(window, (0, first_col, first_row), (2, block_cols, length))
        measured = lax.dynamic_index_in_dim(frames, slot_index, 0, keepdims=False)
        object_term, probe_term = spectral_pass(
            patch_cells, probe, measured, cosine_table, sine_table, block_count
        )
        active = (slot_index < used_count).astype(jnp.float32)
        current = lax.dynamic_slice(window_grad, (0, first_col, first_row), (2, block_cols, length))
        window_grad = lax.dynamic_update_slice(
            window_grad, current + active * object_term, (0, first_col, first_row)
        )
        return (window_grad, probe_sum + active * probe_term)

    initial = (jnp.zeros(window.shape, jnp.float32), jnp.zeros(probe.shape, jnp.float32))
    return lax.fori_loop(0, slot_total, visit_slot, initial)


def general_device(object_field, probe, amplitudes, strip_counts, row_offsets, col_offsets):
    block_cols = object_field.shape[1]
    strip_rows = object_field.shape[2]
    length = probe.shape[3]
    block_count = lax.axis_size("cols")
    strip_total = lax.axis_size("rows")
    cosine_table, sine_table = dft_tables(length)
    beside = shifted(object_field, "cols", -1)
    beside = vacuum_where(beside, lax.axis_index("cols") == block_count - 1)
    paired = jnp.concatenate([object_field, beside], axis=1)
    counts_all, rows_all, cols_all = (
        lax.all_gather(strip_counts, "rows", axis=0, tiled=True),
        lax.all_gather(row_offsets, "rows", axis=0, tiled=True),
        lax.all_gather(col_offsets, "rows", axis=0, tiled=True),
    )
    totals = jnp.cumsum(counts_all)
    starts = totals - counts_all
    position_block = (lax.axis_index("rows") + strip_total // 2) % strip_total
    my_positions = position_block * POS_AVG + jnp.arange(POS_AVG, dtype=jnp.int32)
    strip_of = jnp.sum((totals[None, :] <= my_positions[:, None]).astype(jnp.int32), axis=1)
    wanted = strip_of * POS_MAX + my_positions - jnp.take(starts, strip_of)
    first_rows = strip_of * strip_rows + jnp.take(rows_all, wanted)
    first_cols = jnp.take(cols_all, wanted)
    empty_frames = jnp.zeros((POS_AVG,) + amplitudes.shape[1:], jnp.float32)
    received = lax.all_gather(amplitudes, "rows", axis=0, tiled=True)
    inside = (wanted >= 0) & (wanted < received.shape[0])
    picked = jnp.take(received, jnp.clip(wanted, 0, received.shape[0] - 1), axis=0)
    frames = jnp.where(inside[:, None, None], picked, empty_frames)
    column_all = lax.all_gather(paired, "rows", axis=2, tiled=True)
    all_rows = column_all.shape[2]
    vacuum_tail = vacuum_where(jnp.zeros((2, column_all.shape[1], length), jnp.float32), True)
    window = jnp.concatenate([column_all, vacuum_tail], axis=2)
    window_grad, probe_sum = run_positions(
        window,
        probe,
        frames,
        first_rows,
        first_cols,
        POS_AVG,
        POS_AVG,
        cosine_table,
        sine_table,
        block_count,
    )
    folded = window_grad[:, :, :all_rows]
    summed = lax.psum_scatter(folded, "rows", scatter_dimension=2, tiled=True)
    upper_half = shifted(summed[:, block_cols:], "cols", 1)
    object_grad = summed[:, :block_cols] + upper_half
    probe_grad = lax.psum(probe_sum, "rows")
    return (object_grad, probe_grad)


def tables(length):
    indices = np.arange(length)
    angles = (indices[:, None] * indices[None, :] % length) * (2.0 * np.pi / length)
    scaling = 1.0 / length**0.5
    cosine, sine = np.cos(angles) * scaling, np.sin(angles) * scaling
    table = np.block([[cosine, -sine], [sine, cosine]])
    return jnp.asarray(table, jnp.bfloat16), jnp.asarray(table.T, jnp.bfloat16)


ANY = pl.BlockSpec(memory_space=pl.ANY)
WHOLE = pl.BlockSpec(memory_space=pltpu.VMEM)
LIMIT = 56 * 1024 * 1024
N = 4


def greet(axes):
    barrier = pltpu.get_barrier_semaphore()
    for axis in axes:
        me = lax.axis_index(axis)
        for k in range(1, N):
            pl.semaphore_signal(
                barrier, inc=1, device_id={axis: lax.rem(me + k, N)}, device_id_type=pl.DeviceIdType.MESH
            )
    pl.semaphore_wait(barrier, (N - 1) * len(axes))


def remote(src, dst, sems, slot, device):
    return pltpu.make_async_remote_copy(
        src_ref=src,
        dst_ref=dst,
        send_sem=sems.at[0, slot],
        recv_sem=sems.at[1, slot],
        device_id=device,
        device_id_type=pl.DeviceIdType.MESH,
    )


class Gather:
    def __init__(self, axis, src, out, sems, base, scatter=False):
        self.me = lax.axis_index(axis)
        self.axis, self.src, self.out, self.sems, self.base, self.scatter = axis, src, out, sems, base, scatter

    def piece(self, index):
        return self.src.at[index] if self.scatter else self.src

    def start(self):
        self.local = pltpu.make_async_copy(
            self.piece(self.me), self.out.at[self.me], self.sems.at[0, self.base]
        )
        self.sent = []
        for k in range(1, N):
            to = lax.rem(self.me + k, N)
            copy = remote(self.piece(to), self.out.at[self.me], self.sems, self.base + k, {self.axis: to})
            copy.start()
            self.sent.append(copy)
        self.local.start()

    def wait(self):
        self.local.wait()
        for k in range(1, N):
            source = lax.rem(self.me + N - k, N)
            remote(
                self.piece(source), self.out.at[source], self.sems, self.base + k, {self.axis: source}
            ).wait_recv()
        for copy in self.sent:
            copy.wait_send()


def spread_inputs(meta, probe, cells, frames, meta_out, probe_out, cells_out, frames_out, sems):
    row, col = lax.axis_index("rows"), lax.axis_index("cols")
    sibling = row + 1 - 2 * lax.rem(row, 2)
    across = lax.rem(row + 2, N)
    greet(("rows", "cols"))
    blocks = Gather("cols", cells, cells_out.at[row], sems, 0)
    blocks.start()
    small = Gather("rows", meta, meta_out, sems, 4)
    small.start()
    modes = Gather("cols", probe, probe_out, sems, 8)
    modes.start()
    local_frames = pltpu.make_async_copy(frames, frames_out.at[row], sems.at[0, 12])

    @pl.when(row == col)
    def _():
        local_frames.start()

    for k in range(1, N):

        @pl.when(lax.rem(row + k, N) == col)
        def _():
            remote(frames, frames_out.at[row], sems, 12 + k, {"rows": lax.rem(row + k, N)}).start()

    started = []
    for k in range(N):
        source = lax.rem(col + N - k, N)
        mine = cells_out.at[row, source]
        if k == 0:
            blocks.local.wait()
        else:
            remote(cells, mine, sems, k, {"cols": source}).wait_recv()
        for slot, to in ((16 + k, across), (20 + k, sibling)):
            copy = remote(mine, mine, sems, slot, {"rows": to})
            copy.start()
            started.append(copy)
    for k in range(N):
        source = lax.rem(col + N - k, N)
        landed = cells_out.at[across, source]
        remote(landed, landed, sems, 16 + k, {"rows": across}).wait_recv()
        copy = remote(landed, landed, sems, 24 + k, {"rows": sibling})
        copy.start()
        started.append(copy)
    opposite = lax.rem(sibling + 2, N)
    for k in range(N):
        source = lax.rem(col + N - k, N)
        near = cells_out.at[sibling, source]
        remote(near, near, sems, 20 + k, {"rows": sibling}).wait_recv()
        far = cells_out.at[opposite, source]
        remote(far, far, sems, 24 + k, {"rows": sibling}).wait_recv()
    for copy in started + blocks.sent:
        copy.wait_send()
    small.wait()
    modes.wait()

    @pl.when(row == col)
    def _():
        local_frames.wait()
        for k in range(1, N):
            source = lax.rem(row + N - k, N)
            remote(frames, frames_out.at[source], sems, 12 + k, {"rows": source}).wait_recv()

    for k in range(1, N):

        @pl.when(lax.rem(row + k, N) == col)
        def _():
            remote(frames, frames_out.at[row], sems, 12 + k, {"rows": lax.rem(row + k, N)}).wait_send()


def propagate(
    patch, probe, frames, table, table_t, probe_out, terms, field, power, parts, scale, measured, wide, tall, total, sems
):
    row, col = lax.axis_index("rows"), lax.axis_index("cols")
    length = patch.shape[-1]
    quarter = length // N
    f32, bf16 = jnp.float32, jnp.bfloat16
    greet(("rows", "cols"))

    def frame_copy(to):
        return remote(frames.at[to], measured, sems, 18 + lax.rem(to + N - row, N), {"cols": to})

    local_frames = pltpu.make_async_copy(frames.at[col], measured, sems.at[0, 18])

    @pl.when(row == col)
    def _():
        local_frames.start()
        for k in range(1, N):
            frame_copy(lax.rem(col + k, N)).start()

    def power_copy(p, k):
        to = lax.rem(row + k, N)
        return remote(power.at[p, to], parts.at[p, k - 1], sems, p * 3 + k - 1, {"rows": to})

    def scale_copy(p, k, index):
        to = lax.rem(row + k, N)
        return remote(scale.at[p, index], scale.at[p, index], sems, 9 + p * 3 + k - 1, {"rows": to})

    def factors(p):
        for k in range(1, N):
            power_copy(p, k).wait_recv()
        intensity = power[p, row].astype(f32)
        for k in range(1, N):
            intensity += parts[p, k - 1].astype(f32)
        amplitude = measured[p].astype(f32).T
        scale[p, row] = (1.0 - amplitude * lax.rsqrt(jnp.maximum(intensity, 0.25))).astype(bf16)
        for k in range(1, N):
            scale_copy(p, k, row).start()

    def transform(p, carry):
        probe_real = probe[:, 0].reshape(length, length).astype(f32)
        probe_imag = probe[:, 1].reshape(length, length).astype(f32)
        patch_real = patch[p, 0].astype(f32)
        patch_imag = patch[p, 1].astype(f32)
        wide[:, :length] = (probe_real * patch_real - probe_imag * patch_imag).astype(bf16)
        wide[:, length:] = (probe_real * patch_imag + probe_imag * patch_real).astype(bf16)
        spread = mul(wide[...], table[...])
        tall[:length] = spread[:, :length].astype(bf16)
        tall[length:] = spread[:, length:].astype(bf16)
        result = mul(table_t[...], tall[...])
        field[p] = result
        square = result[:length] * result[:length] + result[length:] * result[length:]
        for q in range(N):
            power[p, q] = square[:, q * quarter : (q + 1) * quarter].astype(bf16)
        for k in range(1, N):
            power_copy(p, k).start()

        @pl.when(p == 1)
        def _():
            @pl.when(row == col)
            def _():
                local_frames.wait()

            for k in range(1, N):

                @pl.when(lax.rem(row + k, N) == col)
                def _():
                    remote(measured, measured, sems, 18 + k, {"cols": row}).wait_recv()

        @pl.when(p >= 1)
        def _():
            factors(p - 1)

        return carry

    lax.fori_loop(0, POS_AVG, transform, 0)
    total[...] = jnp.zeros(total.shape, f32)

    def back_transform(p, carry):
        for k in range(1, N):
            scale_copy(p, k, lax.rem(row + N - k, N)).wait_recv()
        for q in range(N):
            lanes = pl.ds(q * quarter, quarter)
            gain = scale[p, q].astype(f32)
            tall[:length, lanes] = (field[p, :length, lanes] * gain).astype(bf16)
            tall[length:, lanes] = (field[p, length:, lanes] * gain).astype(bf16)
        inner = mul(table[...], tall[...])
        wide[:, :length] = inner[:length].astype(bf16)
        wide[:, length:] = inner[length:].astype(bf16)
        back = mul(wide[...], table_t[...])
        back_real, back_imag = back[:, :length], back[:, length:]
        probe_real = probe[:, 0].reshape(length, length).astype(f32)
        probe_imag = probe[:, 1].reshape(length, length).astype(f32)
        terms[p, 0] = probe_real * back_real + probe_imag * back_imag
        terms[p, 1] = probe_real * back_imag - probe_imag * back_real
        patch_real = patch[p, 0].astype(f32)
        patch_imag = patch[p, 1].astype(f32)
        total[0] += patch_real * back_real + patch_imag * back_imag
        total[1] += patch_real * back_imag - patch_imag * back_real

        @pl.when(p == 0)
        def _():
            factors(POS_AVG - 1)

        return carry

    lax.fori_loop(0, POS_AVG, back_transform, 0)
    for b in range(N):
        for part in range(2):
            probe_out[b, part] = total[part, b * quarter : (b + 1) * quarter].astype(bf16)

    def finish(p, carry):
        for k in range(1, N):
            power_copy(p, k).wait_send()
            scale_copy(p, k, row).wait_send()
        return carry

    lax.fori_loop(0, POS_AVG, finish, 0)

    @pl.when(row == col)
    def _():
        for k in range(1, N):
            frame_copy(lax.rem(col + k, N)).wait_send()


def scatter_gradients(probe_grad, cells_grad, probe_out, cells_out, sems):
    greet(("rows", "cols"))
    jobs = [
        Gather("cols", probe_grad, probe_out, sems, 0, scatter=True),
        Gather("rows", cells_grad, cells_out, sems, 4, scatter=True),
    ]
    for job in jobs:
        job.start()
    for job in jobs:
        job.wait()


def finish_gradients(cells_grad, probe_grad, cells_out, probe_out, sems):
    greet(("rows", "cols"))
    jobs = [
        Gather("cols", cells_grad, cells_out, sems, 0, scatter=True),
        Gather("rows", probe_grad, probe_out, sems, 4),
    ]
    for job in jobs:
        job.start()
    for job in jobs:
        job.wait()


def communicate(kernel, number, slots, outs, *args):
    return pl.pallas_call(
        kernel,
        out_shape=[jax.ShapeDtypeStruct(shape, dtype) for shape, dtype in outs],
        in_specs=[ANY] * len(args),
        out_specs=[ANY] * len(outs),
        scratch_shapes=[pltpu.SemaphoreType.DMA((2, slots))],
        compiler_params=pltpu.CompilerParams(collective_id=number, has_side_effects=True),
        name=kernel.__name__,
    )(*args)


def mul(left, right):
    return jnp.dot(left, right, preferred_element_type=jnp.float32)


def cut(rows, cols, cells, patch_out, window):
    p = pl.program_id(0)
    strips, blocks, _, width, depth = cells.shape
    length = patch_out.shape[-1]
    all_rows, all_cols = strips * depth, blocks * width

    @pl.when(p == 0)
    def _():
        for part, fill in ((0, 1.0), (1, 0.0)):
            window[part, all_cols:, :] = jnp.full((width, window.shape[2]), fill, jnp.float32)
            window[part, :all_cols, all_rows:] = jnp.full((all_cols, length), fill, jnp.float32)
            for s in range(strips):
                for b in range(blocks):
                    window[part, pl.ds(b * width, width), pl.ds(s * depth, depth)] = cells[s, b, part].astype(
                        jnp.float32
                    )

    first = rows[p]
    rest = lax.rem(first, 128)
    base = pl.multiple_of(first - rest, 128)
    span = length + 128
    tall = window.shape[1]
    for part in range(2):
        block = pltpu.roll(window[part, :, pl.ds(base, span)], lax.rem(span - rest, span), 1)[:, :length]
        block = pltpu.roll(block, lax.rem(tall - cols[p], tall), 0)[:length]
        patch_out[0, part] = block.astype(jnp.bfloat16)


def place(rows, cols, terms, cells_out, window, padded):
    p = pl.program_id(0)
    strips, blocks, _, width, depth = cells_out.shape
    length = terms.shape[-1]
    span = length + 128

    @pl.when(p == 0)
    def _():
        window[...] = jnp.zeros(window.shape, jnp.float32)
        padded[...] = jnp.zeros(padded.shape, jnp.float32)

    first = rows[p]
    rest = lax.rem(first, 128)
    base = pl.multiple_of(first - rest, 128)
    for part in range(2):
        padded[:length, :length] = terms[0, part]
        window[part, :, pl.ds(base, span)] += pltpu.roll(pltpu.roll(padded[...], cols[p], 0), rest, 1)

    @pl.when(p == pl.num_programs(0) - 1)
    def _():
        for part in range(2):
            for b in range(blocks):
                for s in range(strips):
                    cells_out[s, b, part] = window[part, pl.ds(b * width, width), pl.ds(s * depth, depth)].astype(
                        jnp.bfloat16
                    )


def balanced_device(object_field, probe, amplitudes, strip_counts, row_offsets, col_offsets):
    f32, bf16 = jnp.float32, jnp.bfloat16
    width, depth = object_field.shape[1:]
    length = probe.shape[3]
    row, col = lax.axis_index("rows"), lax.axis_index("cols")
    table, table_t = tables(length)
    meta = jnp.concatenate([strip_counts, row_offsets, col_offsets])
    meta = jnp.pad(meta, (0, 128 - meta.shape[0]))[None, :]
    meta = jnp.broadcast_to(meta, (8, 128))
    mode = lax.dynamic_index_in_dim(probe, row, 0, keepdims=False).astype(bf16)
    meta_all, mode_all, cells, frames_all = communicate(
        spread_inputs,
        1,
        28,
        [
            ((N, 8, 128), jnp.int32),
            ((N,) + mode.shape, bf16),
            ((N, N) + object_field.shape, bf16),
            ((N,) + amplitudes.shape, bf16),
        ],
        meta,
        mode,
        object_field.astype(bf16),
        amplitudes.astype(bf16),
    )
    counts = meta_all[:, 0, 0]
    totals = jnp.cumsum(counts)
    starts = totals - counts
    ids = jnp.arange(POS_AVG * N, dtype=jnp.int32)
    strip_of = jnp.sum((totals[None, :] <= ids[:, None]).astype(jnp.int32), axis=1)
    slot = strip_of * POS_MAX + ids - jnp.take(starts, strip_of)
    rows_all = meta_all[:, 0, 1 : 1 + POS_MAX].reshape(-1)
    cols_all = meta_all[:, 0, 1 + POS_MAX : 1 + 2 * POS_MAX].reshape(-1)
    mine = lax.dynamic_slice(slot, (col * POS_AVG,), (POS_AVG,))
    my_strip = lax.dynamic_slice(strip_of, (col * POS_AVG,), (POS_AVG,))
    first_rows = my_strip * depth + jnp.take(rows_all, mine)
    first_cols = jnp.take(cols_all, mine)
    frames = jnp.take(frames_all.reshape((-1,) + amplitudes.shape[1:]), slot, axis=0, mode="clip")
    frames = frames.reshape((N, POS_AVG) + amplitudes.shape[1:])

    plane = (1, 2, length, length)
    whole = lambda *shape: pl.BlockSpec(shape, lambda p, *_: (0,) * len(shape))
    per_slot = pl.BlockSpec(plane, lambda p, *_: (p, 0, 0, 0))
    window = pltpu.VMEM((2, N * width + 128, N * depth + length), f32)
    quarters = (POS_AVG, N, length, length // N)
    patch = pl.pallas_call(
        cut,
        grid_spec=pltpu.PrefetchScalarGridSpec(
            num_scalar_prefetch=2,
            grid=(POS_AVG,),
            in_specs=[whole(*cells.shape)],
            out_specs=per_slot,
            scratch_shapes=[window],
        ),
        out_shape=jax.ShapeDtypeStruct((POS_AVG,) + plane[1:], bf16),
        compiler_params=pltpu.CompilerParams(vmem_limit_bytes=LIMIT),
        name="cut",
    )(first_rows, first_cols, cells)
    probe_part, terms = pl.pallas_call(
        propagate,
        in_specs=[WHOLE, WHOLE, ANY, WHOLE, WHOLE],
        out_specs=[WHOLE, WHOLE],
        out_shape=[
            jax.ShapeDtypeStruct(mode_all.shape, bf16),
            jax.ShapeDtypeStruct((POS_AVG,) + plane[1:], f32),
        ],
        scratch_shapes=[
            pltpu.VMEM((POS_AVG, 2 * length, length), f32),
            pltpu.VMEM(quarters, bf16),
            pltpu.VMEM((POS_AVG, N - 1) + quarters[2:], bf16),
            pltpu.VMEM(quarters, bf16),
            pltpu.VMEM(frames.shape[1:], bf16),
            pltpu.VMEM((length, 2 * length), bf16),
            pltpu.VMEM((2 * length, length), bf16),
            pltpu.VMEM((2, length, length), f32),
            pltpu.SemaphoreType.DMA((2, 22)),
        ],
        compiler_params=pltpu.CompilerParams(collective_id=2, has_side_effects=True, vmem_limit_bytes=LIMIT),
        name="propagate",
    )(patch, mode_all, frames, table, table_t)
    cells_part = pl.pallas_call(
        place,
        grid_spec=pltpu.PrefetchScalarGridSpec(
            num_scalar_prefetch=2,
            grid=(POS_AVG,),
            in_specs=[per_slot],
            out_specs=whole(*cells.shape),
            scratch_shapes=[window, pltpu.VMEM((window.shape[1], length + 128), f32)],
        ),
        out_shape=jax.ShapeDtypeStruct(cells.shape, bf16),
        compiler_params=pltpu.CompilerParams(vmem_limit_bytes=LIMIT),
        name="place",
    )(first_rows, first_cols, terms)
    probe_parts, cells_parts = communicate(
        scatter_gradients, 4, 8, [(probe_part.shape, bf16), (cells_part.shape, bf16)], probe_part, cells_part
    )
    probe_sum = jnp.sum(probe_parts.astype(f32), axis=0).astype(bf16)
    cells_sum = jnp.sum(cells_parts.astype(f32), axis=0).astype(bf16)
    cells_last, probe_last = communicate(
        finish_gradients, 5, 8, [(cells_sum.shape, bf16), ((N,) + probe_sum.shape, bf16)], cells_sum, probe_sum
    )
    return jnp.sum(cells_last.astype(f32), axis=0), probe_last.astype(f32)


def solution(mesh):
    on_device = balanced_device if mesh.shape["rows"] == N and mesh.shape["cols"] == N else general_device
    placed = (
        P("groups", "cols", "rows"),
        P("groups", None, "cols", None),
        P(("groups", "rows"), "cols", None),
        P(("groups", "rows")),
        P(("groups", "rows")),
        P(("groups", "rows")),
    )
    return jax.shard_map(
        on_device,
        mesh=mesh,
        in_specs=placed,
        out_specs=(P("groups", "cols", "rows"), P("groups", None, "cols", None)),
        check_vma=False,
    )
```

```python
import functools

import jax
import jax.numpy as jnp
import numpy as np
from jax import lax
from jax.experimental import pallas as pl
from jax.experimental.pallas import tpu as pltpu
from jax.sharding import PartitionSpec as P

POS_AVG = 3
POS_MAX = 6


def shifted(block, axis, distance):
    devices = range(lax.axis_size(axis))
    route = [(i - distance, i) for i in devices if i - distance in devices]
    return lax.ppermute(block, axis, route)


def dft_tables(length):
    indices = jnp.arange(length, dtype=jnp.int32)
    product = indices[:, None] * indices[None, :] % length
    angles = product.astype(jnp.float32) * jnp.float32(2.0 * 3.141592653589793 / length)
    scaling = jnp.float32(1.0 / length**0.5)
    cosine_table = (jnp.cos(angles) * scaling).astype(jnp.bfloat16)
    sine_table = (jnp.sin(angles) * scaling).astype(jnp.bfloat16)
    return (cosine_table, sine_table)


def leading(values, matrix):
    return jnp.einsum("mca,asu->mscu", values, matrix, preferred_element_type=jnp.float32)


def second(values, matrix):
    return jnp.einsum("mscu,scv->muv", values, matrix, preferred_element_type=jnp.float32)


def third(values, matrix):
    return jnp.einsum("muv,vsb->msub", values, matrix, preferred_element_type=jnp.float32)


def fourth(values, matrix):
    return jnp.einsum("msub,sua->mba", values, matrix, preferred_element_type=jnp.float32)


def vacuum_where(block, outside):
    fill_real = jnp.where(outside, jnp.float32(1.0), block[0])
    fill_imag = jnp.where(outside, jnp.float32(0.0), block[1])
    return jnp.stack([fill_real, fill_imag])


def spectral_pass(patch_cells, probe, measured, cosine_table, sine_table, block_count):
    mode_count = probe.shape[0]
    block_cols = patch_cells.shape[1]
    length = patch_cells.shape[2]
    block_freq = length // block_count
    probe_real = probe[:, 0]
    probe_imag = probe[:, 1]
    patch_real = patch_cells[0]
    patch_imag = patch_cells[1]
    wave_real = (probe_real * patch_real - probe_imag * patch_imag).astype(jnp.bfloat16)
    wave_imag = (probe_real * patch_imag + probe_imag * patch_real).astype(jnp.bfloat16)
    cos_lead = cosine_table.reshape(length, block_count, block_freq)
    sin_lead = sine_table.reshape(length, block_count, block_freq)
    first_real = leading(wave_real, cos_lead) + leading(wave_imag, sin_lead)
    first_imag = leading(wave_imag, cos_lead) - leading(wave_real, sin_lead)
    outgoing = jnp.stack([first_real, first_imag], axis=1).astype(jnp.bfloat16)
    outgoing = outgoing.reshape(mode_count, 2, block_count, block_cols * block_freq)
    arrived = lax.all_to_all(outgoing, "cols", split_axis=2, concat_axis=2, tiled=True)
    arrived = arrived.reshape(mode_count, 2, block_count, block_cols, block_freq)
    cos_rows = cosine_table.reshape(block_count, block_cols, length)
    sin_rows = sine_table.reshape(block_count, block_cols, length)
    field_real = second(arrived[:, 0], cos_rows) + second(arrived[:, 1], sin_rows)
    field_imag = second(arrived[:, 1], cos_rows) - second(arrived[:, 0], sin_rows)
    intensity = jnp.sum(field_real * field_real + field_imag * field_imag, axis=0)
    modulus = jnp.sqrt(jnp.maximum(intensity, 0.25))
    factor = 1.0 - measured / modulus
    back_real = (field_real * factor).astype(jnp.bfloat16)
    back_imag = (field_imag * factor).astype(jnp.bfloat16)
    cos_back = cosine_table.reshape(length, block_count, block_cols)
    sin_back = sine_table.reshape(length, block_count, block_cols)
    inner_real = third(back_real, cos_back) - third(back_imag, sin_back)
    inner_imag = third(back_imag, cos_back) + third(back_real, sin_back)
    returning = jnp.stack([inner_real, inner_imag], axis=1).astype(jnp.bfloat16)
    returning = returning.reshape(mode_count, 2, block_count, block_freq * block_cols)
    landed = lax.all_to_all(returning, "cols", split_axis=2, concat_axis=2, tiled=True)
    landed = landed.reshape(mode_count, 2, block_count, block_freq, block_cols)
    cos_freq = cosine_table.reshape(block_count, block_freq, length)
    sin_freq = sine_table.reshape(block_count, block_freq, length)
    grad_real = fourth(landed[:, 0], cos_freq) - fourth(landed[:, 1], sin_freq)
    grad_imag = fourth(landed[:, 1], cos_freq) + fourth(landed[:, 0], sin_freq)
    object_real = jnp.sum(probe_real * grad_real + probe_imag * grad_imag, axis=0)
    object_imag = jnp.sum(probe_real * grad_imag - probe_imag * grad_real, axis=0)
    probe_real_term = patch_real * grad_real + patch_imag * grad_imag
    probe_imag_term = patch_real * grad_imag - patch_imag * grad_real
    return (
        jnp.stack([object_real, object_imag]),
        jnp.stack([probe_real_term, probe_imag_term], axis=1),
    )


def run_positions(
    window,
    probe,
    frames,
    first_rows,
    first_cols,
    slot_total,
    used_count,
    cosine_table,
    sine_table,
    block_count,
):
    block_cols = probe.shape[2]
    length = probe.shape[3]

    def visit_slot(slot_index, state_pair):
        window_grad, probe_sum = state_pair
        first_row = first_rows[slot_index]
        first_col = first_cols[slot_index]
        patch_cells = lax.dynamic_slice(window, (0, first_col, first_row), (2, block_cols, length))
        measured = lax.dynamic_index_in_dim(frames, slot_index, 0, keepdims=False)
        object_term, probe_term = spectral_pass(
            patch_cells, probe, measured, cosine_table, sine_table, block_count
        )
        active = (slot_index < used_count).astype(jnp.float32)
        current = lax.dynamic_slice(window_grad, (0, first_col, first_row), (2, block_cols, length))
        window_grad = lax.dynamic_update_slice(
            window_grad, current + active * object_term, (0, first_col, first_row)
        )
        return (window_grad, probe_sum + active * probe_term)

    initial = (jnp.zeros(window.shape, jnp.float32), jnp.zeros(probe.shape, jnp.float32))
    return lax.fori_loop(0, slot_total, visit_slot, initial)


def general_device(object_field, probe, amplitudes, strip_counts, row_offsets, col_offsets):
    block_cols = object_field.shape[1]
    strip_rows = object_field.shape[2]
    length = probe.shape[3]
    block_count = lax.axis_size("cols")
    strip_total = lax.axis_size("rows")
    cosine_table, sine_table = dft_tables(length)
    beside = shifted(object_field, "cols", -1)
    beside = vacuum_where(beside, lax.axis_index("cols") == block_count - 1)
    paired = jnp.concatenate([object_field, beside], axis=1)
    counts_all, rows_all, cols_all = (
        lax.all_gather(strip_counts, "rows", axis=0, tiled=True),
        lax.all_gather(row_offsets, "rows", axis=0, tiled=True),
        lax.all_gather(col_offsets, "rows", axis=0, tiled=True),
    )
    totals = jnp.cumsum(counts_all)
    starts = totals - counts_all
    position_block = (lax.axis_index("rows") + strip_total // 2) % strip_total
    my_positions = position_block * POS_AVG + jnp.arange(POS_AVG, dtype=jnp.int32)
    strip_of = jnp.sum((totals[None, :] <= my_positions[:, None]).astype(jnp.int32), axis=1)
    wanted = strip_of * POS_MAX + my_positions - jnp.take(starts, strip_of)
    first_rows = strip_of * strip_rows + jnp.take(rows_all, wanted)
    first_cols = jnp.take(cols_all, wanted)
    empty_frames = jnp.zeros((POS_AVG,) + amplitudes.shape[1:], jnp.float32)
    received = lax.all_gather(amplitudes, "rows", axis=0, tiled=True)
    inside = (wanted >= 0) & (wanted < received.shape[0])
    picked = jnp.take(received, jnp.clip(wanted, 0, received.shape[0] - 1), axis=0)
    frames = jnp.where(inside[:, None, None], picked, empty_frames)
    column_all = lax.all_gather(paired, "rows", axis=2, tiled=True)
    all_rows = column_all.shape[2]
    vacuum_tail = vacuum_where(jnp.zeros((2, column_all.shape[1], length), jnp.float32), True)
    window = jnp.concatenate([column_all, vacuum_tail], axis=2)
    window_grad, probe_sum = run_positions(
        window,
        probe,
        frames,
        first_rows,
        first_cols,
        POS_AVG,
        POS_AVG,
        cosine_table,
        sine_table,
        block_count,
    )
    folded = window_grad[:, :, :all_rows]
    summed = lax.psum_scatter(folded, "rows", scatter_dimension=2, tiled=True)
    upper_half = shifted(summed[:, block_cols:], "cols", 1)
    object_grad = summed[:, :block_cols] + upper_half
    probe_grad = lax.psum(probe_sum, "rows")
    return (object_grad, probe_grad)


def tables(length):
    indices = np.arange(length)
    angles = (indices[:, None] * indices[None, :] % length) * (2.0 * np.pi / length)
    scaling = 1.0 / length**0.5
    cosine, sine = np.cos(angles) * scaling, np.sin(angles) * scaling
    table = np.block([[cosine, -sine], [sine, cosine]])
    return jnp.asarray(table, jnp.bfloat16), jnp.asarray(table.T, jnp.bfloat16)


ANY = pl.BlockSpec(memory_space=pl.ANY)
WHOLE = pl.BlockSpec(memory_space=pltpu.VMEM)
LIMIT = 56 * 1024 * 1024
N = 4


def greet(axes):
    barrier = pltpu.get_barrier_semaphore()
    for axis in axes:
        me = lax.axis_index(axis)
        for k in range(1, N):
            pl.semaphore_signal(
                barrier, inc=1, device_id={axis: lax.rem(me + k, N)}, device_id_type=pl.DeviceIdType.MESH
            )
    pl.semaphore_wait(barrier, (N - 1) * len(axes))


def remote(src, dst, sems, slot, device):
    return pltpu.make_async_remote_copy(
        src_ref=src,
        dst_ref=dst,
        send_sem=sems.at[0, slot],
        recv_sem=sems.at[1, slot],
        device_id=device,
        device_id_type=pl.DeviceIdType.MESH,
    )


class Gather:
    def __init__(self, axis, src, out, sems, base, scatter=False):
        self.me = lax.axis_index(axis)
        self.axis, self.src, self.out, self.sems, self.base, self.scatter = axis, src, out, sems, base, scatter

    def piece(self, index):
        return self.src.at[index] if self.scatter else self.src

    def start(self):
        self.local = pltpu.make_async_copy(
            self.piece(self.me), self.out.at[self.me], self.sems.at[0, self.base]
        )
        self.sent = []
        for k in range(1, N):
            to = lax.rem(self.me + k, N)
            copy = remote(self.piece(to), self.out.at[self.me], self.sems, self.base + k, {self.axis: to})
            copy.start()
            self.sent.append(copy)
        self.local.start()

    def wait(self):
        self.local.wait()
        for k in range(1, N):
            source = lax.rem(self.me + N - k, N)
            remote(
                self.piece(source), self.out.at[source], self.sems, self.base + k, {self.axis: source}
            ).wait_recv()
        for copy in self.sent:
            copy.wait_send()


def spread_inputs(
    meta, cells, probe, frames, meta_out, probe_out, cells_out, frames_out,
    raw_probe, raw_frames, own_cells, own_probe, own_frames, sems, local
):
    bf16 = jnp.bfloat16
    row, col = lax.axis_index("rows"), lax.axis_index("cols")
    sibling = row + 1 - 2 * lax.rem(row, 2)
    across = lax.rem(row + 2, N)
    opposite = lax.rem(sibling + 2, N)
    right, left = lax.rem(col + 1, N), lax.rem(col + N - 1, N)
    load_probe = pltpu.make_async_copy(probe.at[row], raw_probe, local.at[0])
    load_frames = pltpu.make_async_copy(frames, raw_frames, local.at[1])
    load_probe.start()
    load_frames.start()
    own_cells[...] = cells[...].astype(bf16)
    greet(("rows", "cols"))

    def line_copy(base, src, dst, origin, rightward):
        return pltpu.make_async_remote_copy(
            src_ref=src,
            dst_ref=dst,
            send_sem=sems.at[0 if rightward else 2, base + origin],
            recv_sem=sems.at[1, base + origin],
            device_id={"cols": right if rightward else left},
            device_id_type=pl.DeviceIdType.MESH,
        )

    def line_start(base, src, dst, origin, rightward):
        @pl.when(col < N - 1 if rightward else col > 0)
        def _():
            line_copy(base, src, dst, origin, rightward).start()

    def line_sent(base, src, dst, origin, rightward):
        @pl.when(col < N - 1 if rightward else col > 0)
        def _():
            line_copy(base, src, dst, origin, rightward).wait_send()

    def cell(index, origin):
        return cells_out.at[index, origin]

    def row_copy(slot, src, dst, to):
        return remote(src, dst, sems, slot, {"rows": to})

    for rightward in (True, False):
        line_start(0, own_cells, cell(row, col), col, rightward)
    small = Gather("rows", meta, meta_out, sems, 8)
    small.start()
    row_copy(16 + col, own_cells, cell(row, col), across).start()
    row_copy(20 + col, own_cells, cell(row, col), sibling).start()
    keep_cells = pltpu.make_async_copy(own_cells, cell(row, col), local.at[2])
    keep_cells.start()
    load_probe.wait()
    own_probe[...] = raw_probe[...].astype(bf16)
    for rightward in (True, False):
        line_start(4, own_probe, probe_out.at[col], col, rightward)
    keep_probe = pltpu.make_async_copy(own_probe, probe_out.at[col], local.at[3])
    keep_probe.start()
    load_frames.wait()
    own_frames[...] = raw_frames[...].astype(bf16)
    keep_frames = pltpu.make_async_copy(own_frames, frames_out.at[row], local.at[4])

    @pl.when(row == col)
    def _():
        keep_frames.start()

    def frame_copy(k):
        return row_copy(12 + k, own_frames, frames_out.at[row], lax.rem(row + k, N))

    for k in range(1, N):

        @pl.when(lax.rem(row + k, N) == col)
        def _():
            frame_copy(k).start()

    def from_side(d, rightward):
        if rightward:
            return col >= d, lax.rem(col + N - d, N)
        return col + d < N, lax.rem(col + d, N)

    for d in range(1, N):
        for rightward in (True, False):
            here, origin = from_side(d, rightward)

            @pl.when(here)
            def _():
                mine = cell(row, origin)
                line_copy(0, mine, mine, origin, rightward).wait_recv()
                line_start(0, mine, mine, origin, rightward)
                row_copy(16 + origin, mine, mine, across).start()
                row_copy(20 + origin, mine, mine, sibling).start()

        for rightward in (True, False):
            here, origin = from_side(d, rightward)

            @pl.when(here)
            def _():
                mine = probe_out.at[origin]
                line_copy(4, mine, mine, origin, rightward).wait_recv()
                line_start(4, mine, mine, origin, rightward)

        if d == 1:
            landed = cell(across, col)
            row_copy(16 + col, landed, landed, across).wait_recv()
            row_copy(24 + col, landed, landed, sibling).start()
    for k in range(1, N):
        origin = lax.rem(col + k, N)
        landed = cell(across, origin)
        row_copy(16 + origin, landed, landed, across).wait_recv()
        row_copy(24 + origin, landed, landed, sibling).start()
    for origin in range(N):
        near, far = cell(sibling, origin), cell(opposite, origin)
        row_copy(20 + origin, near, near, sibling).wait_recv()
        row_copy(24 + origin, far, far, sibling).wait_recv()
    keep_cells.wait()
    keep_probe.wait()
    for rightward in (True, False):
        line_sent(0, own_cells, cell(row, col), col, rightward)
        line_sent(4, own_probe, probe_out.at[col], col, rightward)
        for d in range(1, N):
            here, origin = from_side(d, rightward)

            @pl.when(here)
            def _():
                line_sent(0, cell(row, origin), cell(row, origin), origin, rightward)
                line_sent(4, probe_out.at[origin], probe_out.at[origin], origin, rightward)

    for origin in range(N):
        mine, landed = cell(row, origin), cell(across, origin)
        row_copy(16 + origin, mine, mine, across).wait_send()
        row_copy(20 + origin, mine, mine, sibling).wait_send()
        row_copy(24 + origin, landed, landed, sibling).wait_send()
    small.wait()

    @pl.when(row == col)
    def _():
        keep_frames.wait()
        for k in range(1, N):
            source = lax.rem(row + N - k, N)
            row_copy(12 + k, own_frames, frames_out.at[source], source).wait_recv()

    for k in range(1, N):

        @pl.when(lax.rem(row + k, N) == col)
        def _():
            frame_copy(k).wait_send()


def propagate(
    patch, probe, frames, table, table_t, probe_out, terms, field, power, parts, scale, measured, wide, tall, total, sems
):
    row, col = lax.axis_index("rows"), lax.axis_index("cols")
    length = patch.shape[-1]
    quarter = length // N
    f32, bf16 = jnp.float32, jnp.bfloat16
    greet(("rows", "cols"))

    def frame_copy(to):
        return remote(frames.at[to], measured, sems, 18 + lax.rem(to + N - row, N), {"cols": to})

    local_frames = pltpu.make_async_copy(frames.at[col], measured, sems.at[0, 18])

    @pl.when(row == col)
    def _():
        local_frames.start()
        for k in range(1, N):
            frame_copy(lax.rem(col + k, N)).start()

    def power_copy(p, k):
        to = lax.rem(row + k, N)
        return remote(power.at[p, to], parts.at[p, k - 1], sems, p * 3 + k - 1, {"rows": to})

    def scale_copy(p, k, index):
        to = lax.rem(row + k, N)
        return remote(scale.at[p, index], scale.at[p, index], sems, 9 + p * 3 + k - 1, {"rows": to})

    def factors(p):
        for k in range(1, N):
            power_copy(p, k).wait_recv()
        intensity = power[p, row].astype(f32)
        for k in range(1, N):
            intensity += parts[p, k - 1].astype(f32)
        amplitude = measured[p].astype(f32).T
        scale[p, row] = (1.0 - amplitude * lax.rsqrt(jnp.maximum(intensity, 0.25))).astype(bf16)
        for k in range(1, N):
            scale_copy(p, k, row).start()

    def transform(p, carry):
        probe_real = probe[:, 0].reshape(length, length).astype(f32)
        probe_imag = probe[:, 1].reshape(length, length).astype(f32)
        patch_real = patch[p, 0].astype(f32)
        patch_imag = patch[p, 1].astype(f32)
        wide[:, :length] = (probe_real * patch_real - probe_imag * patch_imag).astype(bf16)
        wide[:, length:] = (probe_real * patch_imag + probe_imag * patch_real).astype(bf16)
        spread = mul(wide[...], table[...])
        tall[:length] = spread[:, :length].astype(bf16)
        tall[length:] = spread[:, length:].astype(bf16)
        result = mul(table_t[...], tall[...])
        field[p] = result
        square = result[:length] * result[:length] + result[length:] * result[length:]
        for q in range(N):
            power[p, q] = square[:, q * quarter : (q + 1) * quarter].astype(bf16)
        for k in range(1, N):
            power_copy(p, k).start()

        @pl.when(p == 1)
        def _():
            @pl.when(row == col)
            def _():
                local_frames.wait()

            for k in range(1, N):

                @pl.when(lax.rem(row + k, N) == col)
                def _():
                    remote(measured, measured, sems, 18 + k, {"cols": row}).wait_recv()

        @pl.when(p >= 1)
        def _():
            factors(p - 1)

        return carry

    lax.fori_loop(0, POS_AVG, transform, 0)
    total[...] = jnp.zeros(total.shape, f32)

    def back_transform(p, carry):
        for k in range(1, N):
            scale_copy(p, k, lax.rem(row + N - k, N)).wait_recv()
        for q in range(N):
            lanes = pl.ds(q * quarter, quarter)
            gain = scale[p, q].astype(f32)
            tall[:length, lanes] = (field[p, :length, lanes] * gain).astype(bf16)
            tall[length:, lanes] = (field[p, length:, lanes] * gain).astype(bf16)
        inner = mul(table[...], tall[...])
        wide[:, :length] = inner[:length].astype(bf16)
        wide[:, length:] = inner[length:].astype(bf16)
        back = mul(wide[...], table_t[...])
        back_real, back_imag = back[:, :length], back[:, length:]
        probe_real = probe[:, 0].reshape(length, length).astype(f32)
        probe_imag = probe[:, 1].reshape(length, length).astype(f32)
        terms[p, 0] = probe_real * back_real + probe_imag * back_imag
        terms[p, 1] = probe_real * back_imag - probe_imag * back_real
        patch_real = patch[p, 0].astype(f32)
        patch_imag = patch[p, 1].astype(f32)
        total[0] += patch_real * back_real + patch_imag * back_imag
        total[1] += patch_real * back_imag - patch_imag * back_real

        @pl.when(p == 0)
        def _():
            factors(POS_AVG - 1)

        return carry

    lax.fori_loop(0, POS_AVG, back_transform, 0)
    for b in range(N):
        for part in range(2):
            probe_out[b, part] = total[part, b * quarter : (b + 1) * quarter].astype(bf16)

    def finish(p, carry):
        for k in range(1, N):
            power_copy(p, k).wait_send()
            scale_copy(p, k, row).wait_send()
        return carry

    lax.fori_loop(0, POS_AVG, finish, 0)

    @pl.when(row == col)
    def _():
        for k in range(1, N):
            frame_copy(lax.rem(col + k, N)).wait_send()


def scatter_gradients(probe_grad, cells_grad, probe_out, cells_out, sems):
    greet(("rows", "cols"))
    jobs = [
        Gather("cols", probe_grad, probe_out, sems, 0, scatter=True),
        Gather("rows", cells_grad, cells_out, sems, 4, scatter=True),
    ]
    for job in jobs:
        job.start()
    for job in jobs:
        job.wait()


def finish_gradients(cells_grad, probe_grad, cells_out, probe_out, sems):
    greet(("rows", "cols"))
    jobs = [
        Gather("cols", cells_grad, cells_out, sems, 0, scatter=True),
        Gather("rows", probe_grad, probe_out, sems, 4),
    ]
    for job in jobs:
        job.start()
    for job in jobs:
        job.wait()


def communicate(kernel, number, slots, outs, *args):
    return pl.pallas_call(
        kernel,
        out_shape=[jax.ShapeDtypeStruct(shape, dtype) for shape, dtype in outs],
        in_specs=[ANY] * len(args),
        out_specs=[ANY] * len(outs),
        scratch_shapes=[pltpu.SemaphoreType.DMA((2, slots))],
        compiler_params=pltpu.CompilerParams(collective_id=number, has_side_effects=True),
        name=kernel.__name__,
    )(*args)


def mul(left, right):
    return jnp.dot(left, right, preferred_element_type=jnp.float32)


def locate(meta, position, depth):
    strip, slot, start = 0, 0, 0
    for s in range(N):
        count = meta[s, 0, 0]
        inside = (position >= start) & (position < start + count)
        strip = jnp.where(inside, s, strip)
        slot = jnp.where(inside, position - start, slot)
        start = start + count
    return strip, slot, strip * depth + meta[strip, 0, 1 + slot], meta[strip, 0, 1 + POS_MAX + slot]


def iota(shape, axis):
    return lax.broadcasted_iota(jnp.int32, shape, axis)


def cut(meta, cells, frames_all, patch_out, frames_out, window, sems):
    p = pl.program_id(0)
    strips, blocks, _, width, depth = cells.shape
    length = patch_out.shape[-1]
    all_rows, all_cols = strips * depth, blocks * width

    def frame_copies():
        copies = []
        for i in range(POS_AVG * N):
            strip, slot, _, _ = locate(meta, i, depth)
            copies.append(
                pltpu.make_async_copy(
                    frames_all.at[strip, slot], frames_out.at[i // POS_AVG, i % POS_AVG], sems.at[i]
                )
            )
        return copies

    @pl.when(p == 0)
    def _():
        for copy in frame_copies():
            copy.start()
        for part, fill in ((0, 1.0), (1, 0.0)):
            window[part, all_cols:, :] = jnp.full((width, window.shape[2]), fill, jnp.float32)
            window[part, :all_cols, all_rows:] = jnp.full((all_cols, length), fill, jnp.float32)
            for s in range(strips):
                for b in range(blocks):
                    window[part, pl.ds(b * width, width), pl.ds(s * depth, depth)] = cells[s, b, part].astype(
                        jnp.float32
                    )

    _, _, first, column = locate(meta, lax.axis_index("cols") * POS_AVG + p, depth)
    rest = lax.rem(first, 128)
    base = first - rest
    low = lax.rem(column, 8)
    top = pl.multiple_of(column - low, 8)
    groups = length // 8
    for part in range(2):
        before = None
        for j in range(length // 128 + 1):
            block = window[part, pl.ds(top, length + 8), pl.ds(pl.multiple_of(base + 128 * j, 128), 128)]
            block = pltpu.roll(block.reshape(groups + 1, 8, 128), lax.rem(8 - low, 8), 1)
            block = jnp.where(iota((groups, 8, 128), 1) < 8 - low, block[:groups], block[1:])
            block = pltpu.roll(block.reshape(length, 128), lax.rem(128 - rest, 128), 1)
            if j > 0:
                joined = jnp.where(iota((length, 128), 1) < 128 - rest, before, block)
                patch_out[0, part, :, 128 * (j - 1) : 128 * j] = joined.astype(jnp.bfloat16)
            before = block

    @pl.when(p == pl.num_programs(0) - 1)
    def _():
        for copy in frame_copies():
            copy.wait()


def place(meta, terms, cells_out, window):
    p = pl.program_id(0)
    strips, blocks, _, width, depth = cells_out.shape
    length = terms.shape[-1]

    @pl.when(p == 0)
    def _():
        window[...] = jnp.zeros(window.shape, jnp.float32)

    _, _, first, column = locate(meta, lax.axis_index("cols") * POS_AVG + p, depth)
    rest = lax.rem(first, 128)
    base = first - rest
    low = lax.rem(column, 8)
    top = pl.multiple_of(column - low, 8)
    groups = length // 8
    edge = jnp.zeros((1, 8, 128), jnp.float32)
    for part in range(2):
        before = jnp.zeros((length + 8, 128), jnp.float32)
        for j in range(length // 128 + 1):
            if j < length // 128:
                block = terms[0, part, :, 128 * j : 128 * (j + 1)].reshape(groups, 8, 128)
                block = pltpu.roll(block, low, 1)
                above = jnp.concatenate([edge, block], axis=0)
                below = jnp.concatenate([block, edge], axis=0)
                block = jnp.where(iota((groups + 1, 8, 128), 1) < low, above, below)
                block = pltpu.roll(block.reshape(length + 8, 128), rest, 1)
            else:
                block = jnp.zeros((length + 8, 128), jnp.float32)
            joined = jnp.where(iota((length + 8, 128), 1) < rest, before, block)
            window[part, pl.ds(top, length + 8), pl.ds(pl.multiple_of(base + 128 * j, 128), 128)] += joined
            before = block

    @pl.when(p == pl.num_programs(0) - 1)
    def _():
        for part in range(2):
            for b in range(blocks):
                for s in range(strips):
                    cells_out[s, b, part] = window[part, pl.ds(b * width, width), pl.ds(s * depth, depth)].astype(
                        jnp.bfloat16
                    )


def balanced_device(object_field, probe, amplitudes, strip_counts, row_offsets, col_offsets):
    f32, bf16 = jnp.float32, jnp.bfloat16
    width, depth = object_field.shape[1:]
    length = probe.shape[3]
    row, col = lax.axis_index("rows"), lax.axis_index("cols")
    table, table_t = tables(length)
    meta = jnp.concatenate([strip_counts, row_offsets, col_offsets])
    meta = jnp.pad(meta, (0, 128 - meta.shape[0]))[None, :]
    mode_shape = probe.shape[1:]
    meta_all, mode_all, cells, frames_all = pl.pallas_call(
        spread_inputs,
        in_specs=[ANY, WHOLE, ANY, ANY],
        out_specs=[ANY] * 4,
        out_shape=[
            jax.ShapeDtypeStruct((N, 1, 128), jnp.int32),
            jax.ShapeDtypeStruct((N,) + mode_shape, bf16),
            jax.ShapeDtypeStruct((N, N) + object_field.shape, bf16),
            jax.ShapeDtypeStruct((N,) + amplitudes.shape, bf16),
        ],
        scratch_shapes=[
            pltpu.VMEM(mode_shape, f32),
            pltpu.VMEM(amplitudes.shape, f32),
            pltpu.VMEM(object_field.shape, bf16),
            pltpu.VMEM(mode_shape, bf16),
            pltpu.VMEM(amplitudes.shape, bf16),
            pltpu.SemaphoreType.DMA((3, 28)),
            pltpu.SemaphoreType.DMA((5,)),
        ],
        compiler_params=pltpu.CompilerParams(collective_id=1, has_side_effects=True, vmem_limit_bytes=LIMIT),
        name="spread_inputs",
    )(meta, object_field, probe, amplitudes)

    plane = (1, 2, length, length)
    whole = lambda *shape: pl.BlockSpec(shape, lambda p: (0,) * len(shape))
    per_slot = pl.BlockSpec(plane, lambda p: (p, 0, 0, 0))
    scalars = pl.BlockSpec(memory_space=pltpu.SMEM)
    window = pltpu.VMEM((2, N * width + 128, N * depth + length), f32)
    quarters = (POS_AVG, N, length, length // N)
    patch, frames = pl.pallas_call(
        cut,
        grid=(POS_AVG,),
        in_specs=[scalars, whole(*cells.shape), ANY],
        out_specs=[per_slot, ANY],
        scratch_shapes=[window, pltpu.SemaphoreType.DMA((POS_AVG * N,))],
        out_shape=[
            jax.ShapeDtypeStruct((POS_AVG,) + plane[1:], bf16),
            jax.ShapeDtypeStruct((N, POS_AVG) + amplitudes.shape[1:], bf16),
        ],
        compiler_params=pltpu.CompilerParams(vmem_limit_bytes=LIMIT),
        name="cut",
    )(meta_all, cells, frames_all)
    probe_part, terms = pl.pallas_call(
        propagate,
        in_specs=[WHOLE, WHOLE, ANY, WHOLE, WHOLE],
        out_specs=[WHOLE, WHOLE],
        out_shape=[
            jax.ShapeDtypeStruct(mode_all.shape, bf16),
            jax.ShapeDtypeStruct((POS_AVG,) + plane[1:], f32),
        ],
        scratch_shapes=[
            pltpu.VMEM((POS_AVG, 2 * length, length), f32),
            pltpu.VMEM(quarters, bf16),
            pltpu.VMEM((POS_AVG, N - 1) + quarters[2:], bf16),
            pltpu.VMEM(quarters, bf16),
            pltpu.VMEM(frames.shape[1:], bf16),
            pltpu.VMEM((length, 2 * length), bf16),
            pltpu.VMEM((2 * length, length), bf16),
            pltpu.VMEM((2, length, length), f32),
            pltpu.SemaphoreType.DMA((2, 22)),
        ],
        compiler_params=pltpu.CompilerParams(collective_id=2, has_side_effects=True, vmem_limit_bytes=LIMIT),
        name="propagate",
    )(patch, mode_all, frames, table, table_t)
    cells_part = pl.pallas_call(
        place,
        grid=(POS_AVG,),
        in_specs=[scalars, per_slot],
        out_specs=whole(*cells.shape),
        scratch_shapes=[window],
        out_shape=jax.ShapeDtypeStruct(cells.shape, bf16),
        compiler_params=pltpu.CompilerParams(vmem_limit_bytes=LIMIT),
        name="place",
    )(meta_all, terms)
    probe_parts, cells_parts = communicate(
        scatter_gradients, 4, 8, [(probe_part.shape, bf16), (cells_part.shape, bf16)], probe_part, cells_part
    )
    probe_sum = jnp.sum(probe_parts.astype(f32), axis=0).astype(bf16)
    cells_sum = jnp.sum(cells_parts.astype(f32), axis=0).astype(bf16)
    cells_last, probe_last = communicate(
        finish_gradients, 5, 8, [(cells_sum.shape, bf16), ((N,) + probe_sum.shape, bf16)], cells_sum, probe_sum
    )
    return jnp.sum(cells_last.astype(f32), axis=0), probe_last.astype(f32)


def solution(mesh):
    on_device = balanced_device if mesh.shape["rows"] == N and mesh.shape["cols"] == N else general_device
    placed = (
        P("groups", "cols", "rows"),
        P("groups", None, "cols", None),
        P(("groups", "rows"), "cols", None),
        P(("groups", "rows")),
        P(("groups", "rows")),
        P(("groups", "rows")),
    )
    return jax.shard_map(
        on_device,
        mesh=mesh,
        in_specs=placed,
        out_specs=(P("groups", "cols", "rows"), P("groups", None, "cols", None)),
        check_vma=False,
    )
```

```python
import jax
import jax.numpy as jnp
import numpy as np
from jax import lax
from jax.experimental import pallas as pl
from jax.experimental.pallas import tpu as pltpu
from jax.sharding import PartitionSpec as P

POS_AVG = 3
POS_MAX = 6


def shifted(block, axis, distance):
    devices = range(lax.axis_size(axis))
    route = [(i - distance, i) for i in devices if i - distance in devices]
    return lax.ppermute(block, axis, route)


def dft_tables(length):
    indices = jnp.arange(length, dtype=jnp.int32)
    product = indices[:, None] * indices[None, :] % length
    angles = product.astype(jnp.float32) * jnp.float32(2.0 * 3.141592653589793 / length)
    scaling = jnp.float32(1.0 / length**0.5)
    cosine_table = (jnp.cos(angles) * scaling).astype(jnp.bfloat16)
    sine_table = (jnp.sin(angles) * scaling).astype(jnp.bfloat16)
    return (cosine_table, sine_table)


def leading(values, matrix):
    return jnp.einsum("mca,asu->mscu", values, matrix, preferred_element_type=jnp.float32)


def second(values, matrix):
    return jnp.einsum("mscu,scv->muv", values, matrix, preferred_element_type=jnp.float32)


def third(values, matrix):
    return jnp.einsum("muv,vsb->msub", values, matrix, preferred_element_type=jnp.float32)


def fourth(values, matrix):
    return jnp.einsum("msub,sua->mba", values, matrix, preferred_element_type=jnp.float32)


def vacuum_where(block, outside):
    fill_real = jnp.where(outside, jnp.float32(1.0), block[0])
    fill_imag = jnp.where(outside, jnp.float32(0.0), block[1])
    return jnp.stack([fill_real, fill_imag])


def spectral_pass(patch_cells, probe, measured, cosine_table, sine_table, block_count):
    mode_count = probe.shape[0]
    block_cols = patch_cells.shape[1]
    length = patch_cells.shape[2]
    block_freq = length // block_count
    probe_real = probe[:, 0]
    probe_imag = probe[:, 1]
    patch_real = patch_cells[0]
    patch_imag = patch_cells[1]
    wave_real = (probe_real * patch_real - probe_imag * patch_imag).astype(jnp.bfloat16)
    wave_imag = (probe_real * patch_imag + probe_imag * patch_real).astype(jnp.bfloat16)
    cos_lead = cosine_table.reshape(length, block_count, block_freq)
    sin_lead = sine_table.reshape(length, block_count, block_freq)
    first_real = leading(wave_real, cos_lead) + leading(wave_imag, sin_lead)
    first_imag = leading(wave_imag, cos_lead) - leading(wave_real, sin_lead)
    outgoing = jnp.stack([first_real, first_imag], axis=1).astype(jnp.bfloat16)
    outgoing = outgoing.reshape(mode_count, 2, block_count, block_cols * block_freq)
    arrived = lax.all_to_all(outgoing, "cols", split_axis=2, concat_axis=2, tiled=True)
    arrived = arrived.reshape(mode_count, 2, block_count, block_cols, block_freq)
    cos_rows = cosine_table.reshape(block_count, block_cols, length)
    sin_rows = sine_table.reshape(block_count, block_cols, length)
    field_real = second(arrived[:, 0], cos_rows) + second(arrived[:, 1], sin_rows)
    field_imag = second(arrived[:, 1], cos_rows) - second(arrived[:, 0], sin_rows)
    intensity = jnp.sum(field_real * field_real + field_imag * field_imag, axis=0)
    modulus = jnp.sqrt(jnp.maximum(intensity, 0.25))
    factor = 1.0 - measured / modulus
    back_real = (field_real * factor).astype(jnp.bfloat16)
    back_imag = (field_imag * factor).astype(jnp.bfloat16)
    cos_back = cosine_table.reshape(length, block_count, block_cols)
    sin_back = sine_table.reshape(length, block_count, block_cols)
    inner_real = third(back_real, cos_back) - third(back_imag, sin_back)
    inner_imag = third(back_imag, cos_back) + third(back_real, sin_back)
    returning = jnp.stack([inner_real, inner_imag], axis=1).astype(jnp.bfloat16)
    returning = returning.reshape(mode_count, 2, block_count, block_freq * block_cols)
    landed = lax.all_to_all(returning, "cols", split_axis=2, concat_axis=2, tiled=True)
    landed = landed.reshape(mode_count, 2, block_count, block_freq, block_cols)
    cos_freq = cosine_table.reshape(block_count, block_freq, length)
    sin_freq = sine_table.reshape(block_count, block_freq, length)
    grad_real = fourth(landed[:, 0], cos_freq) - fourth(landed[:, 1], sin_freq)
    grad_imag = fourth(landed[:, 1], cos_freq) + fourth(landed[:, 0], sin_freq)
    object_real = jnp.sum(probe_real * grad_real + probe_imag * grad_imag, axis=0)
    object_imag = jnp.sum(probe_real * grad_imag - probe_imag * grad_real, axis=0)
    probe_real_term = patch_real * grad_real + patch_imag * grad_imag
    probe_imag_term = patch_real * grad_imag - patch_imag * grad_real
    return (
        jnp.stack([object_real, object_imag]),
        jnp.stack([probe_real_term, probe_imag_term], axis=1),
    )


def run_positions(
    window,
    probe,
    frames,
    first_rows,
    first_cols,
    slot_total,
    used_count,
    cosine_table,
    sine_table,
    block_count,
):
    block_cols = probe.shape[2]
    length = probe.shape[3]

    def visit_slot(slot_index, state_pair):
        window_grad, probe_sum = state_pair
        first_row = first_rows[slot_index]
        first_col = first_cols[slot_index]
        patch_cells = lax.dynamic_slice(window, (0, first_col, first_row), (2, block_cols, length))
        measured = lax.dynamic_index_in_dim(frames, slot_index, 0, keepdims=False)
        object_term, probe_term = spectral_pass(
            patch_cells, probe, measured, cosine_table, sine_table, block_count
        )
        active = (slot_index < used_count).astype(jnp.float32)
        current = lax.dynamic_slice(window_grad, (0, first_col, first_row), (2, block_cols, length))
        window_grad = lax.dynamic_update_slice(
            window_grad, current + active * object_term, (0, first_col, first_row)
        )
        return (window_grad, probe_sum + active * probe_term)

    initial = (jnp.zeros(window.shape, jnp.float32), jnp.zeros(probe.shape, jnp.float32))
    return lax.fori_loop(0, slot_total, visit_slot, initial)


def general_device(object_field, probe, amplitudes, strip_counts, row_offsets, col_offsets):
    block_cols = object_field.shape[1]
    strip_rows = object_field.shape[2]
    length = probe.shape[3]
    block_count = lax.axis_size("cols")
    strip_total = lax.axis_size("rows")
    cosine_table, sine_table = dft_tables(length)
    beside = shifted(object_field, "cols", -1)
    beside = vacuum_where(beside, lax.axis_index("cols") == block_count - 1)
    paired = jnp.concatenate([object_field, beside], axis=1)
    counts_all, rows_all, cols_all = (
        lax.all_gather(strip_counts, "rows", axis=0, tiled=True),
        lax.all_gather(row_offsets, "rows", axis=0, tiled=True),
        lax.all_gather(col_offsets, "rows", axis=0, tiled=True),
    )
    totals = jnp.cumsum(counts_all)
    starts = totals - counts_all
    position_block = (lax.axis_index("rows") + strip_total // 2) % strip_total
    my_positions = position_block * POS_AVG + jnp.arange(POS_AVG, dtype=jnp.int32)
    strip_of = jnp.sum((totals[None, :] <= my_positions[:, None]).astype(jnp.int32), axis=1)
    wanted = strip_of * POS_MAX + my_positions - jnp.take(starts, strip_of)
    first_rows = strip_of * strip_rows + jnp.take(rows_all, wanted)
    first_cols = jnp.take(cols_all, wanted)
    empty_frames = jnp.zeros((POS_AVG,) + amplitudes.shape[1:], jnp.float32)
    received = lax.all_gather(amplitudes, "rows", axis=0, tiled=True)
    inside = (wanted >= 0) & (wanted < received.shape[0])
    picked = jnp.take(received, jnp.clip(wanted, 0, received.shape[0] - 1), axis=0)
    frames = jnp.where(inside[:, None, None], picked, empty_frames)
    column_all = lax.all_gather(paired, "rows", axis=2, tiled=True)
    all_rows = column_all.shape[2]
    vacuum_tail = vacuum_where(jnp.zeros((2, column_all.shape[1], length), jnp.float32), True)
    window = jnp.concatenate([column_all, vacuum_tail], axis=2)
    window_grad, probe_sum = run_positions(
        window,
        probe,
        frames,
        first_rows,
        first_cols,
        POS_AVG,
        POS_AVG,
        cosine_table,
        sine_table,
        block_count,
    )
    folded = window_grad[:, :, :all_rows]
    summed = lax.psum_scatter(folded, "rows", scatter_dimension=2, tiled=True)
    upper_half = shifted(summed[:, block_cols:], "cols", 1)
    object_grad = summed[:, :block_cols] + upper_half
    probe_grad = lax.psum(probe_sum, "rows")
    return (object_grad, probe_grad)


def tables(length):
    indices = np.arange(length)
    angles = (indices[:, None] * indices[None, :] % length) * (2.0 * np.pi / length)
    scaling = 1.0 / length**0.5
    cosine, sine = np.cos(angles) * scaling, np.sin(angles) * scaling
    table = np.block([[cosine, -sine], [sine, cosine]])
    return jnp.asarray(table, jnp.bfloat16), jnp.asarray(table.T, jnp.bfloat16)


ANY = pl.BlockSpec(memory_space=pl.ANY)
WHOLE = pl.BlockSpec(memory_space=pltpu.VMEM)
LIMIT = 56 * 1024 * 1024
N = 4


def greet(axes):
    barrier = pltpu.get_barrier_semaphore()
    for axis in axes:
        me = lax.axis_index(axis)
        for k in range(1, N):
            pl.semaphore_signal(
                barrier, inc=1, device_id={axis: lax.rem(me + k, N)}, device_id_type=pl.DeviceIdType.MESH
            )
    pl.semaphore_wait(barrier, (N - 1) * len(axes))


def remote(src, dst, sems, slot, device):
    return pltpu.make_async_remote_copy(
        src_ref=src,
        dst_ref=dst,
        send_sem=sems.at[0, slot],
        recv_sem=sems.at[1, slot],
        device_id=device,
        device_id_type=pl.DeviceIdType.MESH,
    )


class Gather:
    def __init__(self, axis, src, out, sems, base, scatter=False):
        self.me = lax.axis_index(axis)
        self.axis, self.src, self.out, self.sems, self.base, self.scatter = axis, src, out, sems, base, scatter

    def piece(self, index):
        return self.src.at[index] if self.scatter else self.src

    def start(self):
        self.local = pltpu.make_async_copy(
            self.piece(self.me), self.out.at[self.me], self.sems.at[0, self.base]
        )
        self.sent = []
        for k in range(1, N):
            to = lax.rem(self.me + k, N)
            copy = remote(self.piece(to), self.out.at[self.me], self.sems, self.base + k, {self.axis: to})
            copy.start()
            self.sent.append(copy)
        self.local.start()

    def wait(self):
        self.local.wait()
        for k in range(1, N):
            source = lax.rem(self.me + N - k, N)
            remote(
                self.piece(source), self.out.at[source], self.sems, self.base + k, {self.axis: source}
            ).wait_recv()
        for copy in self.sent:
            copy.wait_send()


def spread_inputs(
    meta, cells, probe, frames, meta_out, probe_out, cells_out, frames_out,
    raw_probe, raw_frames, own_cells, own_probe, own_frames, sems, local
):
    bf16 = jnp.bfloat16
    row, col = lax.axis_index("rows"), lax.axis_index("cols")
    sibling = row + 1 - 2 * lax.rem(row, 2)
    across = lax.rem(row + 2, N)
    opposite = lax.rem(sibling + 2, N)
    right, left = lax.rem(col + 1, N), lax.rem(col + N - 1, N)
    load_probe = pltpu.make_async_copy(probe.at[row], raw_probe, local.at[0])
    load_frames = pltpu.make_async_copy(frames, raw_frames, local.at[1])
    load_probe.start()
    load_frames.start()
    own_cells[...] = cells[...].astype(bf16)
    greet(("rows", "cols"))

    def line_copy(base, src, dst, origin, rightward):
        return pltpu.make_async_remote_copy(
            src_ref=src,
            dst_ref=dst,
            send_sem=sems.at[0 if rightward else 2, base + origin],
            recv_sem=sems.at[1, base + origin],
            device_id={"cols": right if rightward else left},
            device_id_type=pl.DeviceIdType.MESH,
        )

    def line_start(base, src, dst, origin, rightward):
        @pl.when(col < N - 1 if rightward else col > 0)
        def _():
            line_copy(base, src, dst, origin, rightward).start()

    def line_sent(base, src, dst, origin, rightward):
        @pl.when(col < N - 1 if rightward else col > 0)
        def _():
            line_copy(base, src, dst, origin, rightward).wait_send()

    def cell(index, origin):
        return cells_out.at[index, origin]

    def row_copy(slot, src, dst, to):
        return remote(src, dst, sems, slot, {"rows": to})

    for rightward in (True, False):
        line_start(0, own_cells, cell(row, col), col, rightward)
    small = Gather("rows", meta, meta_out, sems, 8)
    small.start()
    row_copy(16 + col, own_cells, cell(row, col), across).start()
    row_copy(20 + col, own_cells, cell(row, col), sibling).start()
    keep_cells = pltpu.make_async_copy(own_cells, cell(row, col), local.at[2])
    keep_cells.start()
    load_probe.wait()
    own_probe[...] = raw_probe[...].astype(bf16)
    for rightward in (True, False):
        line_start(4, own_probe, probe_out.at[col], col, rightward)
    keep_probe = pltpu.make_async_copy(own_probe, probe_out.at[col], local.at[3])
    keep_probe.start()
    load_frames.wait()
    own_frames[...] = raw_frames[...].astype(bf16)
    keep_frames = pltpu.make_async_copy(own_frames, frames_out.at[row], local.at[4])

    @pl.when(row == col)
    def _():
        keep_frames.start()

    def frame_copy(k):
        return row_copy(12 + k, own_frames, frames_out.at[row], lax.rem(row + k, N))

    for k in range(1, N):

        @pl.when(lax.rem(row + k, N) == col)
        def _():
            frame_copy(k).start()

    def from_side(d, rightward):
        if rightward:
            return col >= d, lax.rem(col + N - d, N)
        return col + d < N, lax.rem(col + d, N)

    for d in range(1, N):
        for rightward in (True, False):
            here, origin = from_side(d, rightward)

            @pl.when(here)
            def _():
                mine = cell(row, origin)
                line_copy(0, mine, mine, origin, rightward).wait_recv()
                line_start(0, mine, mine, origin, rightward)
                row_copy(16 + origin, mine, mine, across).start()
                row_copy(20 + origin, mine, mine, sibling).start()

        for rightward in (True, False):
            here, origin = from_side(d, rightward)

            @pl.when(here)
            def _():
                mine = probe_out.at[origin]
                line_copy(4, mine, mine, origin, rightward).wait_recv()
                line_start(4, mine, mine, origin, rightward)

        if d == 1:
            landed = cell(across, col)
            row_copy(16 + col, landed, landed, across).wait_recv()
            row_copy(24 + col, landed, landed, sibling).start()
    for k in range(1, N):
        origin = lax.rem(col + k, N)
        landed = cell(across, origin)
        row_copy(16 + origin, landed, landed, across).wait_recv()
        row_copy(24 + origin, landed, landed, sibling).start()
    for origin in range(N):
        near, far = cell(sibling, origin), cell(opposite, origin)
        row_copy(20 + origin, near, near, sibling).wait_recv()
        row_copy(24 + origin, far, far, sibling).wait_recv()
    keep_cells.wait()
    keep_probe.wait()
    for rightward in (True, False):
        line_sent(0, own_cells, cell(row, col), col, rightward)
        line_sent(4, own_probe, probe_out.at[col], col, rightward)
        for d in range(1, N):
            here, origin = from_side(d, rightward)

            @pl.when(here)
            def _():
                line_sent(0, cell(row, origin), cell(row, origin), origin, rightward)
                line_sent(4, probe_out.at[origin], probe_out.at[origin], origin, rightward)

    for origin in range(N):
        mine, landed = cell(row, origin), cell(across, origin)
        row_copy(16 + origin, mine, mine, across).wait_send()
        row_copy(20 + origin, mine, mine, sibling).wait_send()
        row_copy(24 + origin, landed, landed, sibling).wait_send()
    small.wait()

    @pl.when(row == col)
    def _():
        keep_frames.wait()
        for k in range(1, N):
            source = lax.rem(row + N - k, N)
            row_copy(12 + k, own_frames, frames_out.at[source], source).wait_recv()

    for k in range(1, N):

        @pl.when(lax.rem(row + k, N) == col)
        def _():
            frame_copy(k).wait_send()


def propagate(
    patch, probe, frames, table, table_t, probe_out, terms, field, power, parts, scale, measured, wide, tall, total, sems
):
    row, col = lax.axis_index("rows"), lax.axis_index("cols")
    length = patch.shape[-1]
    quarter = length // N
    f32, bf16 = jnp.float32, jnp.bfloat16
    greet(("rows", "cols"))

    def frame_copy(to):
        return remote(frames.at[to], measured, sems, 18 + lax.rem(to + N - row, N), {"cols": to})

    local_frames = pltpu.make_async_copy(frames.at[col], measured, sems.at[0, 18])

    @pl.when(row == col)
    def _():
        local_frames.start()
        for k in range(1, N):
            frame_copy(lax.rem(col + k, N)).start()

    def power_copy(p, k):
        to = lax.rem(row + k, N)
        return remote(power.at[p, to], parts.at[p, k - 1], sems, p * 3 + k - 1, {"rows": to})

    def scale_copy(p, k, index):
        to = lax.rem(row + k, N)
        return remote(scale.at[p, index], scale.at[p, index], sems, 9 + p * 3 + k - 1, {"rows": to})

    def factors(p):
        for k in range(1, N):
            power_copy(p, k).wait_recv()
        intensity = power[p, row].astype(f32)
        for k in range(1, N):
            intensity += parts[p, k - 1].astype(f32)
        amplitude = measured[p].astype(f32).T
        scale[p, row] = (1.0 - amplitude * lax.rsqrt(jnp.maximum(intensity, 0.25))).astype(bf16)
        for k in range(1, N):
            scale_copy(p, k, row).start()

    def transform(p, carry):
        probe_real = probe[:, 0].reshape(length, length).astype(f32)
        probe_imag = probe[:, 1].reshape(length, length).astype(f32)
        patch_real = patch[p, 0].astype(f32)
        patch_imag = patch[p, 1].astype(f32)
        wide[:, :length] = (probe_real * patch_real - probe_imag * patch_imag).astype(bf16)
        wide[:, length:] = (probe_real * patch_imag + probe_imag * patch_real).astype(bf16)
        spread = mul(wide[...], table[...])
        tall[:length] = spread[:, :length].astype(bf16)
        tall[length:] = spread[:, length:].astype(bf16)
        result = mul(table_t[...], tall[...])
        field[p] = result
        square = result[:length] * result[:length] + result[length:] * result[length:]
        for q in range(N):
            power[p, q] = square[:, q * quarter : (q + 1) * quarter].astype(bf16)
        for k in range(1, N):
            power_copy(p, k).start()

        @pl.when(p == 1)
        def _():
            @pl.when(row == col)
            def _():
                local_frames.wait()

            for k in range(1, N):

                @pl.when(lax.rem(row + k, N) == col)
                def _():
                    remote(measured, measured, sems, 18 + k, {"cols": row}).wait_recv()

        @pl.when(p >= 1)
        def _():
            factors(p - 1)

        return carry

    lax.fori_loop(0, POS_AVG, transform, 0)
    total[...] = jnp.zeros(total.shape, f32)

    def back_transform(p, carry):
        for k in range(1, N):
            scale_copy(p, k, lax.rem(row + N - k, N)).wait_recv()
        for q in range(N):
            lanes = pl.ds(q * quarter, quarter)
            gain = scale[p, q].astype(f32)
            tall[:length, lanes] = (field[p, :length, lanes] * gain).astype(bf16)
            tall[length:, lanes] = (field[p, length:, lanes] * gain).astype(bf16)
        inner = mul(table[...], tall[...])
        wide[:, :length] = inner[:length].astype(bf16)
        wide[:, length:] = inner[length:].astype(bf16)
        back = mul(wide[...], table_t[...])
        back_real, back_imag = back[:, :length], back[:, length:]
        probe_real = probe[:, 0].reshape(length, length).astype(f32)
        probe_imag = probe[:, 1].reshape(length, length).astype(f32)
        terms[p, 0] = probe_real * back_real + probe_imag * back_imag
        terms[p, 1] = probe_real * back_imag - probe_imag * back_real
        patch_real = patch[p, 0].astype(f32)
        patch_imag = patch[p, 1].astype(f32)
        total[0] += patch_real * back_real + patch_imag * back_imag
        total[1] += patch_real * back_imag - patch_imag * back_real

        @pl.when(p == 0)
        def _():
            factors(POS_AVG - 1)

        return carry

    lax.fori_loop(0, POS_AVG, back_transform, 0)
    for b in range(N):
        for part in range(2):
            probe_out[b, part] = total[part, b * quarter : (b + 1) * quarter].astype(bf16)

    def finish(p, carry):
        for k in range(1, N):
            power_copy(p, k).wait_send()
            scale_copy(p, k, row).wait_send()
        return carry

    lax.fori_loop(0, POS_AVG, finish, 0)

    @pl.when(row == col)
    def _():
        for k in range(1, N):
            frame_copy(lax.rem(col + k, N)).wait_send()


def reduce_gradients(
    probe_part, cells_part, cells_out, probe_out, probe_in, near, far, relay, outgoing, cells_in, probe_all, sems
):
    f32, bf16 = jnp.float32, jnp.bfloat16
    row, col = lax.axis_index("rows"), lax.axis_index("cols")
    sibling = row + 1 - 2 * lax.rem(row, 2)
    across = lax.rem(row + 2, N)
    opposite = lax.rem(sibling + 2, N)
    greet(("rows", "cols"))

    def probe_copy(k):
        to = lax.rem(col + k, N)
        return remote(probe_part.at[to], probe_in.at[k - 1], sems, k - 1, {"cols": to})

    def near_copy(half, k):
        b = lax.rem(col + k, N)
        strip = opposite if half else sibling
        return remote(cells_part.at[strip, b], near.at[half, b], sems, 3 + 4 * half + k, {"rows": sibling})

    def far_copy(k):
        b = lax.rem(col + k, N)
        return remote(relay.at[b], far.at[b], sems, 11 + k, {"rows": across})

    def cells_copy(k):
        b = lax.rem(col + k, N)
        return remote(outgoing.at[b], cells_in.at[k - 1], sems, 14 + k, {"cols": b})

    def mode_copy(slot, index, to):
        return remote(probe_all.at[index], probe_all.at[index], sems, slot, {"rows": to})

    order = (1, 2, 3, 0)
    for k in range(1, N):
        probe_copy(k).start()
    for half in (1, 0):
        for k in order:
            near_copy(half, k).start()
    for k in order:
        b = lax.rem(col + k, N)
        near_copy(1, k).wait_recv()
        relay[b] = (cells_part[across, b].astype(f32) + near[1, b].astype(f32)).astype(bf16)
        far_copy(k).start()
    for k in order:
        b = lax.rem(col + k, N)
        near_copy(0, k).wait_recv()
        far_copy(k).wait_recv()
        total = cells_part[row, b].astype(f32) + near[0, b].astype(f32) + far[b].astype(f32)
        if k == 0:
            cells_out[...] = total
        else:
            outgoing[b] = total.astype(bf16)
            cells_copy(k).start()
    total = probe_part[col].astype(f32)
    for k in range(1, N):
        probe_copy(k).wait_recv()
        total += probe_in[k - 1].astype(f32)
    probe_all[row] = total.astype(bf16)
    sent = [mode_copy(18, row, across), mode_copy(19, row, sibling)]
    for copy in sent:
        copy.start()
    mode_copy(18, across, across).wait_recv()
    forwarded = mode_copy(20, across, sibling)
    forwarded.start()
    sent.append(forwarded)
    for k in range(1, N):
        cells_copy(k).wait_recv()
        cells_out[...] += cells_in[k - 1].astype(f32)
    mode_copy(19, sibling, sibling).wait_recv()
    mode_copy(20, opposite, sibling).wait_recv()
    probe_out[...] = probe_all[...].astype(f32)
    for copy in sent:
        copy.wait_send()
    for k in range(N):
        near_copy(0, k).wait_send()
        near_copy(1, k).wait_send()
        far_copy(k).wait_send()
        if k > 0:
            probe_copy(k).wait_send()
            cells_copy(k).wait_send()


def mul(left, right):
    return jnp.dot(left, right, preferred_element_type=jnp.float32)


def locate(meta, position, depth):
    strip, slot, start = 0, 0, 0
    for s in range(N):
        count = meta[s, 0, 0]
        inside = (position >= start) & (position < start + count)
        strip = jnp.where(inside, s, strip)
        slot = jnp.where(inside, position - start, slot)
        start = start + count
    return strip, slot, strip * depth + meta[strip, 0, 1 + slot], meta[strip, 0, 1 + POS_MAX + slot]


def iota(shape, axis):
    return lax.broadcasted_iota(jnp.int32, shape, axis)


def cut(meta, cells, frames_all, patch_out, frames_out, window, sems):
    p = pl.program_id(0)
    strips, blocks, _, width, depth = cells.shape
    length = patch_out.shape[-1]
    all_rows, all_cols = strips * depth, blocks * width

    def frame_copies():
        copies = []
        for i in range(POS_AVG * N):
            strip, slot, _, _ = locate(meta, i, depth)
            copies.append(
                pltpu.make_async_copy(
                    frames_all.at[strip, slot], frames_out.at[i // POS_AVG, i % POS_AVG], sems.at[i]
                )
            )
        return copies

    @pl.when(p == 0)
    def _():
        for copy in frame_copies():
            copy.start()
        for part, fill in ((0, 1.0), (1, 0.0)):
            window[part, all_cols:, :] = jnp.full((width, window.shape[2]), fill, jnp.float32)
            window[part, :all_cols, all_rows:] = jnp.full((all_cols, length), fill, jnp.float32)
            for s in range(strips):
                for b in range(blocks):
                    window[part, pl.ds(b * width, width), pl.ds(s * depth, depth)] = cells[s, b, part].astype(
                        jnp.float32
                    )

    _, _, first, column = locate(meta, lax.axis_index("cols") * POS_AVG + p, depth)
    rest = lax.rem(first, 128)
    base = first - rest
    low = lax.rem(column, 8)
    top = pl.multiple_of(column - low, 8)
    groups = length // 8
    for part in range(2):
        before = None
        for j in range(length // 128 + 1):
            block = window[part, pl.ds(top, length + 8), pl.ds(pl.multiple_of(base + 128 * j, 128), 128)]
            block = pltpu.roll(block.reshape(groups + 1, 8, 128), lax.rem(8 - low, 8), 1)
            block = jnp.where(iota((groups, 8, 128), 1) < 8 - low, block[:groups], block[1:])
            block = pltpu.roll(block.reshape(length, 128), lax.rem(128 - rest, 128), 1)
            if j > 0:
                joined = jnp.where(iota((length, 128), 1) < 128 - rest, before, block)
                patch_out[0, part, :, 128 * (j - 1) : 128 * j] = joined.astype(jnp.bfloat16)
            before = block

    @pl.when(p == pl.num_programs(0) - 1)
    def _():
        for copy in frame_copies():
            copy.wait()


def place(meta, terms, cells_out, window):
    p = pl.program_id(0)
    strips, blocks, _, width, depth = cells_out.shape
    length = terms.shape[-1]

    @pl.when(p == 0)
    def _():
        window[...] = jnp.zeros(window.shape, jnp.float32)

    _, _, first, column = locate(meta, lax.axis_index("cols") * POS_AVG + p, depth)
    rest = lax.rem(first, 128)
    base = first - rest
    low = lax.rem(column, 8)
    top = pl.multiple_of(column - low, 8)
    groups = length // 8
    edge = jnp.zeros((1, 8, 128), jnp.float32)
    for part in range(2):
        before = jnp.zeros((length + 8, 128), jnp.float32)
        for j in range(length // 128 + 1):
            if j < length // 128:
                block = terms[0, part, :, 128 * j : 128 * (j + 1)].reshape(groups, 8, 128)
                block = pltpu.roll(block, low, 1)
                above = jnp.concatenate([edge, block], axis=0)
                below = jnp.concatenate([block, edge], axis=0)
                block = jnp.where(iota((groups + 1, 8, 128), 1) < low, above, below)
                block = pltpu.roll(block.reshape(length + 8, 128), rest, 1)
            else:
                block = jnp.zeros((length + 8, 128), jnp.float32)
            joined = jnp.where(iota((length + 8, 128), 1) < rest, before, block)
            window[part, pl.ds(top, length + 8), pl.ds(pl.multiple_of(base + 128 * j, 128), 128)] += joined
            before = block

    @pl.when(p == pl.num_programs(0) - 1)
    def _():
        for part in range(2):
            for b in range(blocks):
                for s in range(strips):
                    cells_out[s, b, part] = window[part, pl.ds(b * width, width), pl.ds(s * depth, depth)].astype(
                        jnp.bfloat16
                    )


def balanced_device(object_field, probe, amplitudes, strip_counts, row_offsets, col_offsets):
    f32, bf16 = jnp.float32, jnp.bfloat16
    width, depth = object_field.shape[1:]
    length = probe.shape[3]
    row, col = lax.axis_index("rows"), lax.axis_index("cols")
    table, table_t = tables(length)
    meta = jnp.concatenate([strip_counts, row_offsets, col_offsets])
    meta = jnp.pad(meta, (0, 128 - meta.shape[0]))[None, :]
    mode_shape = probe.shape[1:]
    meta_all, mode_all, cells, frames_all = pl.pallas_call(
        spread_inputs,
        in_specs=[ANY, WHOLE, ANY, ANY],
        out_specs=[ANY] * 4,
        out_shape=[
            jax.ShapeDtypeStruct((N, 1, 128), jnp.int32),
            jax.ShapeDtypeStruct((N,) + mode_shape, bf16),
            jax.ShapeDtypeStruct((N, N) + object_field.shape, bf16),
            jax.ShapeDtypeStruct((N,) + amplitudes.shape, bf16),
        ],
        scratch_shapes=[
            pltpu.VMEM(mode_shape, f32),
            pltpu.VMEM(amplitudes.shape, f32),
            pltpu.VMEM(object_field.shape, bf16),
            pltpu.VMEM(mode_shape, bf16),
            pltpu.VMEM(amplitudes.shape, bf16),
            pltpu.SemaphoreType.DMA((3, 28)),
            pltpu.SemaphoreType.DMA((5,)),
        ],
        compiler_params=pltpu.CompilerParams(collective_id=1, has_side_effects=True, vmem_limit_bytes=LIMIT),
        name="spread_inputs",
    )(meta, object_field, probe, amplitudes)

    plane = (1, 2, length, length)
    whole = lambda *shape: pl.BlockSpec(shape, lambda p: (0,) * len(shape))
    per_slot = pl.BlockSpec(plane, lambda p: (p, 0, 0, 0))
    scalars = pl.BlockSpec(memory_space=pltpu.SMEM)
    window = pltpu.VMEM((2, N * width + 128, N * depth + length), f32)
    quarters = (POS_AVG, N, length, length // N)
    patch, frames = pl.pallas_call(
        cut,
        grid=(POS_AVG,),
        in_specs=[scalars, whole(*cells.shape), ANY],
        out_specs=[per_slot, whole(N, POS_AVG, *amplitudes.shape[1:])],
        scratch_shapes=[window, pltpu.SemaphoreType.DMA((POS_AVG * N,))],
        out_shape=[
            jax.ShapeDtypeStruct((POS_AVG,) + plane[1:], bf16),
            jax.ShapeDtypeStruct((N, POS_AVG) + amplitudes.shape[1:], bf16),
        ],
        compiler_params=pltpu.CompilerParams(vmem_limit_bytes=LIMIT),
        name="cut",
    )(meta_all, cells, frames_all)
    probe_part, terms = pl.pallas_call(
        propagate,
        in_specs=[WHOLE, WHOLE, ANY, WHOLE, WHOLE],
        out_specs=[WHOLE, WHOLE],
        out_shape=[
            jax.ShapeDtypeStruct(mode_all.shape, bf16),
            jax.ShapeDtypeStruct((POS_AVG,) + plane[1:], f32),
        ],
        scratch_shapes=[
            pltpu.VMEM((POS_AVG, 2 * length, length), f32),
            pltpu.VMEM(quarters, bf16),
            pltpu.VMEM((POS_AVG, N - 1) + quarters[2:], bf16),
            pltpu.VMEM(quarters, bf16),
            pltpu.VMEM(frames.shape[1:], bf16),
            pltpu.VMEM((length, 2 * length), bf16),
            pltpu.VMEM((2 * length, length), bf16),
            pltpu.VMEM((2, length, length), f32),
            pltpu.SemaphoreType.DMA((2, 22)),
        ],
        compiler_params=pltpu.CompilerParams(collective_id=2, has_side_effects=True, vmem_limit_bytes=LIMIT),
        name="propagate",
    )(patch, mode_all, frames, table, table_t)
    cells_part = pl.pallas_call(
        place,
        grid=(POS_AVG,),
        in_specs=[scalars, per_slot],
        out_specs=whole(*cells.shape),
        scratch_shapes=[window],
        out_shape=jax.ShapeDtypeStruct(cells.shape, bf16),
        compiler_params=pltpu.CompilerParams(vmem_limit_bytes=LIMIT),
        name="place",
    )(meta_all, terms)
    strip = (N,) + object_field.shape
    object_grad, probe_grad = pl.pallas_call(
        reduce_gradients,
        in_specs=[WHOLE, WHOLE],
        out_specs=[WHOLE, WHOLE],
        out_shape=[jax.ShapeDtypeStruct(object_field.shape, f32), jax.ShapeDtypeStruct(probe.shape, f32)],
        scratch_shapes=[
            pltpu.VMEM((N - 1,) + mode_shape, bf16),
            pltpu.VMEM((2,) + strip, bf16),
            pltpu.VMEM(strip, bf16),
            pltpu.VMEM(strip, bf16),
            pltpu.VMEM(strip, bf16),
            pltpu.VMEM((N - 1,) + object_field.shape, bf16),
            pltpu.VMEM((N,) + mode_shape, bf16),
            pltpu.SemaphoreType.DMA((2, 21)),
        ],
        compiler_params=pltpu.CompilerParams(collective_id=3, has_side_effects=True, vmem_limit_bytes=LIMIT),
        name="reduce_gradients",
    )(probe_part, cells_part)
    return object_grad, probe_grad


def solution(mesh):
    on_device = balanced_device if mesh.shape["rows"] == N and mesh.shape["cols"] == N else general_device
    placed = (
        P("groups", "cols", "rows"),
        P("groups", None, "cols", None),
        P(("groups", "rows"), "cols", None),
        P(("groups", "rows")),
        P(("groups", "rows")),
        P(("groups", "rows")),
    )
    return jax.shard_map(
        on_device,
        mesh=mesh,
        in_specs=placed,
        out_specs=(P("groups", "cols", "rows"), P("groups", None, "cols", None)),
        check_vma=False,
    )
```

```python
import jax
import jax.numpy as jnp
import numpy as np
from jax import lax
from jax.experimental import pallas as pl
from jax.experimental.pallas import tpu as pltpu
from jax.sharding import PartitionSpec as P

POS_AVG = 3
POS_MAX = 6


def shifted(block, axis, distance):
    devices = range(lax.axis_size(axis))
    route = [(i - distance, i) for i in devices if i - distance in devices]
    return lax.ppermute(block, axis, route)


def dft_tables(length):
    indices = jnp.arange(length, dtype=jnp.int32)
    product = indices[:, None] * indices[None, :] % length
    angles = product.astype(jnp.float32) * jnp.float32(2.0 * 3.141592653589793 / length)
    scaling = jnp.float32(1.0 / length**0.5)
    cosine_table = (jnp.cos(angles) * scaling).astype(jnp.bfloat16)
    sine_table = (jnp.sin(angles) * scaling).astype(jnp.bfloat16)
    return (cosine_table, sine_table)


def leading(values, matrix):
    return jnp.einsum("mca,asu->mscu", values, matrix, preferred_element_type=jnp.float32)


def second(values, matrix):
    return jnp.einsum("mscu,scv->muv", values, matrix, preferred_element_type=jnp.float32)


def third(values, matrix):
    return jnp.einsum("muv,vsb->msub", values, matrix, preferred_element_type=jnp.float32)


def fourth(values, matrix):
    return jnp.einsum("msub,sua->mba", values, matrix, preferred_element_type=jnp.float32)


def vacuum_where(block, outside):
    fill_real = jnp.where(outside, jnp.float32(1.0), block[0])
    fill_imag = jnp.where(outside, jnp.float32(0.0), block[1])
    return jnp.stack([fill_real, fill_imag])


def spectral_pass(patch_cells, probe, measured, cosine_table, sine_table, block_count):
    mode_count = probe.shape[0]
    block_cols = patch_cells.shape[1]
    length = patch_cells.shape[2]
    block_freq = length // block_count
    probe_real = probe[:, 0]
    probe_imag = probe[:, 1]
    patch_real = patch_cells[0]
    patch_imag = patch_cells[1]
    wave_real = (probe_real * patch_real - probe_imag * patch_imag).astype(jnp.bfloat16)
    wave_imag = (probe_real * patch_imag + probe_imag * patch_real).astype(jnp.bfloat16)
    cos_lead = cosine_table.reshape(length, block_count, block_freq)
    sin_lead = sine_table.reshape(length, block_count, block_freq)
    first_real = leading(wave_real, cos_lead) + leading(wave_imag, sin_lead)
    first_imag = leading(wave_imag, cos_lead) - leading(wave_real, sin_lead)
    outgoing = jnp.stack([first_real, first_imag], axis=1).astype(jnp.bfloat16)
    outgoing = outgoing.reshape(mode_count, 2, block_count, block_cols * block_freq)
    arrived = lax.all_to_all(outgoing, "cols", split_axis=2, concat_axis=2, tiled=True)
    arrived = arrived.reshape(mode_count, 2, block_count, block_cols, block_freq)
    cos_rows = cosine_table.reshape(block_count, block_cols, length)
    sin_rows = sine_table.reshape(block_count, block_cols, length)
    field_real = second(arrived[:, 0], cos_rows) + second(arrived[:, 1], sin_rows)
    field_imag = second(arrived[:, 1], cos_rows) - second(arrived[:, 0], sin_rows)
    intensity = jnp.sum(field_real * field_real + field_imag * field_imag, axis=0)
    modulus = jnp.sqrt(jnp.maximum(intensity, 0.25))
    factor = 1.0 - measured / modulus
    back_real = (field_real * factor).astype(jnp.bfloat16)
    back_imag = (field_imag * factor).astype(jnp.bfloat16)
    cos_back = cosine_table.reshape(length, block_count, block_cols)
    sin_back = sine_table.reshape(length, block_count, block_cols)
    inner_real = third(back_real, cos_back) - third(back_imag, sin_back)
    inner_imag = third(back_imag, cos_back) + third(back_real, sin_back)
    returning = jnp.stack([inner_real, inner_imag], axis=1).astype(jnp.bfloat16)
    returning = returning.reshape(mode_count, 2, block_count, block_freq * block_cols)
    landed = lax.all_to_all(returning, "cols", split_axis=2, concat_axis=2, tiled=True)
    landed = landed.reshape(mode_count, 2, block_count, block_freq, block_cols)
    cos_freq = cosine_table.reshape(block_count, block_freq, length)
    sin_freq = sine_table.reshape(block_count, block_freq, length)
    grad_real = fourth(landed[:, 0], cos_freq) - fourth(landed[:, 1], sin_freq)
    grad_imag = fourth(landed[:, 1], cos_freq) + fourth(landed[:, 0], sin_freq)
    object_real = jnp.sum(probe_real * grad_real + probe_imag * grad_imag, axis=0)
    object_imag = jnp.sum(probe_real * grad_imag - probe_imag * grad_real, axis=0)
    probe_real_term = patch_real * grad_real + patch_imag * grad_imag
    probe_imag_term = patch_real * grad_imag - patch_imag * grad_real
    return (
        jnp.stack([object_real, object_imag]),
        jnp.stack([probe_real_term, probe_imag_term], axis=1),
    )


def run_positions(
    window,
    probe,
    frames,
    first_rows,
    first_cols,
    slot_total,
    used_count,
    cosine_table,
    sine_table,
    block_count,
):
    block_cols = probe.shape[2]
    length = probe.shape[3]

    def visit_slot(slot_index, state_pair):
        window_grad, probe_sum = state_pair
        first_row = first_rows[slot_index]
        first_col = first_cols[slot_index]
        patch_cells = lax.dynamic_slice(window, (0, first_col, first_row), (2, block_cols, length))
        measured = lax.dynamic_index_in_dim(frames, slot_index, 0, keepdims=False)
        object_term, probe_term = spectral_pass(
            patch_cells, probe, measured, cosine_table, sine_table, block_count
        )
        active = (slot_index < used_count).astype(jnp.float32)
        current = lax.dynamic_slice(window_grad, (0, first_col, first_row), (2, block_cols, length))
        window_grad = lax.dynamic_update_slice(
            window_grad, current + active * object_term, (0, first_col, first_row)
        )
        return (window_grad, probe_sum + active * probe_term)

    initial = (jnp.zeros(window.shape, jnp.float32), jnp.zeros(probe.shape, jnp.float32))
    return lax.fori_loop(0, slot_total, visit_slot, initial)


def general_device(object_field, probe, amplitudes, strip_counts, row_offsets, col_offsets):
    block_cols = object_field.shape[1]
    strip_rows = object_field.shape[2]
    length = probe.shape[3]
    block_count = lax.axis_size("cols")
    strip_total = lax.axis_size("rows")
    cosine_table, sine_table = dft_tables(length)
    beside = shifted(object_field, "cols", -1)
    beside = vacuum_where(beside, lax.axis_index("cols") == block_count - 1)
    paired = jnp.concatenate([object_field, beside], axis=1)
    counts_all, rows_all, cols_all = (
        lax.all_gather(strip_counts, "rows", axis=0, tiled=True),
        lax.all_gather(row_offsets, "rows", axis=0, tiled=True),
        lax.all_gather(col_offsets, "rows", axis=0, tiled=True),
    )
    totals = jnp.cumsum(counts_all)
    starts = totals - counts_all
    position_block = (lax.axis_index("rows") + strip_total // 2) % strip_total
    my_positions = position_block * POS_AVG + jnp.arange(POS_AVG, dtype=jnp.int32)
    strip_of = jnp.sum((totals[None, :] <= my_positions[:, None]).astype(jnp.int32), axis=1)
    wanted = strip_of * POS_MAX + my_positions - jnp.take(starts, strip_of)
    first_rows = strip_of * strip_rows + jnp.take(rows_all, wanted)
    first_cols = jnp.take(cols_all, wanted)
    empty_frames = jnp.zeros((POS_AVG,) + amplitudes.shape[1:], jnp.float32)
    received = lax.all_gather(amplitudes, "rows", axis=0, tiled=True)
    inside = (wanted >= 0) & (wanted < received.shape[0])
    picked = jnp.take(received, jnp.clip(wanted, 0, received.shape[0] - 1), axis=0)
    frames = jnp.where(inside[:, None, None], picked, empty_frames)
    column_all = lax.all_gather(paired, "rows", axis=2, tiled=True)
    all_rows = column_all.shape[2]
    vacuum_tail = vacuum_where(jnp.zeros((2, column_all.shape[1], length), jnp.float32), True)
    window = jnp.concatenate([column_all, vacuum_tail], axis=2)
    window_grad, probe_sum = run_positions(
        window,
        probe,
        frames,
        first_rows,
        first_cols,
        POS_AVG,
        POS_AVG,
        cosine_table,
        sine_table,
        block_count,
    )
    folded = window_grad[:, :, :all_rows]
    summed = lax.psum_scatter(folded, "rows", scatter_dimension=2, tiled=True)
    upper_half = shifted(summed[:, block_cols:], "cols", 1)
    object_grad = summed[:, :block_cols] + upper_half
    probe_grad = lax.psum(probe_sum, "rows")
    return (object_grad, probe_grad)


def tables(length):
    indices = np.arange(length)
    angles = (indices[:, None] * indices[None, :] % length) * (2.0 * np.pi / length)
    scaling = 1.0 / length**0.5
    cosine, sine = np.cos(angles) * scaling, np.sin(angles) * scaling
    table = np.block([[cosine, -sine], [sine, cosine]])
    return jnp.asarray(table, jnp.bfloat16), jnp.asarray(table.T, jnp.bfloat16)


ANY = pl.BlockSpec(memory_space=pl.ANY)
WHOLE = pl.BlockSpec(memory_space=pltpu.VMEM)
LIMIT = 56 * 1024 * 1024
N = 4


def greet(axes):
    barrier = pltpu.get_barrier_semaphore()
    for axis in axes:
        me = lax.axis_index(axis)
        for k in range(1, N):
            pl.semaphore_signal(
                barrier, inc=1, device_id={axis: lax.rem(me + k, N)}, device_id_type=pl.DeviceIdType.MESH
            )
    pl.semaphore_wait(barrier, (N - 1) * len(axes))


def remote(src, dst, sems, slot, device):
    return pltpu.make_async_remote_copy(
        src_ref=src,
        dst_ref=dst,
        send_sem=sems.at[0, slot],
        recv_sem=sems.at[1, slot],
        device_id=device,
        device_id_type=pl.DeviceIdType.MESH,
    )


class Gather:
    def __init__(self, axis, src, out, sems, base, scatter=False):
        self.me = lax.axis_index(axis)
        self.axis, self.src, self.out, self.sems, self.base, self.scatter = axis, src, out, sems, base, scatter

    def piece(self, index):
        return self.src.at[index] if self.scatter else self.src

    def start(self):
        self.local = pltpu.make_async_copy(
            self.piece(self.me), self.out.at[self.me], self.sems.at[0, self.base]
        )
        self.sent = []
        for k in range(1, N):
            to = lax.rem(self.me + k, N)
            copy = remote(self.piece(to), self.out.at[self.me], self.sems, self.base + k, {self.axis: to})
            copy.start()
            self.sent.append(copy)
        self.local.start()

    def wait(self):
        self.local.wait()
        for k in range(1, N):
            source = lax.rem(self.me + N - k, N)
            remote(
                self.piece(source), self.out.at[source], self.sems, self.base + k, {self.axis: source}
            ).wait_recv()
        for copy in self.sent:
            copy.wait_send()


def spread_inputs(
    meta, cells, probe, frames, meta_out, probe_out, cells_out, frames_out,
    raw_probe, raw_frames, own_cells, own_probe, own_frames, sems, local
):
    bf16 = jnp.bfloat16
    row, col = lax.axis_index("rows"), lax.axis_index("cols")
    sibling = row + 1 - 2 * lax.rem(row, 2)
    across = lax.rem(row + 2, N)
    opposite = lax.rem(sibling + 2, N)
    right, left = lax.rem(col + 1, N), lax.rem(col + N - 1, N)
    load_probe = pltpu.make_async_copy(probe.at[row], raw_probe, local.at[0])
    load_frames = pltpu.make_async_copy(frames, raw_frames, local.at[1])
    load_probe.start()
    load_frames.start()
    own_cells[...] = cells[...].astype(bf16)
    greet(("rows", "cols"))

    def line_copy(base, src, dst, origin, rightward):
        return pltpu.make_async_remote_copy(
            src_ref=src,
            dst_ref=dst,
            send_sem=sems.at[0 if rightward else 2, base + origin],
            recv_sem=sems.at[1, base + origin],
            device_id={"cols": right if rightward else left},
            device_id_type=pl.DeviceIdType.MESH,
        )

    def line_start(base, src, dst, origin, rightward):
        @pl.when(col < N - 1 if rightward else col > 0)
        def _():
            line_copy(base, src, dst, origin, rightward).start()

    def line_sent(base, src, dst, origin, rightward):
        @pl.when(col < N - 1 if rightward else col > 0)
        def _():
            line_copy(base, src, dst, origin, rightward).wait_send()

    def cell(index, origin):
        return cells_out.at[index, origin]

    def row_copy(slot, src, dst, to):
        return remote(src, dst, sems, slot, {"rows": to})

    for rightward in (True, False):
        line_start(0, own_cells, cell(row, col), col, rightward)
    small = Gather("rows", meta, meta_out, sems, 8)
    small.start()
    row_copy(16 + col, own_cells, cell(row, col), across).start()
    row_copy(20 + col, own_cells, cell(row, col), sibling).start()
    keep_cells = pltpu.make_async_copy(own_cells, cell(row, col), local.at[2])
    keep_cells.start()
    load_probe.wait()
    own_probe[...] = raw_probe[...].astype(bf16)
    for rightward in (True, False):
        line_start(4, own_probe, probe_out.at[col], col, rightward)
    keep_probe = pltpu.make_async_copy(own_probe, probe_out.at[col], local.at[3])
    keep_probe.start()
    load_frames.wait()
    own_frames[...] = raw_frames[...].astype(bf16)
    keep_frames = pltpu.make_async_copy(own_frames, frames_out.at[row], local.at[4])

    @pl.when(row == col)
    def _():
        keep_frames.start()

    def frame_copy(k):
        return row_copy(12 + k, own_frames, frames_out.at[row], lax.rem(row + k, N))

    for k in range(1, N):

        @pl.when(lax.rem(row + k, N) == col)
        def _():
            frame_copy(k).start()

    def from_side(d, rightward):
        if rightward:
            return col >= d, lax.rem(col + N - d, N)
        return col + d < N, lax.rem(col + d, N)

    for d in range(1, N):
        for rightward in (True, False):
            here, origin = from_side(d, rightward)

            @pl.when(here)
            def _():
                mine = cell(row, origin)
                line_copy(0, mine, mine, origin, rightward).wait_recv()
                line_start(0, mine, mine, origin, rightward)
                row_copy(16 + origin, mine, mine, across).start()
                row_copy(20 + origin, mine, mine, sibling).start()

        for rightward in (True, False):
            here, origin = from_side(d, rightward)

            @pl.when(here)
            def _():
                mine = probe_out.at[origin]
                line_copy(4, mine, mine, origin, rightward).wait_recv()
                line_start(4, mine, mine, origin, rightward)

        if d == 1:
            landed = cell(across, col)
            row_copy(16 + col, landed, landed, across).wait_recv()
            row_copy(24 + col, landed, landed, sibling).start()
    for k in range(1, N):
        origin = lax.rem(col + k, N)
        landed = cell(across, origin)
        row_copy(16 + origin, landed, landed, across).wait_recv()
        row_copy(24 + origin, landed, landed, sibling).start()
    for origin in range(N):
        near, far = cell(sibling, origin), cell(opposite, origin)
        row_copy(20 + origin, near, near, sibling).wait_recv()
        row_copy(24 + origin, far, far, sibling).wait_recv()
    keep_cells.wait()
    keep_probe.wait()
    for rightward in (True, False):
        line_sent(0, own_cells, cell(row, col), col, rightward)
        line_sent(4, own_probe, probe_out.at[col], col, rightward)
        for d in range(1, N):
            here, origin = from_side(d, rightward)

            @pl.when(here)
            def _():
                line_sent(0, cell(row, origin), cell(row, origin), origin, rightward)
                line_sent(4, probe_out.at[origin], probe_out.at[origin], origin, rightward)

    for origin in range(N):
        mine, landed = cell(row, origin), cell(across, origin)
        row_copy(16 + origin, mine, mine, across).wait_send()
        row_copy(20 + origin, mine, mine, sibling).wait_send()
        row_copy(24 + origin, landed, landed, sibling).wait_send()
    small.wait()

    @pl.when(row == col)
    def _():
        keep_frames.wait()
        for k in range(1, N):
            source = lax.rem(row + N - k, N)
            row_copy(12 + k, own_frames, frames_out.at[source], source).wait_recv()

    for k in range(1, N):

        @pl.when(lax.rem(row + k, N) == col)
        def _():
            frame_copy(k).wait_send()


def propagate(
    patch, probe, frames, table, table_t, probe_out, terms_out,
    terms, field, power, near, relay, far, scale, measured, wide, tall, total, sems, local
):
    row, col = lax.axis_index("rows"), lax.axis_index("cols")
    sibling = row + 1 - 2 * lax.rem(row, 2)
    across = lax.rem(row + 2, N)
    opposite = lax.rem(sibling + 2, N)
    length = patch.shape[-1]
    quarter = length // N
    f32, bf16 = jnp.float32, jnp.bfloat16
    greet(("rows", "cols"))

    def frame_copy(to):
        return remote(frames.at[to], measured, sems, 18 + lax.rem(to + N - row, N), {"cols": to})

    local_frames = pltpu.make_async_copy(frames.at[col], measured, sems.at[0, 18])

    @pl.when(row == col)
    def _():
        local_frames.start()
        for k in range(1, N):
            frame_copy(lax.rem(col + k, N)).start()

    def near_copy(p, half):
        quarters = opposite if half else sibling
        return remote(power.at[p, quarters], near.at[p, half], sems, 2 * p + half, {"rows": sibling})

    def far_copy(p):
        return remote(relay.at[p], far.at[p], sems, 6 + p, {"rows": across})

    def scale_copy(p, kind, index):
        to = across if kind == 0 else sibling
        return remote(scale.at[p, index], scale.at[p, index], sems, 9 + 3 * kind + p, {"rows": to})

    def pass_on(p):
        near_copy(p, 1).wait_recv()
        relay[p] = (power[p, across].astype(f32) + near[p, 1].astype(f32)).astype(bf16)
        far_copy(p).start()

    def factors(p):
        near_copy(p, 0).wait_recv()
        far_copy(p).wait_recv()
        intensity = power[p, row].astype(f32) + near[p, 0].astype(f32) + far[p].astype(f32)
        amplitude = measured[p].astype(f32).T
        scale[p, row] = (1.0 - amplitude * lax.rsqrt(jnp.maximum(intensity, 0.25))).astype(bf16)
        scale_copy(p, 0, row).start()
        scale_copy(p, 1, row).start()

    def hand_over(p):
        scale_copy(p, 0, across).wait_recv()
        scale_copy(p, 2, across).start()

    def transform(p, carry):
        probe_real = probe[:, 0].reshape(length, length).astype(f32)
        probe_imag = probe[:, 1].reshape(length, length).astype(f32)
        patch_real = patch[p, 0].astype(f32)
        patch_imag = patch[p, 1].astype(f32)
        wide[:, :length] = (probe_real * patch_real - probe_imag * patch_imag).astype(bf16)
        wide[:, length:] = (probe_real * patch_imag + probe_imag * patch_real).astype(bf16)
        spread = mul(wide[...], table[...])
        tall[:length] = spread[:, :length].astype(bf16)
        tall[length:] = spread[:, length:].astype(bf16)
        result = mul(table_t[...], tall[...])
        field[p] = result
        square = result[:length] * result[:length] + result[length:] * result[length:]
        for q in range(N):
            power[p, q] = square[:, q * quarter : (q + 1) * quarter].astype(bf16)
        near_copy(p, 1).start()
        near_copy(p, 0).start()

        @pl.when(p >= 1)
        def _():
            pass_on(p - 1)

        return carry

    lax.fori_loop(0, POS_AVG, transform, 0)
    pass_on(POS_AVG - 1)

    @pl.when(row == col)
    def _():
        local_frames.wait()

    for k in range(1, N):

        @pl.when(lax.rem(row + k, N) == col)
        def _():
            remote(measured, measured, sems, 18 + k, {"cols": row}).wait_recv()

    for p in range(POS_AVG):
        factors(p)
        if p > 0:
            hand_over(p - 1)
    total[...] = jnp.zeros(total.shape, f32)

    def back_transform(p, carry):
        scale_copy(p, 1, sibling).wait_recv()
        scale_copy(p, 2, opposite).wait_recv()
        for q in range(N):
            lanes = pl.ds(q * quarter, quarter)
            gain = scale[p, q].astype(f32)
            tall[:length, lanes] = (field[p, :length, lanes] * gain).astype(bf16)
            tall[length:, lanes] = (field[p, length:, lanes] * gain).astype(bf16)
        inner = mul(table[...], tall[...])
        wide[:, :length] = inner[:length].astype(bf16)
        wide[:, length:] = inner[length:].astype(bf16)
        back = mul(wide[...], table_t[...])
        back_real, back_imag = back[:, :length], back[:, length:]
        probe_real = probe[:, 0].reshape(length, length).astype(f32)
        probe_imag = probe[:, 1].reshape(length, length).astype(f32)
        terms[p, 0] = probe_real * back_real + probe_imag * back_imag
        terms[p, 1] = probe_real * back_imag - probe_imag * back_real
        pltpu.make_async_copy(terms.at[p], terms_out.at[p], local.at[p]).start()
        patch_real = patch[p, 0].astype(f32)
        patch_imag = patch[p, 1].astype(f32)
        total[0] += patch_real * back_real + patch_imag * back_imag
        total[1] += patch_real * back_imag - patch_imag * back_real

        @pl.when(p == 0)
        def _():
            hand_over(POS_AVG - 1)

        return carry

    lax.fori_loop(0, POS_AVG, back_transform, 0)
    for b in range(N):
        for part in range(2):
            probe_out[b, part] = total[part, b * quarter : (b + 1) * quarter].astype(bf16)

    def finish(p, carry):
        near_copy(p, 0).wait_send()
        near_copy(p, 1).wait_send()
        far_copy(p).wait_send()
        scale_copy(p, 0, row).wait_send()
        scale_copy(p, 1, row).wait_send()
        scale_copy(p, 2, across).wait_send()
        pltpu.make_async_copy(terms.at[p], terms_out.at[p], local.at[p]).wait()
        return carry

    lax.fori_loop(0, POS_AVG, finish, 0)

    @pl.when(row == col)
    def _():
        for k in range(1, N):
            frame_copy(lax.rem(col + k, N)).wait_send()


class LineSum:
    def __init__(self, blocks, outgoing, from_left, from_right, sems, base):
        self.blocks, self.outgoing, self.from_left, self.from_right = blocks, outgoing, from_left, from_right
        self.sems, self.base = sems, base
        self.col = lax.axis_index("cols")

    def copy(self, d, rightward):
        col = self.col
        to = lax.rem(col + 1, N) if rightward else lax.rem(col + N - 1, N)
        dst = self.from_left if rightward else self.from_right
        slot = self.base + d + (0 if rightward else N)
        return remote(self.outgoing.at[d], dst.at[d], self.sems, slot, {"cols": to})

    def step(self, d, rightward):
        col = self.col
        landed = self.from_left if rightward else self.from_right
        first = 0 if rightward else N - 1

        @pl.when((col < d) if rightward else (col > d))
        def _():
            @pl.when(col == first)
            def _():
                self.outgoing[d] = self.blocks(d).astype(jnp.bfloat16)

            @pl.when(col != first)
            def _():
                self.copy(d, rightward).wait_recv()
                self.outgoing[d] = (self.blocks(d) + landed[d].astype(jnp.float32)).astype(jnp.bfloat16)

            self.copy(d, rightward).start()

    def finish(self, out):
        col = self.col
        out[...] = self.blocks(col)

        @pl.when(col > 0)
        def _():
            self.copy(col, True).wait_recv()
            out[...] += self.from_left[col].astype(jnp.float32)

        @pl.when(col < N - 1)
        def _():
            self.copy(col, False).wait_recv()
            out[...] += self.from_right[col].astype(jnp.float32)

    def wait_sent(self):
        for d in range(N):
            for rightward in (True, False):

                @pl.when((self.col < d) if rightward else (self.col > d))
                def _():
                    self.copy(d, rightward).wait_send()


def reduce_gradients(
    probe_part, cells_part, cells_out, probe_out,
    near, far, relay, cells_total, cells_line, cells_left, cells_right,
    probe_line, probe_left, probe_right, probe_total, probe_all, sems,
):
    f32, bf16 = jnp.float32, jnp.bfloat16
    row, col = lax.axis_index("rows"), lax.axis_index("cols")
    sibling = row + 1 - 2 * lax.rem(row, 2)
    across = lax.rem(row + 2, N)
    opposite = lax.rem(sibling + 2, N)
    greet(("rows", "cols"))
    modes = LineSum(lambda d: probe_part[d].astype(f32), probe_line, probe_left, probe_right, sems, 0)
    cells = LineSum(lambda d: cells_total[d], cells_line, cells_left, cells_right, sems, 8)

    def near_copy(half, b):
        strip = opposite if half else sibling
        return remote(cells_part.at[strip, b], near.at[half, b], sems, 16 + 4 * half + b, {"rows": sibling})

    def far_copy(b):
        return remote(relay.at[b], far.at[b], sems, 24 + b, {"rows": across})

    def mode_copy(slot, index, to):
        return remote(probe_all.at[index], probe_all.at[index], sems, slot, {"rows": to})

    modes.step(N - 1, True)
    modes.step(0, False)
    for half in (1, 0):
        for b in range(N):
            near_copy(half, b).start()
    for b in range(N):
        near_copy(1, b).wait_recv()
        relay[b] = (cells_part[across, b].astype(f32) + near[1, b].astype(f32)).astype(bf16)
        far_copy(b).start()
    for distance in range(1, N - 1):
        modes.step(N - 1 - distance, True)
        modes.step(distance, False)
    for b in range(N):
        near_copy(0, b).wait_recv()
        far_copy(b).wait_recv()
        cells_total[b] = cells_part[row, b].astype(f32) + near[0, b].astype(f32) + far[b].astype(f32)
    cells.step(N - 1, True)
    cells.step(0, False)
    modes.finish(probe_total)
    probe_all[row] = probe_total[...].astype(bf16)
    sent = [mode_copy(28, row, across), mode_copy(29, row, sibling)]
    for copy in sent:
        copy.start()
    for distance in range(1, N - 1):
        cells.step(N - 1 - distance, True)
        cells.step(distance, False)
    mode_copy(28, across, across).wait_recv()
    forwarded = mode_copy(30, across, sibling)
    forwarded.start()
    sent.append(forwarded)
    mode_copy(29, sibling, sibling).wait_recv()
    mode_copy(30, opposite, sibling).wait_recv()
    probe_out[...] = probe_all[...].astype(f32)
    cells.finish(cells_out)
    for copy in sent:
        copy.wait_send()
    for b in range(N):
        near_copy(0, b).wait_send()
        near_copy(1, b).wait_send()
        far_copy(b).wait_send()
    modes.wait_sent()
    cells.wait_sent()


def mul(left, right):
    return jnp.dot(left, right, preferred_element_type=jnp.float32)


def locate(meta, position, depth):
    strip, slot, start = 0, 0, 0
    for s in range(N):
        count = meta[s, 0, 0]
        inside = (position >= start) & (position < start + count)
        strip = jnp.where(inside, s, strip)
        slot = jnp.where(inside, position - start, slot)
        start = start + count
    return strip, slot, strip * depth + meta[strip, 0, 1 + slot], meta[strip, 0, 1 + POS_MAX + slot]


def iota(shape, axis):
    return lax.broadcasted_iota(jnp.int32, shape, axis)


def cut(meta, cells, frames_all, patch_out, frames_out, window, sems):
    p = pl.program_id(0)
    strips, blocks, _, width, depth = cells.shape
    length = patch_out.shape[-1]
    all_rows, all_cols = strips * depth, blocks * width

    def frame_copies():
        copies = []
        for i in range(POS_AVG * N):
            strip, slot, _, _ = locate(meta, i, depth)
            copies.append(
                pltpu.make_async_copy(
                    frames_all.at[strip, slot], frames_out.at[i // POS_AVG, i % POS_AVG], sems.at[i]
                )
            )
        return copies

    @pl.when(p == 0)
    def _():
        for copy in frame_copies():
            copy.start()
        for part, fill in ((0, 1.0), (1, 0.0)):
            window[part, all_cols:, :] = jnp.full((width, window.shape[2]), fill, jnp.float32)
            window[part, :all_cols, all_rows:] = jnp.full((all_cols, length), fill, jnp.float32)
            for s in range(strips):
                for b in range(blocks):
                    window[part, pl.ds(b * width, width), pl.ds(s * depth, depth)] = cells[s, b, part].astype(
                        jnp.float32
                    )

    _, _, first, column = locate(meta, lax.axis_index("cols") * POS_AVG + p, depth)
    rest = lax.rem(first, 128)
    base = first - rest
    low = lax.rem(column, 8)
    top = pl.multiple_of(column - low, 8)
    groups = length // 8
    for part in range(2):
        before = None
        for j in range(length // 128 + 1):
            block = window[part, pl.ds(top, length + 8), pl.ds(pl.multiple_of(base + 128 * j, 128), 128)]
            block = pltpu.roll(block.reshape(groups + 1, 8, 128), lax.rem(8 - low, 8), 1)
            block = jnp.where(iota((groups, 8, 128), 1) < 8 - low, block[:groups], block[1:])
            block = pltpu.roll(block.reshape(length, 128), lax.rem(128 - rest, 128), 1)
            if j > 0:
                joined = jnp.where(iota((length, 128), 1) < 128 - rest, before, block)
                patch_out[0, part, :, 128 * (j - 1) : 128 * j] = joined.astype(jnp.bfloat16)
            before = block

    @pl.when(p == pl.num_programs(0) - 1)
    def _():
        for copy in frame_copies():
            copy.wait()


def place(meta, terms, cells_out, window):
    p = pl.program_id(0)
    strips, blocks, _, width, depth = cells_out.shape
    length = terms.shape[-1]

    @pl.when(p == 0)
    def _():
        window[...] = jnp.zeros(window.shape, jnp.float32)

    _, _, first, column = locate(meta, lax.axis_index("cols") * POS_AVG + p, depth)
    rest = lax.rem(first, 128)
    base = first - rest
    low = lax.rem(column, 8)
    top = pl.multiple_of(column - low, 8)
    groups = length // 8
    edge = jnp.zeros((1, 8, 128), jnp.float32)
    for part in range(2):
        before = jnp.zeros((length + 8, 128), jnp.float32)
        for j in range(length // 128 + 1):
            if j < length // 128:
                block = terms[0, part, :, 128 * j : 128 * (j + 1)].reshape(groups, 8, 128)
                block = pltpu.roll(block, low, 1)
                above = jnp.concatenate([edge, block], axis=0)
                below = jnp.concatenate([block, edge], axis=0)
                block = jnp.where(iota((groups + 1, 8, 128), 1) < low, above, below)
                block = pltpu.roll(block.reshape(length + 8, 128), rest, 1)
            else:
                block = jnp.zeros((length + 8, 128), jnp.float32)
            joined = jnp.where(iota((length + 8, 128), 1) < rest, before, block)
            window[part, pl.ds(top, length + 8), pl.ds(pl.multiple_of(base + 128 * j, 128), 128)] += joined
            before = block

    @pl.when(p == pl.num_programs(0) - 1)
    def _():
        for part in range(2):
            for b in range(blocks):
                for s in range(strips):
                    cells_out[s, b, part] = window[part, pl.ds(b * width, width), pl.ds(s * depth, depth)].astype(
                        jnp.bfloat16
                    )


def balanced_device(object_field, probe, amplitudes, strip_counts, row_offsets, col_offsets):
    f32, bf16 = jnp.float32, jnp.bfloat16
    width, depth = object_field.shape[1:]
    length = probe.shape[3]
    row, col = lax.axis_index("rows"), lax.axis_index("cols")
    table, table_t = tables(length)
    meta = jnp.concatenate([strip_counts, row_offsets, col_offsets])
    meta = jnp.pad(meta, (0, 128 - meta.shape[0]))[None, :]
    mode_shape = probe.shape[1:]
    meta_all, mode_all, cells, frames_all = pl.pallas_call(
        spread_inputs,
        in_specs=[ANY, WHOLE, ANY, ANY],
        out_specs=[ANY] * 4,
        out_shape=[
            jax.ShapeDtypeStruct((N, 1, 128), jnp.int32),
            jax.ShapeDtypeStruct((N,) + mode_shape, bf16),
            jax.ShapeDtypeStruct((N, N) + object_field.shape, bf16),
            jax.ShapeDtypeStruct((N,) + amplitudes.shape, bf16),
        ],
        scratch_shapes=[
            pltpu.VMEM(mode_shape, f32),
            pltpu.VMEM(amplitudes.shape, f32),
            pltpu.VMEM(object_field.shape, bf16),
            pltpu.VMEM(mode_shape, bf16),
            pltpu.VMEM(amplitudes.shape, bf16),
            pltpu.SemaphoreType.DMA((3, 28)),
            pltpu.SemaphoreType.DMA((5,)),
        ],
        compiler_params=pltpu.CompilerParams(collective_id=1, has_side_effects=True, vmem_limit_bytes=LIMIT),
        name="spread_inputs",
    )(meta, object_field, probe, amplitudes)

    plane = (1, 2, length, length)
    whole = lambda *shape: pl.BlockSpec(shape, lambda p: (0,) * len(shape))
    per_slot = pl.BlockSpec(plane, lambda p: (p, 0, 0, 0))
    scalars = pl.BlockSpec(memory_space=pltpu.SMEM)
    window = pltpu.VMEM((2, N * width + 128, N * depth + length), f32)
    quarters = (POS_AVG, N, length, length // N)
    patch, frames = pl.pallas_call(
        cut,
        grid=(POS_AVG,),
        in_specs=[scalars, whole(*cells.shape), ANY],
        out_specs=[per_slot, whole(N, POS_AVG, *amplitudes.shape[1:])],
        scratch_shapes=[window, pltpu.SemaphoreType.DMA((POS_AVG * N,))],
        out_shape=[
            jax.ShapeDtypeStruct((POS_AVG,) + plane[1:], bf16),
            jax.ShapeDtypeStruct((N, POS_AVG) + amplitudes.shape[1:], bf16),
        ],
        compiler_params=pltpu.CompilerParams(vmem_limit_bytes=LIMIT),
        name="cut",
    )(meta_all, cells, frames_all)
    probe_part, terms = pl.pallas_call(
        propagate,
        in_specs=[WHOLE, WHOLE, ANY, WHOLE, WHOLE],
        out_specs=[WHOLE, ANY],
        out_shape=[
            jax.ShapeDtypeStruct(mode_all.shape, bf16),
            jax.ShapeDtypeStruct((POS_AVG,) + plane[1:], f32),
        ],
        scratch_shapes=[
            pltpu.VMEM((POS_AVG,) + plane[1:], f32),
            pltpu.VMEM((POS_AVG, 2 * length, length), f32),
            pltpu.VMEM(quarters, bf16),
            pltpu.VMEM((POS_AVG, 2) + quarters[2:], bf16),
            pltpu.VMEM((POS_AVG,) + quarters[2:], bf16),
            pltpu.VMEM((POS_AVG,) + quarters[2:], bf16),
            pltpu.VMEM(quarters, bf16),
            pltpu.VMEM(frames.shape[1:], bf16),
            pltpu.VMEM((length, 2 * length), bf16),
            pltpu.VMEM((2 * length, length), bf16),
            pltpu.VMEM((2, length, length), f32),
            pltpu.SemaphoreType.DMA((2, 22)),
            pltpu.SemaphoreType.DMA((POS_AVG,)),
        ],
        compiler_params=pltpu.CompilerParams(collective_id=2, has_side_effects=True, vmem_limit_bytes=LIMIT),
        name="propagate",
    )(patch, mode_all, frames, table, table_t)
    cells_part = pl.pallas_call(
        place,
        grid=(POS_AVG,),
        in_specs=[scalars, per_slot],
        out_specs=whole(*cells.shape),
        scratch_shapes=[window],
        out_shape=jax.ShapeDtypeStruct(cells.shape, bf16),
        compiler_params=pltpu.CompilerParams(vmem_limit_bytes=LIMIT),
        name="place",
    )(meta_all, terms)
    strip = (N,) + object_field.shape
    object_grad, probe_grad = pl.pallas_call(
        reduce_gradients,
        in_specs=[WHOLE, WHOLE],
        out_specs=[WHOLE, WHOLE],
        out_shape=[jax.ShapeDtypeStruct(object_field.shape, f32), jax.ShapeDtypeStruct(probe.shape, f32)],
        scratch_shapes=[
            pltpu.VMEM((2,) + strip, bf16),
            pltpu.VMEM(strip, bf16),
            pltpu.VMEM(strip, bf16),
            pltpu.VMEM(strip, f32),
            pltpu.VMEM(strip, bf16),
            pltpu.VMEM(strip, bf16),
            pltpu.VMEM(strip, bf16),
            pltpu.VMEM((N,) + mode_shape, bf16),
            pltpu.VMEM((N,) + mode_shape, bf16),
            pltpu.VMEM((N,) + mode_shape, bf16),
            pltpu.VMEM(mode_shape, f32),
            pltpu.VMEM((N,) + mode_shape, bf16),
            pltpu.SemaphoreType.DMA((2, 31)),
        ],
        compiler_params=pltpu.CompilerParams(collective_id=3, has_side_effects=True, vmem_limit_bytes=LIMIT),
        name="reduce_gradients",
    )(probe_part, cells_part)
    return object_grad, probe_grad


def solution(mesh):
    on_device = balanced_device if mesh.shape["rows"] == N and mesh.shape["cols"] == N else general_device
    placed = (
        P("groups", "cols", "rows"),
        P("groups", None, "cols", None),
        P(("groups", "rows"), "cols", None),
        P(("groups", "rows")),
        P(("groups", "rows")),
        P(("groups", "rows")),
    )
    return jax.shard_map(
        on_device,
        mesh=mesh,
        in_specs=placed,
        out_specs=(P("groups", "cols", "rows"), P("groups", None, "cols", None)),
        check_vma=False,
    )
```

```python
import jax
import jax.numpy as jnp
import numpy as np
from jax import lax
from jax.experimental import pallas as pl
from jax.experimental.pallas import tpu as pltpu
from jax.sharding import PartitionSpec as P

POS_AVG = 3
POS_MAX = 6


def shifted(block, axis, distance):
    devices = range(lax.axis_size(axis))
    route = [(i - distance, i) for i in devices if i - distance in devices]
    return lax.ppermute(block, axis, route)


def dft_tables(length):
    indices = jnp.arange(length, dtype=jnp.int32)
    product = indices[:, None] * indices[None, :] % length
    angles = product.astype(jnp.float32) * jnp.float32(2.0 * 3.141592653589793 / length)
    scaling = jnp.float32(1.0 / length**0.5)
    cosine_table = (jnp.cos(angles) * scaling).astype(jnp.bfloat16)
    sine_table = (jnp.sin(angles) * scaling).astype(jnp.bfloat16)
    return (cosine_table, sine_table)


def leading(values, matrix):
    return jnp.einsum("mca,asu->mscu", values, matrix, preferred_element_type=jnp.float32)


def second(values, matrix):
    return jnp.einsum("mscu,scv->muv", values, matrix, preferred_element_type=jnp.float32)


def third(values, matrix):
    return jnp.einsum("muv,vsb->msub", values, matrix, preferred_element_type=jnp.float32)


def fourth(values, matrix):
    return jnp.einsum("msub,sua->mba", values, matrix, preferred_element_type=jnp.float32)


def vacuum_where(block, outside):
    fill_real = jnp.where(outside, jnp.float32(1.0), block[0])
    fill_imag = jnp.where(outside, jnp.float32(0.0), block[1])
    return jnp.stack([fill_real, fill_imag])


def spectral_pass(patch_cells, probe, measured, cosine_table, sine_table, block_count):
    mode_count = probe.shape[0]
    block_cols = patch_cells.shape[1]
    length = patch_cells.shape[2]
    block_freq = length // block_count
    probe_real = probe[:, 0]
    probe_imag = probe[:, 1]
    patch_real = patch_cells[0]
    patch_imag = patch_cells[1]
    wave_real = (probe_real * patch_real - probe_imag * patch_imag).astype(jnp.bfloat16)
    wave_imag = (probe_real * patch_imag + probe_imag * patch_real).astype(jnp.bfloat16)
    cos_lead = cosine_table.reshape(length, block_count, block_freq)
    sin_lead = sine_table.reshape(length, block_count, block_freq)
    first_real = leading(wave_real, cos_lead) + leading(wave_imag, sin_lead)
    first_imag = leading(wave_imag, cos_lead) - leading(wave_real, sin_lead)
    outgoing = jnp.stack([first_real, first_imag], axis=1).astype(jnp.bfloat16)
    outgoing = outgoing.reshape(mode_count, 2, block_count, block_cols * block_freq)
    arrived = lax.all_to_all(outgoing, "cols", split_axis=2, concat_axis=2, tiled=True)
    arrived = arrived.reshape(mode_count, 2, block_count, block_cols, block_freq)
    cos_rows = cosine_table.reshape(block_count, block_cols, length)
    sin_rows = sine_table.reshape(block_count, block_cols, length)
    field_real = second(arrived[:, 0], cos_rows) + second(arrived[:, 1], sin_rows)
    field_imag = second(arrived[:, 1], cos_rows) - second(arrived[:, 0], sin_rows)
    intensity = jnp.sum(field_real * field_real + field_imag * field_imag, axis=0)
    modulus = jnp.sqrt(jnp.maximum(intensity, 0.25))
    factor = 1.0 - measured / modulus
    back_real = (field_real * factor).astype(jnp.bfloat16)
    back_imag = (field_imag * factor).astype(jnp.bfloat16)
    cos_back = cosine_table.reshape(length, block_count, block_cols)
    sin_back = sine_table.reshape(length, block_count, block_cols)
    inner_real = third(back_real, cos_back) - third(back_imag, sin_back)
    inner_imag = third(back_imag, cos_back) + third(back_real, sin_back)
    returning = jnp.stack([inner_real, inner_imag], axis=1).astype(jnp.bfloat16)
    returning = returning.reshape(mode_count, 2, block_count, block_freq * block_cols)
    landed = lax.all_to_all(returning, "cols", split_axis=2, concat_axis=2, tiled=True)
    landed = landed.reshape(mode_count, 2, block_count, block_freq, block_cols)
    cos_freq = cosine_table.reshape(block_count, block_freq, length)
    sin_freq = sine_table.reshape(block_count, block_freq, length)
    grad_real = fourth(landed[:, 0], cos_freq) - fourth(landed[:, 1], sin_freq)
    grad_imag = fourth(landed[:, 1], cos_freq) + fourth(landed[:, 0], sin_freq)
    object_real = jnp.sum(probe_real * grad_real + probe_imag * grad_imag, axis=0)
    object_imag = jnp.sum(probe_real * grad_imag - probe_imag * grad_real, axis=0)
    probe_real_term = patch_real * grad_real + patch_imag * grad_imag
    probe_imag_term = patch_real * grad_imag - patch_imag * grad_real
    return (
        jnp.stack([object_real, object_imag]),
        jnp.stack([probe_real_term, probe_imag_term], axis=1),
    )


def run_positions(
    window,
    probe,
    frames,
    first_rows,
    first_cols,
    slot_total,
    used_count,
    cosine_table,
    sine_table,
    block_count,
):
    block_cols = probe.shape[2]
    length = probe.shape[3]

    def visit_slot(slot_index, state_pair):
        window_grad, probe_sum = state_pair
        first_row = first_rows[slot_index]
        first_col = first_cols[slot_index]
        patch_cells = lax.dynamic_slice(window, (0, first_col, first_row), (2, block_cols, length))
        measured = lax.dynamic_index_in_dim(frames, slot_index, 0, keepdims=False)
        object_term, probe_term = spectral_pass(
            patch_cells, probe, measured, cosine_table, sine_table, block_count
        )
        active = (slot_index < used_count).astype(jnp.float32)
        current = lax.dynamic_slice(window_grad, (0, first_col, first_row), (2, block_cols, length))
        window_grad = lax.dynamic_update_slice(
            window_grad, current + active * object_term, (0, first_col, first_row)
        )
        return (window_grad, probe_sum + active * probe_term)

    initial = (jnp.zeros(window.shape, jnp.float32), jnp.zeros(probe.shape, jnp.float32))
    return lax.fori_loop(0, slot_total, visit_slot, initial)


def general_device(object_field, probe, amplitudes, strip_counts, row_offsets, col_offsets):
    block_cols = object_field.shape[1]
    strip_rows = object_field.shape[2]
    length = probe.shape[3]
    block_count = lax.axis_size("cols")
    strip_total = lax.axis_size("rows")
    cosine_table, sine_table = dft_tables(length)
    beside = shifted(object_field, "cols", -1)
    beside = vacuum_where(beside, lax.axis_index("cols") == block_count - 1)
    paired = jnp.concatenate([object_field, beside], axis=1)
    counts_all, rows_all, cols_all = (
        lax.all_gather(strip_counts, "rows", axis=0, tiled=True),
        lax.all_gather(row_offsets, "rows", axis=0, tiled=True),
        lax.all_gather(col_offsets, "rows", axis=0, tiled=True),
    )
    totals = jnp.cumsum(counts_all)
    starts = totals - counts_all
    position_block = (lax.axis_index("rows") + strip_total // 2) % strip_total
    my_positions = position_block * POS_AVG + jnp.arange(POS_AVG, dtype=jnp.int32)
    strip_of = jnp.sum((totals[None, :] <= my_positions[:, None]).astype(jnp.int32), axis=1)
    wanted = strip_of * POS_MAX + my_positions - jnp.take(starts, strip_of)
    first_rows = strip_of * strip_rows + jnp.take(rows_all, wanted)
    first_cols = jnp.take(cols_all, wanted)
    empty_frames = jnp.zeros((POS_AVG,) + amplitudes.shape[1:], jnp.float32)
    received = lax.all_gather(amplitudes, "rows", axis=0, tiled=True)
    inside = (wanted >= 0) & (wanted < received.shape[0])
    picked = jnp.take(received, jnp.clip(wanted, 0, received.shape[0] - 1), axis=0)
    frames = jnp.where(inside[:, None, None], picked, empty_frames)
    column_all = lax.all_gather(paired, "rows", axis=2, tiled=True)
    all_rows = column_all.shape[2]
    vacuum_tail = vacuum_where(jnp.zeros((2, column_all.shape[1], length), jnp.float32), True)
    window = jnp.concatenate([column_all, vacuum_tail], axis=2)
    window_grad, probe_sum = run_positions(
        window,
        probe,
        frames,
        first_rows,
        first_cols,
        POS_AVG,
        POS_AVG,
        cosine_table,
        sine_table,
        block_count,
    )
    folded = window_grad[:, :, :all_rows]
    summed = lax.psum_scatter(folded, "rows", scatter_dimension=2, tiled=True)
    upper_half = shifted(summed[:, block_cols:], "cols", 1)
    object_grad = summed[:, :block_cols] + upper_half
    probe_grad = lax.psum(probe_sum, "rows")
    return (object_grad, probe_grad)


def tables(length):
    indices = np.arange(length)
    angles = (indices[:, None] * indices[None, :] % length) * (2.0 * np.pi / length)
    scaling = 1.0 / length**0.5
    cosine, sine = np.cos(angles) * scaling, np.sin(angles) * scaling
    table = np.block([[cosine, -sine], [sine, cosine]])
    return jnp.asarray(table, jnp.bfloat16), jnp.asarray(table.T, jnp.bfloat16)


ANY = pl.BlockSpec(memory_space=pl.ANY)
WHOLE = pl.BlockSpec(memory_space=pltpu.VMEM)
LIMIT = 56 * 1024 * 1024
N = 4


def greet(axes):
    barrier = pltpu.get_barrier_semaphore()
    for axis in axes:
        me = lax.axis_index(axis)
        for k in range(1, N):
            pl.semaphore_signal(
                barrier, inc=1, device_id={axis: lax.rem(me + k, N)}, device_id_type=pl.DeviceIdType.MESH
            )
    pl.semaphore_wait(barrier, (N - 1) * len(axes))


def remote(src, dst, sems, slot, device):
    return pltpu.make_async_remote_copy(
        src_ref=src,
        dst_ref=dst,
        send_sem=sems.at[0, slot],
        recv_sem=sems.at[1, slot],
        device_id=device,
        device_id_type=pl.DeviceIdType.MESH,
    )


class Gather:
    def __init__(self, axis, src, out, sems, base, scatter=False):
        self.me = lax.axis_index(axis)
        self.axis, self.src, self.out, self.sems, self.base, self.scatter = axis, src, out, sems, base, scatter

    def piece(self, index):
        return self.src.at[index] if self.scatter else self.src

    def start(self):
        self.local = pltpu.make_async_copy(
            self.piece(self.me), self.out.at[self.me], self.sems.at[0, self.base]
        )
        self.sent = []
        for k in range(1, N):
            to = lax.rem(self.me + k, N)
            copy = remote(self.piece(to), self.out.at[self.me], self.sems, self.base + k, {self.axis: to})
            copy.start()
            self.sent.append(copy)
        self.local.start()

    def wait(self):
        self.local.wait()
        for k in range(1, N):
            source = lax.rem(self.me + N - k, N)
            remote(
                self.piece(source), self.out.at[source], self.sems, self.base + k, {self.axis: source}
            ).wait_recv()
        for copy in self.sent:
            copy.wait_send()


def spread_inputs(
    meta, cells, probe, frames, meta_out, probe_out, cells_out, frames_out,
    raw_probe, raw_frames, own_cells, own_probe, own_frames, sems, local
):
    bf16 = jnp.bfloat16
    row, col = lax.axis_index("rows"), lax.axis_index("cols")
    sibling = row + 1 - 2 * lax.rem(row, 2)
    across = lax.rem(row + 2, N)
    opposite = lax.rem(sibling + 2, N)
    right, left = lax.rem(col + 1, N), lax.rem(col + N - 1, N)
    load_probe = pltpu.make_async_copy(probe.at[row], raw_probe, local.at[0])
    load_frames = pltpu.make_async_copy(frames, raw_frames, local.at[1])
    load_probe.start()
    load_frames.start()
    own_cells[...] = cells[...].astype(bf16)
    greet(("rows", "cols"))

    def line_copy(base, src, dst, origin, rightward):
        return pltpu.make_async_remote_copy(
            src_ref=src,
            dst_ref=dst,
            send_sem=sems.at[0 if rightward else 2, base + origin],
            recv_sem=sems.at[1, base + origin],
            device_id={"cols": right if rightward else left},
            device_id_type=pl.DeviceIdType.MESH,
        )

    def line_start(base, src, dst, origin, rightward):
        @pl.when(col < N - 1 if rightward else col > 0)
        def _():
            line_copy(base, src, dst, origin, rightward).start()

    def line_sent(base, src, dst, origin, rightward):
        @pl.when(col < N - 1 if rightward else col > 0)
        def _():
            line_copy(base, src, dst, origin, rightward).wait_send()

    def cell(index, origin):
        return cells_out.at[index, origin]

    def row_copy(slot, src, dst, to):
        return remote(src, dst, sems, slot, {"rows": to})

    for rightward in (True, False):
        line_start(0, own_cells, cell(row, col), col, rightward)
    small = Gather("rows", meta, meta_out, sems, 8)
    small.start()
    row_copy(16 + col, own_cells, cell(row, col), across).start()
    row_copy(20 + col, own_cells, cell(row, col), sibling).start()
    keep_cells = pltpu.make_async_copy(own_cells, cell(row, col), local.at[2])
    keep_cells.start()
    load_probe.wait()
    own_probe[...] = raw_probe[...].astype(bf16)
    for rightward in (True, False):
        line_start(4, own_probe, probe_out.at[col], col, rightward)
    keep_probe = pltpu.make_async_copy(own_probe, probe_out.at[col], local.at[3])
    keep_probe.start()
    load_frames.wait()
    own_frames[...] = raw_frames[...].astype(bf16)
    keep_frames = pltpu.make_async_copy(own_frames, frames_out.at[row], local.at[4])

    @pl.when(row == col)
    def _():
        keep_frames.start()

    def frame_copy(k):
        return row_copy(12 + k, own_frames, frames_out.at[row], lax.rem(row + k, N))

    for k in range(1, N):

        @pl.when(lax.rem(row + k, N) == col)
        def _():
            frame_copy(k).start()

    def from_side(d, rightward):
        if rightward:
            return col >= d, lax.rem(col + N - d, N)
        return col + d < N, lax.rem(col + d, N)

    for d in range(1, N):
        for rightward in (True, False):
            here, origin = from_side(d, rightward)

            @pl.when(here)
            def _():
                mine = cell(row, origin)
                line_copy(0, mine, mine, origin, rightward).wait_recv()
                line_start(0, mine, mine, origin, rightward)
                row_copy(16 + origin, mine, mine, across).start()
                row_copy(20 + origin, mine, mine, sibling).start()

        for rightward in (True, False):
            here, origin = from_side(d, rightward)

            @pl.when(here)
            def _():
                mine = probe_out.at[origin]
                line_copy(4, mine, mine, origin, rightward).wait_recv()
                line_start(4, mine, mine, origin, rightward)

        if d == 1:
            landed = cell(across, col)
            row_copy(16 + col, landed, landed, across).wait_recv()
            row_copy(24 + col, landed, landed, sibling).start()
    for k in range(1, N):
        origin = lax.rem(col + k, N)
        landed = cell(across, origin)
        row_copy(16 + origin, landed, landed, across).wait_recv()
        row_copy(24 + origin, landed, landed, sibling).start()
    for origin in range(N):
        near, far = cell(sibling, origin), cell(opposite, origin)
        row_copy(20 + origin, near, near, sibling).wait_recv()
        row_copy(24 + origin, far, far, sibling).wait_recv()
    keep_cells.wait()
    keep_probe.wait()
    for rightward in (True, False):
        line_sent(0, own_cells, cell(row, col), col, rightward)
        line_sent(4, own_probe, probe_out.at[col], col, rightward)
        for d in range(1, N):
            here, origin = from_side(d, rightward)

            @pl.when(here)
            def _():
                line_sent(0, cell(row, origin), cell(row, origin), origin, rightward)
                line_sent(4, probe_out.at[origin], probe_out.at[origin], origin, rightward)

    for origin in range(N):
        mine, landed = cell(row, origin), cell(across, origin)
        row_copy(16 + origin, mine, mine, across).wait_send()
        row_copy(20 + origin, mine, mine, sibling).wait_send()
        row_copy(24 + origin, landed, landed, sibling).wait_send()
    small.wait()

    @pl.when(row == col)
    def _():
        keep_frames.wait()
        for k in range(1, N):
            source = lax.rem(row + N - k, N)
            row_copy(12 + k, own_frames, frames_out.at[source], source).wait_recv()

    for k in range(1, N):

        @pl.when(lax.rem(row + k, N) == col)
        def _():
            frame_copy(k).wait_send()


def propagate(
    patch, probe, frames, table, table_t, probe_out, terms_out,
    terms, field, power, near, relay, far, scale, measured, wide, tall, total, sems, local
):
    row, col = lax.axis_index("rows"), lax.axis_index("cols")
    sibling = row + 1 - 2 * lax.rem(row, 2)
    across = lax.rem(row + 2, N)
    opposite = lax.rem(sibling + 2, N)
    length = patch.shape[-1]
    quarter = length // N
    f32, bf16 = jnp.float32, jnp.bfloat16
    greet(("rows", "cols"))

    def frame_copy(to):
        return remote(frames.at[to], measured, sems, 18 + lax.rem(to + N - row, N), {"cols": to})

    local_frames = pltpu.make_async_copy(frames.at[col], measured, sems.at[0, 18])

    @pl.when(row == col)
    def _():
        local_frames.start()
        for k in range(1, N):
            frame_copy(lax.rem(col + k, N)).start()

    def near_copy(p, half):
        quarters = opposite if half else sibling
        return remote(power.at[p, quarters], near.at[p, half], sems, 2 * p + half, {"rows": sibling})

    def far_copy(p):
        return remote(relay.at[p], far.at[p], sems, 6 + p, {"rows": across})

    def scale_copy(p, kind, index):
        to = across if kind == 0 else sibling
        return remote(scale.at[p, index], scale.at[p, index], sems, 9 + 3 * kind + p, {"rows": to})

    def pass_on(p):
        near_copy(p, 1).wait_recv()
        relay[p] = (power[p, across].astype(f32) + near[p, 1].astype(f32)).astype(bf16)
        far_copy(p).start()

    def factors(p):
        near_copy(p, 0).wait_recv()
        far_copy(p).wait_recv()
        intensity = power[p, row].astype(f32) + near[p, 0].astype(f32) + far[p].astype(f32)
        amplitude = measured[p].astype(f32).T
        scale[p, row] = (1.0 - amplitude * lax.rsqrt(jnp.maximum(intensity, 0.25))).astype(bf16)
        scale_copy(p, 0, row).start()
        scale_copy(p, 1, row).start()

    def hand_over(p):
        scale_copy(p, 0, across).wait_recv()
        scale_copy(p, 2, across).start()

    def transform(p, carry):
        probe_real = probe[:, 0].reshape(length, length).astype(f32)
        probe_imag = probe[:, 1].reshape(length, length).astype(f32)
        patch_real = patch[p, 0].astype(f32)
        patch_imag = patch[p, 1].astype(f32)
        wide[:, :length] = (probe_real * patch_real - probe_imag * patch_imag).astype(bf16)
        wide[:, length:] = (probe_real * patch_imag + probe_imag * patch_real).astype(bf16)
        spread = mul(wide[...], table[...])
        tall[:length] = spread[:, :length].astype(bf16)
        tall[length:] = spread[:, length:].astype(bf16)
        result = mul(table_t[...], tall[...])
        field[p] = result
        square = result[:length] * result[:length] + result[length:] * result[length:]
        for q in range(N):
            power[p, q] = square[:, q * quarter : (q + 1) * quarter].astype(bf16)
        near_copy(p, 1).start()
        near_copy(p, 0).start()

        @pl.when(p >= 1)
        def _():
            pass_on(p - 1)

        return carry

    lax.fori_loop(0, POS_AVG, transform, 0)
    pass_on(POS_AVG - 1)

    @pl.when(row == col)
    def _():
        local_frames.wait()

    for k in range(1, N):

        @pl.when(lax.rem(row + k, N) == col)
        def _():
            remote(measured, measured, sems, 18 + k, {"cols": row}).wait_recv()

    for p in range(POS_AVG):
        factors(p)
        if p > 0:
            hand_over(p - 1)
    total[...] = jnp.zeros(total.shape, f32)

    def back_transform(p, carry):
        scale_copy(p, 1, sibling).wait_recv()
        scale_copy(p, 2, opposite).wait_recv()
        for q in range(N):
            lanes = pl.ds(q * quarter, quarter)
            gain = scale[p, q].astype(f32)
            tall[:length, lanes] = (field[p, :length, lanes] * gain).astype(bf16)
            tall[length:, lanes] = (field[p, length:, lanes] * gain).astype(bf16)
        inner = mul(table[...], tall[...])
        wide[:, :length] = inner[:length].astype(bf16)
        wide[:, length:] = inner[length:].astype(bf16)
        back = mul(wide[...], table_t[...])
        back_real, back_imag = back[:, :length], back[:, length:]
        probe_real = probe[:, 0].reshape(length, length).astype(f32)
        probe_imag = probe[:, 1].reshape(length, length).astype(f32)
        terms[p, 0] = probe_real * back_real + probe_imag * back_imag
        terms[p, 1] = probe_real * back_imag - probe_imag * back_real
        pltpu.make_async_copy(terms.at[p], terms_out.at[p], local.at[p]).start()
        patch_real = patch[p, 0].astype(f32)
        patch_imag = patch[p, 1].astype(f32)
        total[0] += patch_real * back_real + patch_imag * back_imag
        total[1] += patch_real * back_imag - patch_imag * back_real

        @pl.when(p == 0)
        def _():
            hand_over(POS_AVG - 1)

        return carry

    lax.fori_loop(0, POS_AVG, back_transform, 0)
    for b in range(N):
        for part in range(2):
            probe_out[b, part] = total[part, b * quarter : (b + 1) * quarter].astype(bf16)

    def finish(p, carry):
        near_copy(p, 0).wait_send()
        near_copy(p, 1).wait_send()
        far_copy(p).wait_send()
        scale_copy(p, 0, row).wait_send()
        scale_copy(p, 1, row).wait_send()
        scale_copy(p, 2, across).wait_send()
        pltpu.make_async_copy(terms.at[p], terms_out.at[p], local.at[p]).wait()
        return carry

    lax.fori_loop(0, POS_AVG, finish, 0)

    @pl.when(row == col)
    def _():
        for k in range(1, N):
            frame_copy(lax.rem(col + k, N)).wait_send()


def reduce_gradients(
    probe_part, cells_part, cells_out, probe_out, probe_in, near, far, relay, outgoing, cells_in, probe_all, sems
):
    f32, bf16 = jnp.float32, jnp.bfloat16
    row, col = lax.axis_index("rows"), lax.axis_index("cols")
    sibling = row + 1 - 2 * lax.rem(row, 2)
    across = lax.rem(row + 2, N)
    opposite = lax.rem(sibling + 2, N)
    greet(("rows", "cols"))

    def probe_copy(k):
        to = lax.rem(col + k, N)
        return remote(probe_part.at[to], probe_in.at[k - 1], sems, k - 1, {"cols": to})

    def near_copy(half, k):
        b = lax.rem(col + k, N)
        strip = opposite if half else sibling
        return remote(cells_part.at[strip, b], near.at[half, b], sems, 3 + 4 * half + k, {"rows": sibling})

    def far_copy(k):
        b = lax.rem(col + k, N)
        return remote(relay.at[b], far.at[b], sems, 11 + k, {"rows": across})

    def cells_copy(k):
        b = lax.rem(col + k, N)
        return remote(outgoing.at[b], cells_in.at[k - 1], sems, 14 + k, {"cols": b})

    def mode_copy(slot, index, to):
        return remote(probe_all.at[index], probe_all.at[index], sems, slot, {"rows": to})

    order = (1, 2, 3, 0)
    for k in range(1, N):
        probe_copy(k).start()
    for half in (1, 0):
        for k in order:
            near_copy(half, k).start()
    for k in order:
        b = lax.rem(col + k, N)
        near_copy(1, k).wait_recv()
        relay[b] = (cells_part[across, b].astype(f32) + near[1, b].astype(f32)).astype(bf16)
        far_copy(k).start()
    for k in order:
        b = lax.rem(col + k, N)
        near_copy(0, k).wait_recv()
        far_copy(k).wait_recv()
        total = cells_part[row, b].astype(f32) + near[0, b].astype(f32) + far[b].astype(f32)
        if k == 0:
            cells_out[...] = total
        else:
            outgoing[b] = total.astype(bf16)
            cells_copy(k).start()
    total = probe_part[col].astype(f32)
    for k in range(1, N):
        probe_copy(k).wait_recv()
        total += probe_in[k - 1].astype(f32)
    probe_all[row] = total.astype(bf16)
    sent = [mode_copy(18, row, across), mode_copy(19, row, sibling)]
    for copy in sent:
        copy.start()
    mode_copy(18, across, across).wait_recv()
    forwarded = mode_copy(20, across, sibling)
    forwarded.start()
    sent.append(forwarded)
    for k in range(1, N):
        cells_copy(k).wait_recv()
        cells_out[...] += cells_in[k - 1].astype(f32)
    mode_copy(19, sibling, sibling).wait_recv()
    mode_copy(20, opposite, sibling).wait_recv()
    probe_out[...] = probe_all[...].astype(f32)
    for copy in sent:
        copy.wait_send()
    for k in range(N):
        near_copy(0, k).wait_send()
        near_copy(1, k).wait_send()
        far_copy(k).wait_send()
        if k > 0:
            probe_copy(k).wait_send()
            cells_copy(k).wait_send()


def mul(left, right):
    return jnp.dot(left, right, preferred_element_type=jnp.float32)


def locate(meta, position, depth):
    strip, slot, start = 0, 0, 0
    for s in range(N):
        count = meta[s, 0, 0]
        inside = (position >= start) & (position < start + count)
        strip = jnp.where(inside, s, strip)
        slot = jnp.where(inside, position - start, slot)
        start = start + count
    return strip, slot, strip * depth + meta[strip, 0, 1 + slot], meta[strip, 0, 1 + POS_MAX + slot]


def iota(shape, axis):
    return lax.broadcasted_iota(jnp.int32, shape, axis)


def cut(meta, cells, frames_all, patch_out, frames_out, window, sems):
    p = pl.program_id(0)
    strips, blocks, _, width, depth = cells.shape
    length = patch_out.shape[-1]
    all_rows, all_cols = strips * depth, blocks * width

    def frame_copies():
        copies = []
        for i in range(POS_AVG * N):
            strip, slot, _, _ = locate(meta, i, depth)
            copies.append(
                pltpu.make_async_copy(
                    frames_all.at[strip, slot], frames_out.at[i // POS_AVG, i % POS_AVG], sems.at[i]
                )
            )
        return copies

    @pl.when(p == 0)
    def _():
        for copy in frame_copies():
            copy.start()
        for part, fill in ((0, 1.0), (1, 0.0)):
            window[part, all_cols:, :] = jnp.full((width, window.shape[2]), fill, jnp.float32)
            window[part, :all_cols, all_rows:] = jnp.full((all_cols, length), fill, jnp.float32)
            for s in range(strips):
                for b in range(blocks):
                    window[part, pl.ds(b * width, width), pl.ds(s * depth, depth)] = cells[s, b, part].astype(
                        jnp.float32
                    )

    _, _, first, column = locate(meta, lax.axis_index("cols") * POS_AVG + p, depth)
    rest = lax.rem(first, 128)
    base = first - rest
    low = lax.rem(column, 8)
    top = pl.multiple_of(column - low, 8)
    groups = length // 8
    for part in range(2):
        before = None
        for j in range(length // 128 + 1):
            block = window[part, pl.ds(top, length + 8), pl.ds(pl.multiple_of(base + 128 * j, 128), 128)]
            block = pltpu.roll(block.reshape(groups + 1, 8, 128), lax.rem(8 - low, 8), 1)
            block = jnp.where(iota((groups, 8, 128), 1) < 8 - low, block[:groups], block[1:])
            block = pltpu.roll(block.reshape(length, 128), lax.rem(128 - rest, 128), 1)
            if j > 0:
                joined = jnp.where(iota((length, 128), 1) < 128 - rest, before, block)
                patch_out[0, part, :, 128 * (j - 1) : 128 * j] = joined.astype(jnp.bfloat16)
            before = block

    @pl.when(p == pl.num_programs(0) - 1)
    def _():
        for copy in frame_copies():
            copy.wait()


def place(meta, terms, cells_out, window):
    p = pl.program_id(0)
    strips, blocks, _, width, depth = cells_out.shape
    length = terms.shape[-1]

    @pl.when(p == 0)
    def _():
        window[...] = jnp.zeros(window.shape, jnp.float32)

    _, _, first, column = locate(meta, lax.axis_index("cols") * POS_AVG + p, depth)
    rest = lax.rem(first, 128)
    base = first - rest
    low = lax.rem(column, 8)
    top = pl.multiple_of(column - low, 8)
    groups = length // 8
    edge = jnp.zeros((1, 8, 128), jnp.float32)
    for part in range(2):
        before = jnp.zeros((length + 8, 128), jnp.float32)
        for j in range(length // 128 + 1):
            if j < length // 128:
                block = terms[0, part, :, 128 * j : 128 * (j + 1)].reshape(groups, 8, 128)
                block = pltpu.roll(block, low, 1)
                above = jnp.concatenate([edge, block], axis=0)
                below = jnp.concatenate([block, edge], axis=0)
                block = jnp.where(iota((groups + 1, 8, 128), 1) < low, above, below)
                block = pltpu.roll(block.reshape(length + 8, 128), rest, 1)
            else:
                block = jnp.zeros((length + 8, 128), jnp.float32)
            joined = jnp.where(iota((length + 8, 128), 1) < rest, before, block)
            window[part, pl.ds(top, length + 8), pl.ds(pl.multiple_of(base + 128 * j, 128), 128)] += joined
            before = block

    @pl.when(p == pl.num_programs(0) - 1)
    def _():
        for part in range(2):
            for b in range(blocks):
                for s in range(strips):
                    cells_out[s, b, part] = window[part, pl.ds(b * width, width), pl.ds(s * depth, depth)].astype(
                        jnp.bfloat16
                    )


def balanced_device(object_field, probe, amplitudes, strip_counts, row_offsets, col_offsets):
    f32, bf16 = jnp.float32, jnp.bfloat16
    width, depth = object_field.shape[1:]
    length = probe.shape[3]
    row, col = lax.axis_index("rows"), lax.axis_index("cols")
    table, table_t = tables(length)
    meta = jnp.concatenate([strip_counts, row_offsets, col_offsets])
    meta = jnp.pad(meta, (0, 128 - meta.shape[0]))[None, :]
    mode_shape = probe.shape[1:]
    meta_all, mode_all, cells, frames_all = pl.pallas_call(
        spread_inputs,
        in_specs=[ANY, WHOLE, ANY, ANY],
        out_specs=[ANY] * 4,
        out_shape=[
            jax.ShapeDtypeStruct((N, 1, 128), jnp.int32),
            jax.ShapeDtypeStruct((N,) + mode_shape, bf16),
            jax.ShapeDtypeStruct((N, N) + object_field.shape, bf16),
            jax.ShapeDtypeStruct((N,) + amplitudes.shape, bf16),
        ],
        scratch_shapes=[
            pltpu.VMEM(mode_shape, f32),
            pltpu.VMEM(amplitudes.shape, f32),
            pltpu.VMEM(object_field.shape, bf16),
            pltpu.VMEM(mode_shape, bf16),
            pltpu.VMEM(amplitudes.shape, bf16),
            pltpu.SemaphoreType.DMA((3, 28)),
            pltpu.SemaphoreType.DMA((5,)),
        ],
        compiler_params=pltpu.CompilerParams(collective_id=1, has_side_effects=True, vmem_limit_bytes=LIMIT),
        name="spread_inputs",
    )(meta, object_field, probe, amplitudes)

    plane = (1, 2, length, length)
    whole = lambda *shape: pl.BlockSpec(shape, lambda p: (0,) * len(shape))
    per_slot = pl.BlockSpec(plane, lambda p: (p, 0, 0, 0))
    scalars = pl.BlockSpec(memory_space=pltpu.SMEM)
    window = pltpu.VMEM((2, N * width + 128, N * depth + length), f32)
    quarters = (POS_AVG, N, length, length // N)
    patch, frames = pl.pallas_call(
        cut,
        grid=(POS_AVG,),
        in_specs=[scalars, whole(*cells.shape), ANY],
        out_specs=[per_slot, whole(N, POS_AVG, *amplitudes.shape[1:])],
        scratch_shapes=[window, pltpu.SemaphoreType.DMA((POS_AVG * N,))],
        out_shape=[
            jax.ShapeDtypeStruct((POS_AVG,) + plane[1:], bf16),
            jax.ShapeDtypeStruct((N, POS_AVG) + amplitudes.shape[1:], bf16),
        ],
        compiler_params=pltpu.CompilerParams(vmem_limit_bytes=LIMIT),
        name="cut",
    )(meta_all, cells, frames_all)
    probe_part, terms = pl.pallas_call(
        propagate,
        in_specs=[WHOLE, WHOLE, ANY, WHOLE, WHOLE],
        out_specs=[WHOLE, ANY],
        out_shape=[
            jax.ShapeDtypeStruct(mode_all.shape, bf16),
            jax.ShapeDtypeStruct((POS_AVG,) + plane[1:], f32),
        ],
        scratch_shapes=[
            pltpu.VMEM((POS_AVG,) + plane[1:], f32),
            pltpu.VMEM((POS_AVG, 2 * length, length), f32),
            pltpu.VMEM(quarters, bf16),
            pltpu.VMEM((POS_AVG, 2) + quarters[2:], bf16),
            pltpu.VMEM((POS_AVG,) + quarters[2:], bf16),
            pltpu.VMEM((POS_AVG,) + quarters[2:], bf16),
            pltpu.VMEM(quarters, bf16),
            pltpu.VMEM(frames.shape[1:], bf16),
            pltpu.VMEM((length, 2 * length), bf16),
            pltpu.VMEM((2 * length, length), bf16),
            pltpu.VMEM((2, length, length), f32),
            pltpu.SemaphoreType.DMA((2, 22)),
            pltpu.SemaphoreType.DMA((POS_AVG,)),
        ],
        compiler_params=pltpu.CompilerParams(collective_id=2, has_side_effects=True, vmem_limit_bytes=LIMIT),
        name="propagate",
    )(patch, mode_all, frames, table, table_t)
    cells_part = pl.pallas_call(
        place,
        grid=(POS_AVG,),
        in_specs=[scalars, per_slot],
        out_specs=whole(*cells.shape),
        scratch_shapes=[window],
        out_shape=jax.ShapeDtypeStruct(cells.shape, bf16),
        compiler_params=pltpu.CompilerParams(vmem_limit_bytes=LIMIT),
        name="place",
    )(meta_all, terms)
    strip = (N,) + object_field.shape
    object_grad, probe_grad = pl.pallas_call(
        reduce_gradients,
        in_specs=[WHOLE, WHOLE],
        out_specs=[WHOLE, WHOLE],
        out_shape=[jax.ShapeDtypeStruct(object_field.shape, f32), jax.ShapeDtypeStruct(probe.shape, f32)],
        scratch_shapes=[
            pltpu.VMEM((N - 1,) + mode_shape, bf16),
            pltpu.VMEM((2,) + strip, bf16),
            pltpu.VMEM(strip, bf16),
            pltpu.VMEM(strip, bf16),
            pltpu.VMEM(strip, bf16),
            pltpu.VMEM((N - 1,) + object_field.shape, bf16),
            pltpu.VMEM((N,) + mode_shape, bf16),
            pltpu.SemaphoreType.DMA((2, 21)),
        ],
        compiler_params=pltpu.CompilerParams(collective_id=3, has_side_effects=True, vmem_limit_bytes=LIMIT),
        name="reduce_gradients",
    )(probe_part, cells_part)
    return object_grad, probe_grad


def solution(mesh):
    on_device = balanced_device if mesh.shape["rows"] == N and mesh.shape["cols"] == N else general_device
    placed = (
        P("groups", "cols", "rows"),
        P("groups", None, "cols", None),
        P(("groups", "rows"), "cols", None),
        P(("groups", "rows")),
        P(("groups", "rows")),
        P(("groups", "rows")),
    )
    return jax.shard_map(
        on_device,
        mesh=mesh,
        in_specs=placed,
        out_specs=(P("groups", "cols", "rows"), P("groups", None, "cols", None)),
        check_vma=False,
    )
```

```python
import jax
import jax.numpy as jnp
import numpy as np
from jax import lax
from jax.experimental import pallas as pl
from jax.experimental.pallas import tpu as pltpu
from jax.sharding import PartitionSpec as P

POS_AVG = 3
POS_MAX = 6


def shifted(block, axis, distance):
    devices = range(lax.axis_size(axis))
    route = [(i - distance, i) for i in devices if i - distance in devices]
    return lax.ppermute(block, axis, route)


def dft_tables(length):
    indices = jnp.arange(length, dtype=jnp.int32)
    product = indices[:, None] * indices[None, :] % length
    angles = product.astype(jnp.float32) * jnp.float32(2.0 * 3.141592653589793 / length)
    scaling = jnp.float32(1.0 / length**0.5)
    cosine_table = (jnp.cos(angles) * scaling).astype(jnp.bfloat16)
    sine_table = (jnp.sin(angles) * scaling).astype(jnp.bfloat16)
    return (cosine_table, sine_table)


def leading(values, matrix):
    return jnp.einsum("mca,asu->mscu", values, matrix, preferred_element_type=jnp.float32)


def second(values, matrix):
    return jnp.einsum("mscu,scv->muv", values, matrix, preferred_element_type=jnp.float32)


def third(values, matrix):
    return jnp.einsum("muv,vsb->msub", values, matrix, preferred_element_type=jnp.float32)


def fourth(values, matrix):
    return jnp.einsum("msub,sua->mba", values, matrix, preferred_element_type=jnp.float32)


def vacuum_where(block, outside):
    fill_real = jnp.where(outside, jnp.float32(1.0), block[0])
    fill_imag = jnp.where(outside, jnp.float32(0.0), block[1])
    return jnp.stack([fill_real, fill_imag])


def spectral_pass(patch_cells, probe, measured, cosine_table, sine_table, block_count):
    mode_count = probe.shape[0]
    block_cols = patch_cells.shape[1]
    length = patch_cells.shape[2]
    block_freq = length // block_count
    probe_real = probe[:, 0]
    probe_imag = probe[:, 1]
    patch_real = patch_cells[0]
    patch_imag = patch_cells[1]
    wave_real = (probe_real * patch_real - probe_imag * patch_imag).astype(jnp.bfloat16)
    wave_imag = (probe_real * patch_imag + probe_imag * patch_real).astype(jnp.bfloat16)
    cos_lead = cosine_table.reshape(length, block_count, block_freq)
    sin_lead = sine_table.reshape(length, block_count, block_freq)
    first_real = leading(wave_real, cos_lead) + leading(wave_imag, sin_lead)
    first_imag = leading(wave_imag, cos_lead) - leading(wave_real, sin_lead)
    outgoing = jnp.stack([first_real, first_imag], axis=1).astype(jnp.bfloat16)
    outgoing = outgoing.reshape(mode_count, 2, block_count, block_cols * block_freq)
    arrived = lax.all_to_all(outgoing, "cols", split_axis=2, concat_axis=2, tiled=True)
    arrived = arrived.reshape(mode_count, 2, block_count, block_cols, block_freq)
    cos_rows = cosine_table.reshape(block_count, block_cols, length)
    sin_rows = sine_table.reshape(block_count, block_cols, length)
    field_real = second(arrived[:, 0], cos_rows) + second(arrived[:, 1], sin_rows)
    field_imag = second(arrived[:, 1], cos_rows) - second(arrived[:, 0], sin_rows)
    intensity = jnp.sum(field_real * field_real + field_imag * field_imag, axis=0)
    modulus = jnp.sqrt(jnp.maximum(intensity, 0.25))
    factor = 1.0 - measured / modulus
    back_real = (field_real * factor).astype(jnp.bfloat16)
    back_imag = (field_imag * factor).astype(jnp.bfloat16)
    cos_back = cosine_table.reshape(length, block_count, block_cols)
    sin_back = sine_table.reshape(length, block_count, block_cols)
    inner_real = third(back_real, cos_back) - third(back_imag, sin_back)
    inner_imag = third(back_imag, cos_back) + third(back_real, sin_back)
    returning = jnp.stack([inner_real, inner_imag], axis=1).astype(jnp.bfloat16)
    returning = returning.reshape(mode_count, 2, block_count, block_freq * block_cols)
    landed = lax.all_to_all(returning, "cols", split_axis=2, concat_axis=2, tiled=True)
    landed = landed.reshape(mode_count, 2, block_count, block_freq, block_cols)
    cos_freq = cosine_table.reshape(block_count, block_freq, length)
    sin_freq = sine_table.reshape(block_count, block_freq, length)
    grad_real = fourth(landed[:, 0], cos_freq) - fourth(landed[:, 1], sin_freq)
    grad_imag = fourth(landed[:, 1], cos_freq) + fourth(landed[:, 0], sin_freq)
    object_real = jnp.sum(probe_real * grad_real + probe_imag * grad_imag, axis=0)
    object_imag = jnp.sum(probe_real * grad_imag - probe_imag * grad_real, axis=0)
    probe_real_term = patch_real * grad_real + patch_imag * grad_imag
    probe_imag_term = patch_real * grad_imag - patch_imag * grad_real
    return (
        jnp.stack([object_real, object_imag]),
        jnp.stack([probe_real_term, probe_imag_term], axis=1),
    )


def run_positions(
    window,
    probe,
    frames,
    first_rows,
    first_cols,
    slot_total,
    used_count,
    cosine_table,
    sine_table,
    block_count,
):
    block_cols = probe.shape[2]
    length = probe.shape[3]

    def visit_slot(slot_index, state_pair):
        window_grad, probe_sum = state_pair
        first_row = first_rows[slot_index]
        first_col = first_cols[slot_index]
        patch_cells = lax.dynamic_slice(window, (0, first_col, first_row), (2, block_cols, length))
        measured = lax.dynamic_index_in_dim(frames, slot_index, 0, keepdims=False)
        object_term, probe_term = spectral_pass(
            patch_cells, probe, measured, cosine_table, sine_table, block_count
        )
        active = (slot_index < used_count).astype(jnp.float32)
        current = lax.dynamic_slice(window_grad, (0, first_col, first_row), (2, block_cols, length))
        window_grad = lax.dynamic_update_slice(
            window_grad, current + active * object_term, (0, first_col, first_row)
        )
        return (window_grad, probe_sum + active * probe_term)

    initial = (jnp.zeros(window.shape, jnp.float32), jnp.zeros(probe.shape, jnp.float32))
    return lax.fori_loop(0, slot_total, visit_slot, initial)


def general_device(object_field, probe, amplitudes, strip_counts, row_offsets, col_offsets):
    block_cols = object_field.shape[1]
    strip_rows = object_field.shape[2]
    length = probe.shape[3]
    block_count = lax.axis_size("cols")
    strip_total = lax.axis_size("rows")
    cosine_table, sine_table = dft_tables(length)
    beside = shifted(object_field, "cols", -1)
    beside = vacuum_where(beside, lax.axis_index("cols") == block_count - 1)
    paired = jnp.concatenate([object_field, beside], axis=1)
    counts_all, rows_all, cols_all = (
        lax.all_gather(strip_counts, "rows", axis=0, tiled=True),
        lax.all_gather(row_offsets, "rows", axis=0, tiled=True),
        lax.all_gather(col_offsets, "rows", axis=0, tiled=True),
    )
    totals = jnp.cumsum(counts_all)
    starts = totals - counts_all
    position_block = (lax.axis_index("rows") + strip_total // 2) % strip_total
    my_positions = position_block * POS_AVG + jnp.arange(POS_AVG, dtype=jnp.int32)
    strip_of = jnp.sum((totals[None, :] <= my_positions[:, None]).astype(jnp.int32), axis=1)
    wanted = strip_of * POS_MAX + my_positions - jnp.take(starts, strip_of)
    first_rows = strip_of * strip_rows + jnp.take(rows_all, wanted)
    first_cols = jnp.take(cols_all, wanted)
    empty_frames = jnp.zeros((POS_AVG,) + amplitudes.shape[1:], jnp.float32)
    received = lax.all_gather(amplitudes, "rows", axis=0, tiled=True)
    inside = (wanted >= 0) & (wanted < received.shape[0])
    picked = jnp.take(received, jnp.clip(wanted, 0, received.shape[0] - 1), axis=0)
    frames = jnp.where(inside[:, None, None], picked, empty_frames)
    column_all = lax.all_gather(paired, "rows", axis=2, tiled=True)
    all_rows = column_all.shape[2]
    vacuum_tail = vacuum_where(jnp.zeros((2, column_all.shape[1], length), jnp.float32), True)
    window = jnp.concatenate([column_all, vacuum_tail], axis=2)
    window_grad, probe_sum = run_positions(
        window,
        probe,
        frames,
        first_rows,
        first_cols,
        POS_AVG,
        POS_AVG,
        cosine_table,
        sine_table,
        block_count,
    )
    folded = window_grad[:, :, :all_rows]
    summed = lax.psum_scatter(folded, "rows", scatter_dimension=2, tiled=True)
    upper_half = shifted(summed[:, block_cols:], "cols", 1)
    object_grad = summed[:, :block_cols] + upper_half
    probe_grad = lax.psum(probe_sum, "rows")
    return (object_grad, probe_grad)


def tables(length):
    indices = np.arange(length)
    angles = (indices[:, None] * indices[None, :] % length) * (2.0 * np.pi / length)
    scaling = 1.0 / length**0.5
    cosine, sine = np.cos(angles) * scaling, np.sin(angles) * scaling
    table = np.block([[cosine, -sine], [sine, cosine]])
    return jnp.asarray(table, jnp.bfloat16), jnp.asarray(table.T, jnp.bfloat16)


ANY = pl.BlockSpec(memory_space=pl.ANY)
WHOLE = pl.BlockSpec(memory_space=pltpu.VMEM)
LIMIT = 56 * 1024 * 1024
N = 4


def greet(axes):
    barrier = pltpu.get_barrier_semaphore()
    for axis in axes:
        me = lax.axis_index(axis)
        for k in range(1, N):
            pl.semaphore_signal(
                barrier, inc=1, device_id={axis: lax.rem(me + k, N)}, device_id_type=pl.DeviceIdType.MESH
            )
    pl.semaphore_wait(barrier, (N - 1) * len(axes))


def remote(src, dst, sems, slot, device):
    return pltpu.make_async_remote_copy(
        src_ref=src,
        dst_ref=dst,
        send_sem=sems.at[0, slot],
        recv_sem=sems.at[1, slot],
        device_id=device,
        device_id_type=pl.DeviceIdType.MESH,
    )


class Gather:
    def __init__(self, axis, src, out, sems, base, scatter=False):
        self.me = lax.axis_index(axis)
        self.axis, self.src, self.out, self.sems, self.base, self.scatter = axis, src, out, sems, base, scatter

    def piece(self, index):
        return self.src.at[index] if self.scatter else self.src

    def start(self):
        self.local = pltpu.make_async_copy(
            self.piece(self.me), self.out.at[self.me], self.sems.at[0, self.base]
        )
        self.sent = []
        for k in range(1, N):
            to = lax.rem(self.me + k, N)
            copy = remote(self.piece(to), self.out.at[self.me], self.sems, self.base + k, {self.axis: to})
            copy.start()
            self.sent.append(copy)
        self.local.start()

    def wait(self):
        self.local.wait()
        for k in range(1, N):
            source = lax.rem(self.me + N - k, N)
            remote(
                self.piece(source), self.out.at[source], self.sems, self.base + k, {self.axis: source}
            ).wait_recv()
        for copy in self.sent:
            copy.wait_send()


def spread_inputs(
    meta, cells, probe, frames, meta_out, probe_out, cells_out, frames_out,
    raw_probe, raw_frames, own_cells, own_probe, own_frames, sems, local
):
    bf16 = jnp.bfloat16
    row, col = lax.axis_index("rows"), lax.axis_index("cols")
    sibling = row + 1 - 2 * lax.rem(row, 2)
    across = lax.rem(row + 2, N)
    opposite = lax.rem(sibling + 2, N)
    right, left = lax.rem(col + 1, N), lax.rem(col + N - 1, N)
    load_probe = pltpu.make_async_copy(probe.at[row], raw_probe, local.at[0])
    load_frames = pltpu.make_async_copy(frames, raw_frames, local.at[1])
    load_probe.start()
    load_frames.start()
    own_cells[...] = cells[...].astype(bf16)
    greet(("rows", "cols"))

    def line_copy(base, src, dst, origin, rightward):
        return pltpu.make_async_remote_copy(
            src_ref=src,
            dst_ref=dst,
            send_sem=sems.at[0 if rightward else 2, base + origin],
            recv_sem=sems.at[1, base + origin],
            device_id={"cols": right if rightward else left},
            device_id_type=pl.DeviceIdType.MESH,
        )

    def line_start(base, src, dst, origin, rightward):
        @pl.when(col < N - 1 if rightward else col > 0)
        def _():
            line_copy(base, src, dst, origin, rightward).start()

    def line_sent(base, src, dst, origin, rightward):
        @pl.when(col < N - 1 if rightward else col > 0)
        def _():
            line_copy(base, src, dst, origin, rightward).wait_send()

    def cell(index, origin):
        return cells_out.at[index, origin]

    def row_copy(slot, src, dst, to):
        return remote(src, dst, sems, slot, {"rows": to})

    for rightward in (True, False):
        line_start(0, own_cells, cell(row, col), col, rightward)
    small = Gather("rows", meta, meta_out, sems, 8)
    small.start()
    row_copy(16 + col, own_cells, cell(row, col), across).start()
    row_copy(20 + col, own_cells, cell(row, col), sibling).start()
    keep_cells = pltpu.make_async_copy(own_cells, cell(row, col), local.at[2])
    keep_cells.start()
    load_probe.wait()
    own_probe[...] = raw_probe[...].astype(bf16)
    for rightward in (True, False):
        line_start(4, own_probe, probe_out.at[col], col, rightward)
    keep_probe = pltpu.make_async_copy(own_probe, probe_out.at[col], local.at[3])
    keep_probe.start()
    load_frames.wait()
    own_frames[...] = raw_frames[...].astype(bf16)
    keep_frames = pltpu.make_async_copy(own_frames, frames_out.at[row], local.at[4])

    @pl.when(row == col)
    def _():
        keep_frames.start()

    def frame_copy(k):
        return row_copy(12 + k, own_frames, frames_out.at[row], lax.rem(row + k, N))

    for k in range(1, N):

        @pl.when(lax.rem(row + k, N) == col)
        def _():
            frame_copy(k).start()

    def from_side(d, rightward):
        if rightward:
            return col >= d, lax.rem(col + N - d, N)
        return col + d < N, lax.rem(col + d, N)

    for d in range(1, N):
        for rightward in (True, False):
            here, origin = from_side(d, rightward)

            @pl.when(here)
            def _():
                mine = cell(row, origin)
                line_copy(0, mine, mine, origin, rightward).wait_recv()
                line_start(0, mine, mine, origin, rightward)
                row_copy(16 + origin, mine, mine, across).start()
                row_copy(20 + origin, mine, mine, sibling).start()

        for rightward in (True, False):
            here, origin = from_side(d, rightward)

            @pl.when(here)
            def _():
                mine = probe_out.at[origin]
                line_copy(4, mine, mine, origin, rightward).wait_recv()
                line_start(4, mine, mine, origin, rightward)

        if d == 1:
            landed = cell(across, col)
            row_copy(16 + col, landed, landed, across).wait_recv()
            row_copy(24 + col, landed, landed, sibling).start()
    for k in range(1, N):
        origin = lax.rem(col + k, N)
        landed = cell(across, origin)
        row_copy(16 + origin, landed, landed, across).wait_recv()
        row_copy(24 + origin, landed, landed, sibling).start()
    for origin in range(N):
        near, far = cell(sibling, origin), cell(opposite, origin)
        row_copy(20 + origin, near, near, sibling).wait_recv()
        row_copy(24 + origin, far, far, sibling).wait_recv()
    keep_cells.wait()
    keep_probe.wait()
    for rightward in (True, False):
        line_sent(0, own_cells, cell(row, col), col, rightward)
        line_sent(4, own_probe, probe_out.at[col], col, rightward)
        for d in range(1, N):
            here, origin = from_side(d, rightward)

            @pl.when(here)
            def _():
                line_sent(0, cell(row, origin), cell(row, origin), origin, rightward)
                line_sent(4, probe_out.at[origin], probe_out.at[origin], origin, rightward)

    for origin in range(N):
        mine, landed = cell(row, origin), cell(across, origin)
        row_copy(16 + origin, mine, mine, across).wait_send()
        row_copy(20 + origin, mine, mine, sibling).wait_send()
        row_copy(24 + origin, landed, landed, sibling).wait_send()
    small.wait()

    @pl.when(row == col)
    def _():
        keep_frames.wait()
        for k in range(1, N):
            source = lax.rem(row + N - k, N)
            row_copy(12 + k, own_frames, frames_out.at[source], source).wait_recv()

    for k in range(1, N):

        @pl.when(lax.rem(row + k, N) == col)
        def _():
            frame_copy(k).wait_send()


def propagate(
    patch_in, probe_in, frames, table_in, table_t_in, probe_out, terms_out,
    patch, probe, table, table_t, terms, field, power, near, relay, far, scale, measured, wide, tall, total, sems, local
):
    row, col = lax.axis_index("rows"), lax.axis_index("cols")
    sibling = row + 1 - 2 * lax.rem(row, 2)
    across = lax.rem(row + 2, N)
    opposite = lax.rem(sibling + 2, N)
    length = patch.shape[-1]
    quarter = length // N
    f32, bf16 = jnp.float32, jnp.bfloat16
    sources = (probe_in, patch_in, table_in, table_t_in)
    loads = [
        pltpu.make_async_copy(src, dst, local.at[POS_AVG + i])
        for i, (src, dst) in enumerate(zip(sources, (probe, patch, table, table_t)))
    ]
    for load in loads:
        load.start()
    greet(("rows", "cols"))

    def frame_copy(to):
        return remote(frames.at[to], measured, sems, 18 + lax.rem(to + N - row, N), {"cols": to})

    local_frames = pltpu.make_async_copy(frames.at[col], measured, sems.at[0, 18])

    @pl.when(row == col)
    def _():
        local_frames.start()
        for k in range(1, N):
            frame_copy(lax.rem(col + k, N)).start()

    def near_copy(p, half):
        quarters = opposite if half else sibling
        return remote(power.at[p, quarters], near.at[p, half], sems, 2 * p + half, {"rows": sibling})

    def far_copy(p):
        return remote(relay.at[p], far.at[p], sems, 6 + p, {"rows": across})

    def scale_copy(p, kind, index):
        to = across if kind == 0 else sibling
        return remote(scale.at[p, index], scale.at[p, index], sems, 9 + 3 * kind + p, {"rows": to})

    def pass_on(p):
        near_copy(p, 1).wait_recv()
        relay[p] = (power[p, across].astype(f32) + near[p, 1].astype(f32)).astype(bf16)
        far_copy(p).start()

    def factors(p):
        near_copy(p, 0).wait_recv()
        far_copy(p).wait_recv()
        intensity = power[p, row].astype(f32) + near[p, 0].astype(f32) + far[p].astype(f32)
        amplitude = measured[p].astype(f32).T
        scale[p, row] = (1.0 - amplitude * lax.rsqrt(jnp.maximum(intensity, 0.25))).astype(bf16)
        scale_copy(p, 0, row).start()
        scale_copy(p, 1, row).start()

    def hand_over(p):
        scale_copy(p, 0, across).wait_recv()
        scale_copy(p, 2, across).start()

    def transform(p, carry):
        probe_real = probe[:, 0].reshape(length, length).astype(f32)
        probe_imag = probe[:, 1].reshape(length, length).astype(f32)
        patch_real = patch[p, 0].astype(f32)
        patch_imag = patch[p, 1].astype(f32)
        wide[:, :length] = (probe_real * patch_real - probe_imag * patch_imag).astype(bf16)
        wide[:, length:] = (probe_real * patch_imag + probe_imag * patch_real).astype(bf16)
        spread = mul(wide[...], table[...])
        tall[:length] = spread[:, :length].astype(bf16)
        tall[length:] = spread[:, length:].astype(bf16)
        result = mul(table_t[...], tall[...])
        field[p] = result
        square = result[:length] * result[:length] + result[length:] * result[length:]
        for q in range(N):
            power[p, q] = square[:, q * quarter : (q + 1) * quarter].astype(bf16)
        near_copy(p, 1).start()
        near_copy(p, 0).start()

        @pl.when(p >= 1)
        def _():
            pass_on(p - 1)

        return carry

    for load in loads:
        load.wait()
    lax.fori_loop(0, POS_AVG, transform, 0)
    pass_on(POS_AVG - 1)

    @pl.when(row == col)
    def _():
        local_frames.wait()

    for k in range(1, N):

        @pl.when(lax.rem(row + k, N) == col)
        def _():
            remote(measured, measured, sems, 18 + k, {"cols": row}).wait_recv()

    for p in range(POS_AVG):
        factors(p)
        if p > 0:
            hand_over(p - 1)
    total[...] = jnp.zeros(total.shape, f32)

    def back_transform(p, carry):
        scale_copy(p, 1, sibling).wait_recv()
        scale_copy(p, 2, opposite).wait_recv()
        for q in range(N):
            lanes = pl.ds(q * quarter, quarter)
            gain = scale[p, q].astype(f32)
            tall[:length, lanes] = (field[p, :length, lanes] * gain).astype(bf16)
            tall[length:, lanes] = (field[p, length:, lanes] * gain).astype(bf16)
        inner = mul(table[...], tall[...])
        wide[:, :length] = inner[:length].astype(bf16)
        wide[:, length:] = inner[length:].astype(bf16)
        back = mul(wide[...], table_t[...])
        back_real, back_imag = back[:, :length], back[:, length:]
        probe_real = probe[:, 0].reshape(length, length).astype(f32)
        probe_imag = probe[:, 1].reshape(length, length).astype(f32)
        terms[p, 0] = probe_real * back_real + probe_imag * back_imag
        terms[p, 1] = probe_real * back_imag - probe_imag * back_real
        pltpu.make_async_copy(terms.at[p], terms_out.at[p], local.at[p]).start()
        patch_real = patch[p, 0].astype(f32)
        patch_imag = patch[p, 1].astype(f32)
        total[0] += patch_real * back_real + patch_imag * back_imag
        total[1] += patch_real * back_imag - patch_imag * back_real

        @pl.when(p == 0)
        def _():
            hand_over(POS_AVG - 1)

        return carry

    lax.fori_loop(0, POS_AVG, back_transform, 0)
    for b in range(N):
        for part in range(2):
            probe_out[b, part] = total[part, b * quarter : (b + 1) * quarter].astype(bf16)

    def finish(p, carry):
        near_copy(p, 0).wait_send()
        near_copy(p, 1).wait_send()
        far_copy(p).wait_send()
        scale_copy(p, 0, row).wait_send()
        scale_copy(p, 1, row).wait_send()
        scale_copy(p, 2, across).wait_send()
        pltpu.make_async_copy(terms.at[p], terms_out.at[p], local.at[p]).wait()
        return carry

    lax.fori_loop(0, POS_AVG, finish, 0)

    @pl.when(row == col)
    def _():
        for k in range(1, N):
            frame_copy(lax.rem(col + k, N)).wait_send()


def reduce_gradients(
    probe_part, cells_part, cells_out, probe_all, probe_in, near, far, relay, outgoing, cells_in, sems
):
    f32, bf16 = jnp.float32, jnp.bfloat16
    row, col = lax.axis_index("rows"), lax.axis_index("cols")
    sibling = row + 1 - 2 * lax.rem(row, 2)
    across = lax.rem(row + 2, N)
    opposite = lax.rem(sibling + 2, N)
    greet(("rows", "cols"))

    def probe_copy(k):
        to = lax.rem(col + k, N)
        return remote(probe_part.at[to], probe_in.at[k - 1], sems, k - 1, {"cols": to})

    def near_copy(half, k):
        b = lax.rem(col + k, N)
        strip = opposite if half else sibling
        return remote(cells_part.at[strip, b], near.at[half, b], sems, 3 + 4 * half + k, {"rows": sibling})

    def far_copy(k):
        b = lax.rem(col + k, N)
        return remote(relay.at[b], far.at[b], sems, 11 + k, {"rows": across})

    def cells_copy(k):
        b = lax.rem(col + k, N)
        return remote(outgoing.at[b], cells_in.at[k - 1], sems, 14 + k, {"cols": b})

    def mode_copy(slot, index, to):
        return remote(probe_all.at[index], probe_all.at[index], sems, slot, {"rows": to})

    order = (1, 2, 3, 0)
    for k in range(1, N):
        probe_copy(k).start()
    for half in (1, 0):
        for k in order:
            near_copy(half, k).start()
    for k in order:
        b = lax.rem(col + k, N)
        near_copy(1, k).wait_recv()
        relay[b] = (cells_part[across, b].astype(f32) + near[1, b].astype(f32)).astype(bf16)
        far_copy(k).start()
    for k in order:
        b = lax.rem(col + k, N)
        near_copy(0, k).wait_recv()
        far_copy(k).wait_recv()
        total = cells_part[row, b].astype(f32) + near[0, b].astype(f32) + far[b].astype(f32)
        if k == 0:
            cells_out[...] = total
        else:
            outgoing[b] = total.astype(bf16)
            cells_copy(k).start()
    total = probe_part[col].astype(f32)
    for k in range(1, N):
        probe_copy(k).wait_recv()
        total += probe_in[k - 1].astype(f32)
    probe_all[row] = total.astype(bf16)
    sent = [mode_copy(18, row, across), mode_copy(19, row, sibling)]
    for copy in sent:
        copy.start()
    mode_copy(18, across, across).wait_recv()
    forwarded = mode_copy(20, across, sibling)
    forwarded.start()
    sent.append(forwarded)
    for k in range(1, N):
        cells_copy(k).wait_recv()
        cells_out[...] += cells_in[k - 1].astype(f32)
    mode_copy(19, sibling, sibling).wait_recv()
    mode_copy(20, opposite, sibling).wait_recv()
    for copy in sent:
        copy.wait_send()
    for k in range(N):
        near_copy(0, k).wait_send()
        near_copy(1, k).wait_send()
        far_copy(k).wait_send()
        if k > 0:
            probe_copy(k).wait_send()
            cells_copy(k).wait_send()


def mul(left, right):
    return jnp.dot(left, right, preferred_element_type=jnp.float32)


def locate(meta, position, depth):
    strip, slot, start = 0, 0, 0
    for s in range(N):
        count = meta[s, 0, 0]
        inside = (position >= start) & (position < start + count)
        strip = jnp.where(inside, s, strip)
        slot = jnp.where(inside, position - start, slot)
        start = start + count
    return strip, slot, strip * depth + meta[strip, 0, 1 + slot], meta[strip, 0, 1 + POS_MAX + slot]


def iota(shape, axis):
    return lax.broadcasted_iota(jnp.int32, shape, axis)


def cut(meta, cells, frames_all, patch_out, frames_out, window, sems):
    p = pl.program_id(0)
    strips, blocks, _, width, depth = cells.shape
    length = patch_out.shape[-1]
    all_rows, all_cols = strips * depth, blocks * width

    def frame_copies():
        copies = []
        for i in range(POS_AVG * N):
            strip, slot, _, _ = locate(meta, i, depth)
            copies.append(
                pltpu.make_async_copy(
                    frames_all.at[strip, slot], frames_out.at[i // POS_AVG, i % POS_AVG], sems.at[i]
                )
            )
        return copies

    @pl.when(p == 0)
    def _():
        for copy in frame_copies():
            copy.start()
        for part, fill in ((0, 1.0), (1, 0.0)):
            window[part, all_cols:, :] = jnp.full((width, window.shape[2]), fill, jnp.float32)
            window[part, :all_cols, all_rows:] = jnp.full((all_cols, length), fill, jnp.float32)
            for s in range(strips):
                for b in range(blocks):
                    window[part, pl.ds(b * width, width), pl.ds(s * depth, depth)] = cells[s, b, part].astype(
                        jnp.float32
                    )

    _, _, first, column = locate(meta, lax.axis_index("cols") * POS_AVG + p, depth)
    rest = lax.rem(first, 128)
    base = first - rest
    low = lax.rem(column, 8)
    top = pl.multiple_of(column - low, 8)
    groups = length // 8
    for part in range(2):
        before = None
        for j in range(length // 128 + 1):
            block = window[part, pl.ds(top, length + 8), pl.ds(pl.multiple_of(base + 128 * j, 128), 128)]
            block = pltpu.roll(block.reshape(groups + 1, 8, 128), lax.rem(8 - low, 8), 1)
            block = jnp.where(iota((groups, 8, 128), 1) < 8 - low, block[:groups], block[1:])
            block = pltpu.roll(block.reshape(length, 128), lax.rem(128 - rest, 128), 1)
            if j > 0:
                joined = jnp.where(iota((length, 128), 1) < 128 - rest, before, block)
                patch_out[0, part, :, 128 * (j - 1) : 128 * j] = joined.astype(jnp.bfloat16)
            before = block

    @pl.when(p == pl.num_programs(0) - 1)
    def _():
        for copy in frame_copies():
            copy.wait()


def place(meta, terms, cells_out, window):
    p = pl.program_id(0)
    strips, blocks, _, width, depth = cells_out.shape
    length = terms.shape[-1]

    @pl.when(p == 0)
    def _():
        window[...] = jnp.zeros(window.shape, jnp.float32)

    _, _, first, column = locate(meta, lax.axis_index("cols") * POS_AVG + p, depth)
    rest = lax.rem(first, 128)
    base = first - rest
    low = lax.rem(column, 8)
    top = pl.multiple_of(column - low, 8)
    groups = length // 8
    edge = jnp.zeros((1, 8, 128), jnp.float32)
    for part in range(2):
        before = jnp.zeros((length + 8, 128), jnp.float32)
        for j in range(length // 128 + 1):
            if j < length // 128:
                block = terms[0, part, :, 128 * j : 128 * (j + 1)].reshape(groups, 8, 128)
                block = pltpu.roll(block, low, 1)
                above = jnp.concatenate([edge, block], axis=0)
                below = jnp.concatenate([block, edge], axis=0)
                block = jnp.where(iota((groups + 1, 8, 128), 1) < low, above, below)
                block = pltpu.roll(block.reshape(length + 8, 128), rest, 1)
            else:
                block = jnp.zeros((length + 8, 128), jnp.float32)
            joined = jnp.where(iota((length + 8, 128), 1) < rest, before, block)
            window[part, pl.ds(top, length + 8), pl.ds(pl.multiple_of(base + 128 * j, 128), 128)] += joined
            before = block

    @pl.when(p == pl.num_programs(0) - 1)
    def _():
        for part in range(2):
            for b in range(blocks):
                for s in range(strips):
                    cells_out[s, b, part] = window[part, pl.ds(b * width, width), pl.ds(s * depth, depth)].astype(
                        jnp.bfloat16
                    )


def balanced_device(object_field, probe, amplitudes, strip_counts, row_offsets, col_offsets):
    f32, bf16 = jnp.float32, jnp.bfloat16
    width, depth = object_field.shape[1:]
    length = probe.shape[3]
    row, col = lax.axis_index("rows"), lax.axis_index("cols")
    table, table_t = tables(length)
    meta = jnp.concatenate([strip_counts, row_offsets, col_offsets])
    meta = jnp.pad(meta, (0, 128 - meta.shape[0]))[None, :]
    mode_shape = probe.shape[1:]
    meta_all, mode_all, cells, frames_all = pl.pallas_call(
        spread_inputs,
        in_specs=[ANY, WHOLE, ANY, ANY],
        out_specs=[ANY] * 4,
        out_shape=[
            jax.ShapeDtypeStruct((N, 1, 128), jnp.int32),
            jax.ShapeDtypeStruct((N,) + mode_shape, bf16),
            jax.ShapeDtypeStruct((N, N) + object_field.shape, bf16),
            jax.ShapeDtypeStruct((N,) + amplitudes.shape, bf16),
        ],
        scratch_shapes=[
            pltpu.VMEM(mode_shape, f32),
            pltpu.VMEM(amplitudes.shape, f32),
            pltpu.VMEM(object_field.shape, bf16),
            pltpu.VMEM(mode_shape, bf16),
            pltpu.VMEM(amplitudes.shape, bf16),
            pltpu.SemaphoreType.DMA((3, 28)),
            pltpu.SemaphoreType.DMA((5,)),
        ],
        compiler_params=pltpu.CompilerParams(collective_id=1, has_side_effects=True, vmem_limit_bytes=LIMIT),
        name="spread_inputs",
    )(meta, object_field, probe, amplitudes)

    plane = (1, 2, length, length)
    whole = lambda *shape: pl.BlockSpec(shape, lambda p: (0,) * len(shape))
    per_slot = pl.BlockSpec(plane, lambda p: (p, 0, 0, 0))
    scalars = pl.BlockSpec(memory_space=pltpu.SMEM)
    window = pltpu.VMEM((2, N * width + 128, N * depth + length), f32)
    quarters = (POS_AVG, N, length, length // N)
    patch, frames = pl.pallas_call(
        cut,
        grid=(POS_AVG,),
        in_specs=[scalars, whole(*cells.shape), ANY],
        out_specs=[per_slot, whole(N, POS_AVG, *amplitudes.shape[1:])],
        scratch_shapes=[window, pltpu.SemaphoreType.DMA((POS_AVG * N,))],
        out_shape=[
            jax.ShapeDtypeStruct((POS_AVG,) + plane[1:], bf16),
            jax.ShapeDtypeStruct((N, POS_AVG) + amplitudes.shape[1:], bf16),
        ],
        compiler_params=pltpu.CompilerParams(vmem_limit_bytes=LIMIT),
        name="cut",
    )(meta_all, cells, frames_all)
    probe_part, terms = pl.pallas_call(
        propagate,
        in_specs=[ANY] * 5,
        out_specs=[WHOLE, ANY],
        out_shape=[
            jax.ShapeDtypeStruct(mode_all.shape, bf16),
            jax.ShapeDtypeStruct((POS_AVG,) + plane[1:], f32),
        ],
        scratch_shapes=[
            pltpu.VMEM(patch.shape, bf16),
            pltpu.VMEM(mode_all.shape, bf16),
            pltpu.VMEM(table.shape, bf16),
            pltpu.VMEM(table.shape, bf16),
            pltpu.VMEM((POS_AVG,) + plane[1:], f32),
            pltpu.VMEM((POS_AVG, 2 * length, length), f32),
            pltpu.VMEM(quarters, bf16),
            pltpu.VMEM((POS_AVG, 2) + quarters[2:], bf16),
            pltpu.VMEM((POS_AVG,) + quarters[2:], bf16),
            pltpu.VMEM((POS_AVG,) + quarters[2:], bf16),
            pltpu.VMEM(quarters, bf16),
            pltpu.VMEM(frames.shape[1:], bf16),
            pltpu.VMEM((length, 2 * length), bf16),
            pltpu.VMEM((2 * length, length), bf16),
            pltpu.VMEM((2, length, length), f32),
            pltpu.SemaphoreType.DMA((2, 22)),
            pltpu.SemaphoreType.DMA((POS_AVG + 4,)),
        ],
        compiler_params=pltpu.CompilerParams(collective_id=2, has_side_effects=True, vmem_limit_bytes=LIMIT),
        name="propagate",
    )(patch, mode_all, frames, table, table_t)
    cells_part = pl.pallas_call(
        place,
        grid=(POS_AVG,),
        in_specs=[scalars, per_slot],
        out_specs=whole(*cells.shape),
        scratch_shapes=[window],
        out_shape=jax.ShapeDtypeStruct(cells.shape, bf16),
        compiler_params=pltpu.CompilerParams(vmem_limit_bytes=LIMIT),
        name="place",
    )(meta_all, terms)
    strip = (N,) + object_field.shape
    object_grad, probe_grad = pl.pallas_call(
        reduce_gradients,
        in_specs=[WHOLE, WHOLE],
        out_specs=[WHOLE, WHOLE],
        out_shape=[jax.ShapeDtypeStruct(object_field.shape, f32), jax.ShapeDtypeStruct(probe.shape, bf16)],
        scratch_shapes=[
            pltpu.VMEM((N - 1,) + mode_shape, bf16),
            pltpu.VMEM((2,) + strip, bf16),
            pltpu.VMEM(strip, bf16),
            pltpu.VMEM(strip, bf16),
            pltpu.VMEM(strip, bf16),
            pltpu.VMEM((N - 1,) + object_field.shape, bf16),
            pltpu.SemaphoreType.DMA((2, 21)),
        ],
        compiler_params=pltpu.CompilerParams(collective_id=3, has_side_effects=True, vmem_limit_bytes=LIMIT),
        name="reduce_gradients",
    )(probe_part, cells_part)
    return object_grad, probe_grad.astype(f32)


def solution(mesh):
    on_device = balanced_device if mesh.shape["rows"] == N and mesh.shape["cols"] == N else general_device
    placed = (
        P("groups", "cols", "rows"),
        P("groups", None, "cols", None),
        P(("groups", "rows"), "cols", None),
        P(("groups", "rows")),
        P(("groups", "rows")),
        P(("groups", "rows")),
    )
    return jax.shard_map(
        on_device,
        mesh=mesh,
        in_specs=placed,
        out_specs=(P("groups", "cols", "rows"), P("groups", None, "cols", None)),
        check_vma=False,
    )
```
